128 devices in a mesh: lat: 16 (over z_lo, y, core), lon: 8 (over z_hi, x).
Axes of the slice: x: 4, y: 4, z: 4 (z_hi: 2, z_lo: 2; z = z_hi * 2 + z_lo), core: 2. Of those that a mesh axis runs over, the one named last changes fastest.
Arguments:
- obs_values: float32 [128, 128, 2, 8, 128], P(('lat', 'lon')), may hold values from -6 to 6
- obs_cells: int32 [128, 128, 128], P(('lat', 'lon')), may hold values from 0 to 32767
- obs_counts: int32 [128, 128], P(('lat', 'lon')), may hold values from 32 to 128, as said below
- filter_lengths: float32 [2, 3], replicated, may hold values from 1 to 16
- filter_weights: float32 [2, 3], replicated, may hold values from 0.25 to 1
- vertical_mix: float32 [2, 8, 8], replicated, may hold values from -2 to 2
Outputs:
- increment: float32 [2, 8, 1024, 4096], P(None, None, 'lat', 'lon')
The draws below stay inside these ranges and needn't reach their ends.
Inputs may be any that keep to these rules, and one draw needn't show every extreme that they name: `obs_counts`: every sending device fills all 128 slots toward some tiles.
All inputs are finite; a program needn't handle non-finite values.
Results may differ from the reference program's by a relative error of at most 0.000078.
Values sent between devices are 32-bit elements; how exact they have to be, the bound alone decides.
A program may use at most 576 MiB of HBM per device.

```python
import math
import jax
import jax.numpy as jnp
from jax import lax

CLAT = 64
CLON = 512
LEV = 8
VARS = 2
SCALES = 3
HALF = 31
CAP = 128
NLAT = 1024
NLON = 4096
N_LON = 8
DEVICES = 128


def draw_obs_counts(key, part):
    key = jax.random.fold_in(key, 7)
    key_counts, key_crowd, key_chosen = jax.random.split(key, 3)
    drawn_counts = jax.random.randint(key_counts, (DEVICES, DEVICES), CAP // 4, CAP + 1)
    crowded = jax.random.randint(key_crowd, (DEVICES,), 0, 4) == 0
    chosen_tile = jax.random.randint(key_chosen, (), 0, DEVICES)
    crowded = crowded | (jnp.arange(DEVICES) == chosen_tile)
    return jnp.where(crowded[None, :], CAP, drawn_counts).astype(jnp.int32)


def set_ends(drawn, rng, low, largest):
    index_at = [jax.random.randint(jax.random.fold_in(rng, axis), (), 0, length) for axis, length in enumerate(drawn.shape)]
    widest = drawn.shape.index(max(drawn.shape))
    neighbour = index_at[:widest] + [(index_at[widest] + 1) % drawn.shape[widest]] + index_at[widest + 1:]
    return drawn.at[tuple(index_at)].set(low).at[tuple(neighbour)].set(largest)


def block_levels(own_key, shape, cuts, least, high):
    def one(dim, parts):
        steps = jax.random.uniform(jax.random.fold_in(jax.random.fold_in(own_key, 6), dim), (parts,), jnp.float32, least / len(cuts), high / len(cuts))
        return jnp.repeat(jnp.exp(steps), shape[dim] // parts).reshape((-1,) + (1,) * (len(shape) - dim - 1))

    gain = one(*cuts[0])
    for cut in cuts[1:]:
        gain = gain * one(*cut)
    return gain


def noise(own_key, dims, deviation, bound, cuts=(), held_as=jnp.bfloat16):
    values = jax.random.normal(own_key, dims, jnp.float32) * deviation
    if len(cuts) > 0:
        values = block_levels(own_key, dims, cuts, -0.22, 0.18) * values
    return jnp.clip(values, min=-bound, max=bound).astype(held_as)


def setup_inputs(seed: int = 0) -> dict:
    key_of = jax.random.split(jax.random.key(seed), 7)
    return {
        "obs_values": noise(key_of[0], (DEVICES, DEVICES, VARS, LEV, CAP), 1.0, 6.0, ((0, 128),), jnp.float32),
        "obs_cells": set_ends(jax.random.randint(key_of[1], (DEVICES, DEVICES, CAP), 0, CLAT * CLON), jax.random.fold_in(key_of[1], 1), 0, (CLAT * CLON) - 1).astype(jnp.int32),
        "obs_counts": draw_obs_counts(jax.random.fold_in(key_of[6], 71), 0),
        "filter_lengths": jnp.clip(jnp.exp(jax.random.uniform(key_of[3], (VARS, SCALES), jnp.float32, math.log(1.0), math.log(16.0))), 1.0, 16.0),
        "filter_weights": jnp.clip(jnp.exp(jax.random.uniform(key_of[4], (VARS, SCALES), jnp.float32, math.log(0.25), math.log(1.0))), 0.25, 1.0),
        "vertical_mix": noise(key_of[5], (VARS, LEV, LEV), LEV ** -0.5, 2.0, (), jnp.float32),
    }


def kernels(lengths, weights):
    offsets = (jnp.arange(2 * HALF + 1) - HALF).astype(jnp.float32)
    profile = jnp.exp(-0.5 * (offsets[None, None, :] / lengths[:, :, None]) ** 2)
    filter_taps = lax.optimization_barrier(jnp.sum(weights[:, :, None] * profile, axis=1))
    filter_taps = filter_taps / jnp.sqrt(lax.optimization_barrier(jnp.sum(filter_taps * filter_taps, axis=1, keepdims=True)))
    return jnp.repeat(filter_taps, LEV, axis=0)

def convolve(values_grid, filter_taps, direction):
    if direction == 2:
        kernel_shape = filter_taps[:, None, None, :]
    else:
        kernel_shape = filter_taps[:, None, :, None]
    result = lax.conv_general_dilated(values_grid[None], kernel_shape, (1, 1), 'VALID', dimension_numbers=('NCHW', 'OIHW', 'NCHW'), feature_group_count=values_grid.shape[0], precision=lax.Precision.HIGHEST)
    return result[0]

def reference(obs_values, obs_cells, obs_counts, filter_lengths, filter_weights, vertical_mix):
    channels = VARS * LEV
    slot_live = (jnp.arange(CAP)[None, None, :] < obs_counts[:, :, None]).astype(jnp.float32)
    weighted = obs_values * slot_live[:, :, None, None, :]
    target = jnp.arange(DEVICES).astype(jnp.int32)
    tile_lat = (target // N_LON)[None, :, None]
    tile_lon = (target % N_LON)[None, :, None]
    grid_lat = tile_lat * CLAT + obs_cells // CLON
    grid_lon = tile_lon * CLON + obs_cells % CLON
    flat_index = (grid_lat * NLON + grid_lon).astype(jnp.int32).reshape(-1)
    spread = weighted.transpose(2, 3, 0, 1, 4).reshape(channels, -1)
    gridded = jnp.zeros((channels, NLAT * NLON), jnp.float32).at[:, flat_index].add(spread)
    gridded = gridded.reshape(channels, NLAT, NLON)
    filter_taps = kernels(filter_lengths, filter_weights)
    wrapped = jnp.concatenate([gridded[:, :, NLON - HALF:], gridded, gridded[:, :, :HALF]], axis=2)
    along_lon = convolve(wrapped, filter_taps, 2)
    padded = jnp.pad(along_lon, ((0, 0), (HALF, HALF), (0, 0)))
    along_lat = convolve(padded, filter_taps, 1).reshape(VARS, LEV, NLAT, NLON)
    return jnp.einsum('vlm,vmab->vlab', vertical_mix, along_lat, precision=lax.Precision.HIGHEST)
```

```python
import functools

import jax
import jax.numpy as jnp
import numpy as np
from jax import lax
from jax.experimental import pallas as pl
from jax.experimental.pallas import tpu as pltpu
from jax.sharding import PartitionSpec as P

HALF = 31
LEV = 8
BITREV = (0, 4, 2, 6, 1, 5, 3, 7)
NACC = 2
MESH = pl.DeviceIdType.MESH


def split(x):
    hi = x.astype(jnp.bfloat16)
    return hi, (x - hi.astype(jnp.float32)).astype(jnp.bfloat16)


def dot(a, b):
    return jnp.dot(a, b, preferred_element_type=jnp.float32)


def dot3(a, b):
    return dot(a[0], b[0]) + dot(a[1], b[0]) + dot(a[0], b[1])


def grid_kernel(vals_hbm, cells_hbm, mixer, out, edges, vals, cells_v, cells_t, cells, table, sems, *grids):
    copies = [
        pltpu.make_async_copy(vals_hbm.at[pl.ds(q * 32, 32)], vals.at[pl.ds(q * 32, 32)], sems.at[q])
        for q in range(4)
    ]
    cell_copy = pltpu.make_async_copy(cells_hbm, cells_v, sems.at[4])
    cell_copy.start()
    for copy in copies:
        copy.start()
    cell_copy.wait()
    cells_t[...] = cells_v[...].T
    to_smem = pltpu.make_async_copy(cells_t, cells, sems.at[5])
    to_smem.start()

    def clear(i, carry):
        for grid in grids:
            grid[pl.ds(pl.multiple_of(i * 256, 256), 256), :] = jnp.zeros((256, 128), jnp.float32)
        return carry

    lax.fori_loop(0, 32768 // 256, clear, 0)
    mix = split(mixer[...])
    for copy in copies:
        copy.wait()

    def mix_rows(step, carry):
        for u in range(4):
            sg = step * 4 + u
            v = vals[pl.ds(pl.multiple_of(sg * 8, 8), 8)].reshape(128, 128).T
            table[pl.ds(pl.multiple_of(sg * 128, 128), 128), :] = dot3(split(v), mix)
        return carry

    lax.fori_loop(0, 4, mix_rows, 0)
    lane = lax.broadcasted_iota(jnp.int32, (1, 128), 1) // 16
    masks = [lane == i for i in range(8)]
    to_smem.wait()

    def scatter(j, carry):
        for g0 in range(0, 16, NACC):
            updates = []
            for a in range(NACC):
                sg = g0 + a
                row = table[pl.ds(sg * 128 + j, 1), :]
                for i in range(8):
                    c = cells[j, sg * 8 + i]
                    updates.append((a, i, c, grids[a][pl.ds(c, 1), :] + row))
            for a, i, c, total in updates:
                pltpu.store(grids[a].at[pl.ds(c, 1), :], total, mask=masks[i])
        return carry

    lax.fori_loop(0, 128, scatter, 0)

    lane8 = lax.broadcasted_iota(jnp.int32, (8, 128), 1) // 16
    b0 = (lane8 & 1) == 0
    b1 = (lane8 & 2) == 0
    b2 = (lane8 & 4) == 0
    packed = table

    def gather(t, carry):
        for u in range(2):
            base = t * 16 + u * 8
            a = []
            for q in range(8):
                off = pl.multiple_of(BITREV[q] * 4096 + base, 8)
                x = grids[0][pl.ds(off, 8), :]
                for grid in grids[1:]:
                    x = x + grid[pl.ds(off, 8), :]
                a.append(x)
            b = [
                jnp.where(b0, a[q], a[q + 4]) + pltpu.roll(jnp.where(b0, a[q + 4], a[q]), 16, 1)
                for q in range(4)
            ]
            c = [
                jnp.where(b1, b[q], b[q + 2]) + pltpu.roll(jnp.where(b1, b[q + 2], b[q]), 32, 1)
                for q in range(2)
            ]
            d = jnp.where(b2, c[0], c[1]) + pltpu.roll(jnp.where(b2, c[1], c[0]), 64, 1)
            packed[pl.ds(pl.multiple_of(base, 8), 8), :] = d
        return carry

    lax.fori_loop(0, 256, gather, 0)

    def turn(k2, carry):
        for cb in range(4):
            block = packed[pl.ds(pl.multiple_of(k2 * 512 + cb * 128, 128), 128), :].T
            block = block.reshape(8, 2, 8, 128)
            for v in range(2):
                for h in range(2):
                    out[h, v, k2, :, :, pl.ds(cb * 128, 128)] = block[h * 4 : h * 4 + 4, v]
        return carry

    lax.fori_loop(0, 8, turn, 0)

    quarter = lax.broadcasted_iota(jnp.int32, (32, 128), 1) // 32
    for h in range(2):
        for v in range(2):
            for kk in range(2):
                for side, (col, at) in enumerate(((0, 0), (384, 96))):
                    total = None
                    for kq in range(4):
                        x = out[h, v, kk * 4 + kq, :, :, pl.ds(col, 128)].reshape(32, 128)
                        shift = (kq * 32 - at) % 128
                        x = pltpu.roll(x, shift, 1) if shift else x
                        total = x if total is None else jnp.where(quarter == kq, x, total)
                    edges[side, h, v, pl.ds(kk * 32, 32), :] = total


def grid_tile(vals, cells, mixer):
    return pl.pallas_call(
        grid_kernel,
        out_shape=(
            jax.ShapeDtypeStruct((2, 2, 8, 4, 8, 512), jnp.float32),
            jax.ShapeDtypeStruct((2, 2, 2, 64, 128), jnp.float32),
        ),
        in_specs=[
            pl.BlockSpec(memory_space=pl.ANY),
            pl.BlockSpec(memory_space=pl.ANY),
            pl.BlockSpec(memory_space=pltpu.VMEM),
        ],
        out_specs=[pl.BlockSpec(memory_space=pltpu.VMEM)] * 2,
        scratch_shapes=[
            pltpu.VMEM((128, 16, 128), jnp.float32),
            pltpu.VMEM((128, 128), jnp.int32),
            pltpu.VMEM((128, 128), jnp.int32),
            pltpu.SMEM((128, 128), jnp.int32),
            pltpu.VMEM((4096, 128), jnp.float32),
            pltpu.SemaphoreType.DMA((6,)),
        ]
        + [pltpu.VMEM((32768, 128), jnp.float32)] * NACC,
        compiler_params=pltpu.CompilerParams(vmem_limit_bytes=60 * 2**20),
        cost_estimate=pl.CostEstimate(flops=10**9, bytes_accessed=4 * 2**20, transcendentals=0),
        name="scatter",
    )(vals, cells, mixer)


ROWS = np.concatenate([[base + rg * 8 + k2 for k2 in range(8) for rg in range(4)] for base in (0, 32, -32, 64)])


def filter_kernel(n_lat, n_lon, x_hbm, e_hbm, thi, tlo, whi, wlo, ahi, alo, out, x, e, y, send, recv, local):
    lat = lax.axis_index("lat")
    lon = lax.axis_index("lon")
    west = lax.rem(lon + n_lon - 1, n_lon)
    east = lax.rem(lon + 1, n_lon)
    north = lat - 1
    south = lat + 1
    has_north = lat > 0
    has_south = lat < n_lat - 1

    own_x = pltpu.make_async_copy(x_hbm, x.at[pl.ds(0, 2)], local.at[0])
    own_x.start()

    barrier = pltpu.get_barrier_semaphore()

    def greet(where):
        pl.semaphore_signal(barrier, inc=1, device_id=where, device_id_type=MESH)

    greet((lat, west))
    greet((lat, east))

    @pl.when(has_north)
    def _():
        for side in (west, lon, east):
            greet((north, side))

    @pl.when(has_south)
    def _():
        for side in (west, lon, east):
            greet((south, side))

    ends = lat * (n_lat - 1 - lat)
    pl.semaphore_wait(barrier, jnp.where(ends == 0, 5, 8))

    def remote(src, dst, slot, where):
        return pltpu.make_async_remote_copy(
            src_ref=src, dst_ref=dst, send_sem=send.at[slot], recv_sem=recv.at[slot],
            device_id=where, device_id_type=MESH,
        )

    sides = [
        remote(e_hbm.at[0], e.at[1, pl.ds(0, 2)], 0, (lat, west)),
        remote(e_hbm.at[1], e.at[0, pl.ds(0, 2)], 1, (lat, east)),
    ]
    up = [
        remote(e_hbm.at[0, 0], e.at[1, 3], 2, (north, west)),
        remote(e_hbm.at[1, 0], e.at[0, 3], 3, (north, east)),
        remote(x_hbm.at[0, 0], x.at[3, 0], 4, (north, lon)),
        remote(x_hbm.at[0, 1], x.at[3, 1], 5, (north, lon)),
    ]
    down = [
        remote(e_hbm.at[0, 1], e.at[1, 2], 6, (south, west)),
        remote(e_hbm.at[1, 1], e.at[0, 2], 7, (south, east)),
        remote(x_hbm.at[1, 0], x.at[2, 0], 8, (south, lon)),
        remote(x_hbm.at[1, 1], x.at[2, 1], 9, (south, lon)),
    ]
    for copy in sides:
        copy.start()

    @pl.when(has_north)
    def _():
        for copy in up:
            copy.start()

    @pl.when(has_south)
    def _():
        for copy in down:
            copy.start()

    @pl.when(jnp.logical_not(has_north))
    def _():
        x[2] = jnp.zeros((2, 256, 512), jnp.float32)
        e[:, 2] = jnp.zeros((2, 2, 64, 128), jnp.float32)

    @pl.when(jnp.logical_not(has_south))
    def _():
        x[3] = jnp.zeros((2, 256, 512), jnp.float32)
        e[:, 3] = jnp.zeros((2, 2, 64, 128), jnp.float32)

    def along_lon(s, v):
        rows = dot3(split(x[s, v]), (thi[v], tlo[v]))
        for cb in range(4):
            y[s, v, cb] = rows[:, cb * 128 : cb * 128 + 128]
        for side in range(2):
            rim = dot3(split(e[side, s, v]), (whi[v, side], wlo[v, side]))
            for kk in range(2):
                for kq in range(4):
                    at = pl.ds((kk * 4 + kq) * 32, 32)
                    y[s, v, side * 3, at] += rim[kk * 32 : kk * 32 + 32, kq * 128 : kq * 128 + 128]

    def along_lat(v):
        a = ahi[v], alo[v]

        def level(l, carry):
            rows = jnp.concatenate(
                [
                    jnp.concatenate([y[s, v, cb, pl.ds(l, 32, stride=8), :] for cb in range(4)], axis=1)
                    for s in range(4)
                ],
                axis=0,
            )
            out[v, l] = dot3(a, split(rows))
            return carry

        lax.fori_loop(0, LEV, level, 0)

    own_x.wait()
    for copy in sides:
        copy.wait_recv()

    def own(i, carry):
        along_lon(i // 2, i % 2)
        return carry

    lax.fori_loop(0, 4, own, 0)

    for v in range(2):
        @pl.when(has_north)
        def _():
            if v == 0:
                down[0].wait_recv()
                down[1].wait_recv()
            down[2 + v].wait_recv()

        @pl.when(has_south)
        def _():
            if v == 0:
                up[0].wait_recv()
                up[1].wait_recv()
            up[2 + v].wait_recv()

        lax.fori_loop(2, 4, lambda s, carry: (along_lon(s, v), carry)[1], 0)
        along_lat(v)

    for copy in sides:
        copy.wait_send()

    @pl.when(has_north)
    def _():
        for copy in up:
            copy.wait_send()

    @pl.when(has_south)
    def _():
        for copy in down:
            copy.wait_send()


def filter_tile(n_lat, n_lon, x, e, weights):
    return pl.pallas_call(
        functools.partial(filter_kernel, n_lat, n_lon),
        out_shape=jax.ShapeDtypeStruct((2, 8, 64, 512), jnp.float32),
        in_specs=[pl.BlockSpec(memory_space=pl.ANY)] * 2 + [pl.BlockSpec(memory_space=pltpu.VMEM)] * 6,
        out_specs=pl.BlockSpec(memory_space=pltpu.VMEM),
        scratch_shapes=[
            pltpu.VMEM((4, 2, 256, 512), jnp.float32),
            pltpu.VMEM((2, 4, 2, 64, 128), jnp.float32),
            pltpu.VMEM((4, 2, 4, 256, 128), jnp.float32),
            pltpu.SemaphoreType.DMA((10,)),
            pltpu.SemaphoreType.DMA((10,)),
            pltpu.SemaphoreType.DMA((1,)),
        ],
        compiler_params=pltpu.CompilerParams(
            vmem_limit_bytes=48 * 2**20, collective_id=0, has_side_effects=True
        ),
        cost_estimate=pl.CostEstimate(flops=6 * 10**9, bytes_accessed=8 * 2**20, transcendentals=0),
        name="filters",
    )(x, e, *weights)


def band_weights(lengths, weights):
    def profile(offset):
        t = offset.astype(np.float32)
        shape = (2,) + (1,) * t.ndim
        total = 0.0
        for s in range(lengths.shape[1]):
            scale = t[None] / lengths[:, s].reshape(shape)
            total = total + weights[:, s].reshape(shape) * jnp.exp(-0.5 * scale**2)
        return jnp.where(np.abs(offset)[None] <= HALF, total, 0.0)

    taps = profile(np.arange(-HALF, HALF + 1))
    norm = lax.rsqrt(jnp.sum(taps * taps, axis=1))

    def band(offset):
        x = profile(offset) * norm.reshape((2,) + (1,) * offset.ndim)
        hi = lax.reduce_precision(x, 8, 7)
        return hi.astype(jnp.bfloat16), (x - hi).astype(jnp.bfloat16)

    c = np.arange(512)
    centre = band(c[:, None] - c[None, :])
    lane = np.arange(128)
    kq, t = lane // 32, lane % 32
    same = kq[:, None, None] == np.arange(4)[None, :, None]
    col = np.arange(128)[None, None, :]
    far = 10 * HALF
    left = np.where(same, (t - 32)[:, None, None] - col, far)
    right = np.where(same, (t + 128)[:, None, None] - col, far)
    rims = band(np.stack([left, right]).reshape(2, 128, 512))
    down = band(ROWS[None, :] - np.arange(64)[:, None])
    return centre + rims + down


def local(obs_values, obs_cells, obs_counts, filter_lengths, filter_weights, vertical_mix):
    live = jnp.arange(128)[None, :] < obs_counts[0][:, None]
    vals = jnp.where(live[:, None, :], obs_values[0].reshape(128, 16, 128), 0.0)
    axes = ("lat", "lon")
    cells = lax.all_to_all(obs_cells[0], axes, split_axis=0, concat_axis=0, tiled=True)
    vals = lax.all_to_all(vals, axes, split_axis=0, concat_axis=0, tiled=True)
    eye = jnp.eye(8, dtype=jnp.float32)
    both = jnp.einsum("vlm,vw->vmwl", vertical_mix, jnp.eye(2, dtype=jnp.float32), precision=lax.Precision.HIGHEST)
    mixer = (eye[:, None, :, None] * both.reshape(16, 16)[None, :, None, :]).reshape(128, 128)
    weights = band_weights(filter_lengths, filter_weights)
    x, e = grid_tile(vals, cells, mixer)
    return filter_tile(lax.axis_size("lat"), lax.axis_size("lon"), x.reshape(2, 2, 256, 512), e, weights)


def solution(mesh):
    in_specs = (
        P(("lat", "lon"), None, None, None, None),
        P(("lat", "lon"), None, None),
        P(("lat", "lon"), None),
        P(),
        P(),
        P(),
    )
    return jax.shard_map(
        local, mesh=mesh, in_specs=in_specs, out_specs=P(None, None, "lat", "lon"), check_vma=False
    )
```

```python
import functools

import jax
import jax.numpy as jnp
from jax import lax
from jax.experimental import pallas as pl
from jax.experimental.pallas import tpu as pltpu
from jax.sharding import PartitionSpec as P

HALF = 31
LEV = 8
BITREV = (0, 4, 2, 6, 1, 5, 3, 7)
NACC = 2
CHUNK = 16
MESH = pl.DeviceIdType.MESH


def split(x):
    hi = x.astype(jnp.bfloat16)
    return hi, (x - hi.astype(jnp.float32)).astype(jnp.bfloat16)


def dot(a, b):
    return jnp.dot(a, b, preferred_element_type=jnp.float32)


def dot3(a, b):
    return dot(a[0], b[0]) + dot(a[1], b[0]) + dot(a[0], b[1])


def grid_kernel(vals_hbm, cells_hbm, mixer, out, edges, vals, cells_v, cells_t, cells, table, sems, ga, gb, ha0, ha1, hb0, hb1):
    grids = (ga, gb)
    half1, half2 = (ha0, ha1), (hb0, hb1)
    copies = [
        pltpu.make_async_copy(vals_hbm.at[pl.ds(q * 32, 32)], vals.at[pl.ds(q * 32, 32)], sems.at[q])
        for q in range(4)
    ]
    cell_copy = pltpu.make_async_copy(cells_hbm, cells_v, sems.at[4])
    cell_copy.start()
    for copy in copies:
        copy.start()
    cell_copy.wait()
    cells_t[...] = cells_v[...].T
    to_smem = pltpu.make_async_copy(cells_t, cells, sems.at[5])
    to_smem.start()

    def clear(i, carry):
        for grid in grids:
            grid[pl.ds(pl.multiple_of(i * 256, 256), 256), :] = jnp.zeros((256, 128), jnp.float32)
        return carry

    lax.fori_loop(0, 32768 // 256, clear, 0)
    mix = split(mixer[...])
    for copy in copies:
        copy.wait()

    def mix_rows(step, carry):
        for u in range(4):
            sg = step * 4 + u
            v = vals[pl.ds(pl.multiple_of(sg * 8, 8), 8)].reshape(128, 128).T
            table[pl.ds(pl.multiple_of(sg * 128, 128), 128), :] = dot3(split(v), mix)
        return carry

    lax.fori_loop(0, 4, mix_rows, 0)
    lane = lax.broadcasted_iota(jnp.int32, (1, 128), 1) // 16
    masks = [lane == i for i in range(8)]
    to_smem.wait()

    def scatter(j, carry):
        for g0 in range(0, 16, NACC):
            updates = []
            for a in range(NACC):
                sg = g0 + a
                row = table[pl.ds(sg * 128 + j, 1), :]
                for i in range(8):
                    c = cells[j, sg * 8 + i]
                    updates.append((a, i, c, grids[a][pl.ds(c, 1), :] + row))
            for a, i, c, total in updates:
                pltpu.store(grids[a].at[pl.ds(c, 1), :], total, mask=masks[i])
        return carry

    lax.fori_loop(0, 128, scatter, 0)

    lane8 = lax.broadcasted_iota(jnp.int32, (8, 128), 1) // 16
    b0 = (lane8 & 1) == 0
    b1 = (lane8 & 2) == 0
    b2 = (lane8 & 4) == 0
    packed = table

    def swap(keep, a, b, shift):
        return jnp.where(keep, a, b) + pltpu.roll(jnp.where(keep, b, a), shift, 1)

    def first(chunk, to):
        for s in range(CHUNK):
            base = chunk * (8 * CHUNK) + s * 8
            a = []
            for q in range(8):
                off = pl.multiple_of(BITREV[q] * 4096 + base, 8)
                x = grids[0][pl.ds(off, 8), :]
                for grid in grids[1:]:
                    x = x + grid[pl.ds(off, 8), :]
                a.append(x)
            for q in range(4):
                to[s * 4 + q] = swap(b0, a[q], a[q + 4], 16)

    def second(src, to):
        for s in range(CHUNK):
            for q in range(2):
                to[s * 2 + q] = swap(b1, src[s * 4 + q], src[s * 4 + q + 2], 32)

    def third(src, chunk):
        for s in range(CHUNK):
            base = pl.multiple_of(chunk * (8 * CHUNK) + s * 8, 8)
            packed[pl.ds(base, 8), :] = swap(b2, src[s * 2], src[s * 2 + 1], 64)

    def gather(t, carry):
        last = 4096 // (8 * CHUNK) - 1
        for u in range(2):
            chunk = t * 2 + u
            third(half2[u], jnp.maximum(chunk - 2, 0))
            second(half1[1 - u], half2[1 - u])
            first(jnp.minimum(chunk, last), half1[u])
        return carry

    lax.fori_loop(0, 2048 // (8 * CHUNK) + 1, gather, 0)

    def turn(k2, carry):
        for cb in range(4):
            block = packed[pl.ds(pl.multiple_of(k2 * 512 + cb * 128, 128), 128), :].T
            block = block.reshape(8, 2, 8, 128)
            for v in range(2):
                for h in range(2):
                    out[h, v, k2, :, :, pl.ds(cb * 128, 128)] = block[h * 4 : h * 4 + 4, v]
        return carry

    lax.fori_loop(0, 8, turn, 0)

    quarter = lax.broadcasted_iota(jnp.int32, (32, 128), 1) // 32
    for h in range(2):
        for v in range(2):
            for kk in range(2):
                for side, (col, at) in enumerate(((0, 0), (384, 96))):
                    total = None
                    for kq in range(4):
                        x = out[h, v, kk * 4 + kq, :, :, pl.ds(col, 128)].reshape(32, 128)
                        shift = (kq * 32 - at) % 128
                        x = pltpu.roll(x, shift, 1) if shift else x
                        total = x if total is None else jnp.where(quarter == kq, x, total)
                    edges[side, h, v, pl.ds(kk * 32, 32), :] = total


def grid_tile(vals, cells, mixer):
    return pl.pallas_call(
        grid_kernel,
        out_shape=(
            jax.ShapeDtypeStruct((2, 2, 8, 4, 8, 512), jnp.float32),
            jax.ShapeDtypeStruct((2, 2, 2, 64, 128), jnp.float32),
        ),
        in_specs=[
            pl.BlockSpec(memory_space=pl.ANY),
            pl.BlockSpec(memory_space=pl.ANY),
            pl.BlockSpec(memory_space=pltpu.VMEM),
        ],
        out_specs=[pl.BlockSpec(memory_space=pltpu.VMEM)] * 2,
        scratch_shapes=[
            pltpu.VMEM((128, 16, 128), jnp.float32),
            pltpu.VMEM((128, 128), jnp.int32),
            pltpu.VMEM((128, 128), jnp.int32),
            pltpu.SMEM((128, 128), jnp.int32),
            pltpu.VMEM((4096, 128), jnp.float32),
            pltpu.SemaphoreType.DMA((6,)),
        ]
        + [pltpu.VMEM((32768, 128), jnp.float32)] * NACC
        + [pltpu.VMEM((4 * CHUNK, 8, 128), jnp.float32)] * 2
        + [pltpu.VMEM((2 * CHUNK, 8, 128), jnp.float32)] * 2,
        compiler_params=pltpu.CompilerParams(vmem_limit_bytes=60 * 2**20),
        cost_estimate=pl.CostEstimate(flops=10**9, bytes_accessed=4 * 2**20, transcendentals=0),
        name="scatter",
    )(vals, cells, mixer)


def filter_kernel(n_lat, n_lon, x_hbm, e_hbm, thi, tlo, whi, wlo, ahi, alo, out, x, e, y, send, recv, local):
    lat = lax.axis_index("lat")
    lon = lax.axis_index("lon")
    west = lax.rem(lon + n_lon - 1, n_lon)
    east = lax.rem(lon + 1, n_lon)
    north = lat - 1
    south = lat + 1
    has_north = lat > 0
    has_south = lat < n_lat - 1

    own_x = pltpu.make_async_copy(x_hbm, x.at[pl.ds(0, 2)], local.at[0])
    own_x.start()

    barrier = pltpu.get_barrier_semaphore()

    def greet(where):
        pl.semaphore_signal(barrier, inc=1, device_id=where, device_id_type=MESH)

    greet((lat, west))
    greet((lat, east))

    @pl.when(has_north)
    def _():
        for side in (west, lon, east):
            greet((north, side))

    @pl.when(has_south)
    def _():
        for side in (west, lon, east):
            greet((south, side))

    ends = lat * (n_lat - 1 - lat)
    pl.semaphore_wait(barrier, jnp.where(ends == 0, 5, 8))

    def remote(src, dst, slot, where):
        return pltpu.make_async_remote_copy(
            src_ref=src, dst_ref=dst, send_sem=send.at[slot], recv_sem=recv.at[slot],
            device_id=where, device_id_type=MESH,
        )

    sides = [
        remote(e_hbm.at[0], e.at[1, pl.ds(0, 2)], 0, (lat, west)),
        remote(e_hbm.at[1], e.at[0, pl.ds(0, 2)], 1, (lat, east)),
    ]
    up = [
        remote(e_hbm.at[0, 0], e.at[1, 3], 2, (north, west)),
        remote(e_hbm.at[1, 0], e.at[0, 3], 3, (north, east)),
        remote(x_hbm.at[0, 0], x.at[3, 0], 4, (north, lon)),
        remote(x_hbm.at[0, 1], x.at[3, 1], 5, (north, lon)),
    ]
    down = [
        remote(e_hbm.at[0, 1], e.at[1, 2], 6, (south, west)),
        remote(e_hbm.at[1, 1], e.at[0, 2], 7, (south, east)),
        remote(x_hbm.at[1, 0], x.at[2, 0], 8, (south, lon)),
        remote(x_hbm.at[1, 1], x.at[2, 1], 9, (south, lon)),
    ]
    for copy in sides:
        copy.start()

    @pl.when(has_north)
    def _():
        for copy in up:
            copy.start()

    @pl.when(has_south)
    def _():
        for copy in down:
            copy.start()

    @pl.when(jnp.logical_not(has_north))
    def _():
        x[2] = jnp.zeros((2, 256, 512), jnp.float32)
        e[:, 2] = jnp.zeros((2, 2, 64, 128), jnp.float32)

    @pl.when(jnp.logical_not(has_south))
    def _():
        x[3] = jnp.zeros((2, 256, 512), jnp.float32)
        e[:, 3] = jnp.zeros((2, 2, 64, 128), jnp.float32)

    def along_lon(s, v):
        rows = dot3(split(x[s, v]), (thi[v], tlo[v]))
        for cb in range(4):
            y[s, v, cb] = rows[:, cb * 128 : cb * 128 + 128]
        for side in range(2):
            rim = dot3(split(e[side, s, v]), (whi[v, side], wlo[v, side]))
            for kk in range(2):
                for kq in range(4):
                    at = pl.ds((kk * 4 + kq) * 32, 32)
                    y[s, v, side * 3, at] += rim[kk * 32 : kk * 32 + 32, kq * 128 : kq * 128 + 128]

    def along_lat(v):
        a = ahi[v], alo[v]

        def level(l, carry):
            rows = jnp.concatenate(
                [
                    jnp.concatenate([y[s, v, cb, pl.ds(l, 32, stride=8), :] for cb in range(4)], axis=1)
                    for s in range(4)
                ],
                axis=0,
            )
            out[v, l] = dot3(a, split(rows))
            return carry

        lax.fori_loop(0, LEV, level, 0)

    own_x.wait()
    for copy in sides:
        copy.wait_recv()

    def own(i, carry):
        along_lon(i // 2, i % 2)
        return carry

    lax.fori_loop(0, 4, own, 0)

    for v in range(2):
        @pl.when(has_north)
        def _():
            if v == 0:
                down[0].wait_recv()
                down[1].wait_recv()
            down[2 + v].wait_recv()

        @pl.when(has_south)
        def _():
            if v == 0:
                up[0].wait_recv()
                up[1].wait_recv()
            up[2 + v].wait_recv()

        lax.fori_loop(2, 4, lambda s, carry: (along_lon(s, v), carry)[1], 0)
        along_lat(v)

    for copy in sides:
        copy.wait_send()

    @pl.when(has_north)
    def _():
        for copy in up:
            copy.wait_send()

    @pl.when(has_south)
    def _():
        for copy in down:
            copy.wait_send()


def filter_tile(n_lat, n_lon, x, e, weights):
    return pl.pallas_call(
        functools.partial(filter_kernel, n_lat, n_lon),
        out_shape=jax.ShapeDtypeStruct((2, 8, 64, 512), jnp.float32),
        in_specs=[pl.BlockSpec(memory_space=pl.ANY)] * 2 + [pl.BlockSpec(memory_space=pltpu.VMEM)] * 6,
        out_specs=pl.BlockSpec(memory_space=pltpu.VMEM),
        scratch_shapes=[
            pltpu.VMEM((4, 2, 256, 512), jnp.float32),
            pltpu.VMEM((2, 4, 2, 64, 128), jnp.float32),
            pltpu.VMEM((4, 2, 4, 256, 128), jnp.float32),
            pltpu.SemaphoreType.DMA((10,)),
            pltpu.SemaphoreType.DMA((10,)),
            pltpu.SemaphoreType.DMA((1,)),
        ],
        compiler_params=pltpu.CompilerParams(
            vmem_limit_bytes=48 * 2**20, collective_id=0, has_side_effects=True
        ),
        cost_estimate=pl.CostEstimate(flops=6 * 10**9, bytes_accessed=8 * 2**20, transcendentals=0),
        name="filters",
    )(x, e, *weights)


def route_kernel(n_lat, n_lon, obs, cell_in, counts, lengths, weights, mix,
                 vals, cells, mixer, thi, tlo, whi, wlo, ahi, alo, box, sems):
    lat = lax.axis_index("lat")
    lon = lax.axis_index("lon")
    me = lat * n_lon + lon
    count = n_lat * n_lon
    slot = lax.broadcasted_iota(jnp.int32, (16, 128), 1)

    def load(d):
        box[d] = jnp.where(slot < counts[0, d], obs[d], 0.0)

    def send(k, carry):
        to_lat = lax.rem(lat + k // n_lon, n_lat)
        to_lon = lax.rem(lon + lax.rem(k, n_lon), n_lon)
        d = to_lat * n_lon + to_lon
        load(d)
        pltpu.make_async_remote_copy(
            src_ref=cell_in.at[d], dst_ref=cells.at[me], send_sem=sems.at[0], recv_sem=sems.at[1],
            device_id=(to_lat, to_lon), device_id_type=MESH,
        ).start()
        pltpu.make_async_remote_copy(
            src_ref=box.at[d], dst_ref=vals.at[me], send_sem=sems.at[2], recv_sem=sems.at[3],
            device_id=(to_lat, to_lon), device_id_type=MESH,
        ).start()
        return carry

    lax.fori_loop(1, count, send, 0)
    load(me)
    mine = [
        pltpu.make_async_copy(cell_in.at[me], cells.at[me], sems.at[4]),
        pltpu.make_async_copy(box.at[me], vals.at[me], sems.at[5]),
    ]
    for copy in mine:
        copy.start()

    def profile(v, offset):
        t = offset.astype(jnp.float32)
        total = 0.0
        for s in range(3):
            scale = t / lengths[v, s]
            total = total + weights[v, s] * jnp.exp(-0.5 * (scale * scale))
        return jnp.where(jnp.abs(offset) <= HALF, total, 0.0)

    def iota(shape, dim):
        return lax.broadcasted_iota(jnp.int32, shape, dim)

    taps_at = iota((8, 128), 1) - HALF
    for v in range(2):
        taps = profile(v, taps_at)
        norm = lax.rsqrt(jnp.sum(taps * taps, axis=1, keepdims=True))[0:1, 0:1]

        def centre(i, carry):
            row = iota((32, 512), 0) + i * 32
            at = pl.ds(pl.multiple_of(i * 32, 32), 32)
            thi[v, at], tlo[v, at] = split(profile(v, row - iota((32, 512), 1)) * norm)
            return carry

        lax.fori_loop(0, 16, centre, 0)

        def rim(i, carry):
            for side, start in enumerate((-32, 128)):
                offset = iota((32, 512), 0) + start - lax.rem(iota((32, 512), 1), 128)
                x = jnp.where(iota((32, 512), 1) // 128 == i, profile(v, offset) * norm, 0.0)
                at = pl.ds(pl.multiple_of(i * 32, 32), 32)
                whi[v, side, at], wlo[v, side, at] = split(x)
            return carry

        lax.fori_loop(0, 4, rim, 0)
        k = iota((64, 128), 1)
        band = k // 32
        base = jnp.where(band == 0, 0, jnp.where(band == 1, 32, jnp.where(band == 2, -32, 64)))
        row = base + lax.rem(k, 4) * 8 + lax.rem(k, 32) // 4
        ahi[v], alo[v] = split(profile(v, row - iota((64, 128), 0)) * norm)

    row, col = iota((16, 128), 0), iota((16, 128), 1)
    small = jnp.zeros((16, 128), jnp.float32)
    for v in range(2):
        for l in range(LEV):
            for m in range(LEV):
                here = (row == v * LEV + m) & (lax.rem(col, 16) == v * LEV + l)
                small = jnp.where(here, mix[v, l, m], small)
    for i in range(8):
        mixer[pl.ds(i * 16, 16)] = jnp.where(col // 16 == i, small, 0.0)

    for copy in mine:
        copy.wait()
    rest = pl.ds(0, count - 1)
    pltpu.make_async_copy(cell_in.at[rest], cells.at[rest], sems.at[0]).wait()
    pltpu.make_async_copy(cells.at[rest], cells.at[rest], sems.at[1]).wait()
    pltpu.make_async_copy(box.at[rest], vals.at[rest], sems.at[2]).wait()
    pltpu.make_async_copy(vals.at[rest], vals.at[rest], sems.at[3]).wait()


def route(n_lat, n_lon, obs, cells, counts, lengths, weights, mix):
    n = n_lat * n_lon
    vmem = pl.BlockSpec(memory_space=pltpu.VMEM)
    smem = pl.BlockSpec(memory_space=pltpu.SMEM)
    hbm = pl.BlockSpec(memory_space=pl.ANY)
    bf16 = jnp.bfloat16
    return pl.pallas_call(
        functools.partial(route_kernel, n_lat, n_lon),
        out_shape=(
            jax.ShapeDtypeStruct((n, 16, 128), jnp.float32),
            jax.ShapeDtypeStruct((n, 1, 128), jnp.int32),
            jax.ShapeDtypeStruct((128, 128), jnp.float32),
        )
        + (jax.ShapeDtypeStruct((2, 512, 512), bf16),) * 2
        + (jax.ShapeDtypeStruct((2, 2, 128, 512), bf16),) * 2
        + (jax.ShapeDtypeStruct((2, 64, 128), bf16),) * 2,
        in_specs=[vmem, hbm, smem, smem, smem, smem],
        out_specs=[hbm, hbm] + [vmem] * 7,
        scratch_shapes=[pltpu.VMEM((n, 16, 128), jnp.float32), pltpu.SemaphoreType.DMA((6,))],
        compiler_params=pltpu.CompilerParams(vmem_limit_bytes=32 * 2**20, has_side_effects=True),
        cost_estimate=pl.CostEstimate(flops=10**7, bytes_accessed=4 * 2**20, transcendentals=0),
        name="route",
    )(obs, cells, counts, lengths, weights, mix)


def local(obs_values, obs_cells, obs_counts, filter_lengths, filter_weights, vertical_mix):
    n_lat, n_lon = lax.axis_size("lat"), lax.axis_size("lon")
    n = n_lat * n_lon
    vals, cells, mixer, *weights = route(
        n_lat, n_lon, obs_values.reshape(n, 16, 128), obs_cells.reshape(n, 1, 128), obs_counts,
        filter_lengths, filter_weights, vertical_mix,
    )
    x, e = grid_tile(vals, cells.reshape(128, 128), mixer)
    return filter_tile(n_lat, n_lon, x.reshape(2, 2, 256, 512), e, weights)


def solution(mesh):
    in_specs = (
        P(("lat", "lon"), None, None, None, None),
        P(("lat", "lon"), None, None),
        P(("lat", "lon"), None),
        P(),
        P(),
        P(),
    )
    return jax.shard_map(
        local, mesh=mesh, in_specs=in_specs, out_specs=P(None, None, "lat", "lon"), check_vma=False
    )
```

```python
import functools

import jax
import jax.numpy as jnp
from jax import lax
from jax.experimental import pallas as pl
from jax.experimental.pallas import tpu as pltpu
from jax.sharding import PartitionSpec as P

HALF = 31
LEV = 8
BITREV = (0, 4, 2, 6, 1, 5, 3, 7)
NACC = 2
CHUNK = 16
VMEM = 62 * 2**20
MESH = pl.DeviceIdType.MESH


def split(x):
    hi = x.astype(jnp.bfloat16)
    return hi, (x - hi.astype(jnp.float32)).astype(jnp.bfloat16)


def dot(a, b):
    return jnp.dot(a, b, preferred_element_type=jnp.float32)


def dot3(a, b):
    return dot(a[0], b[0]) + dot(a[1], b[0]) + dot(a[0], b[1])


def grid_kernel(table_hbm, cells_hbm, out_hbm, edges, table, cells, out, sems, ga, gb, ha0, ha1, hb0, hb1):
    grids = (ga, gb)
    half1, half2 = (ha0, ha1), (hb0, hb1)
    loads = [
        pltpu.make_async_copy(table_hbm, table.at[pl.ds(0, 2048)], sems.at[0]),
        pltpu.make_async_copy(cells_hbm, cells, sems.at[1]),
    ]
    for copy in loads:
        copy.start()

    def clear(i, carry):
        for grid in grids:
            grid[pl.ds(pl.multiple_of(i * 256, 256), 256), :] = jnp.zeros((256, 128), jnp.float32)
        return carry

    lax.fori_loop(0, 32768 // 256, clear, 0)
    lane = lax.broadcasted_iota(jnp.int32, (1, 128), 1) // 16
    masks = [lane == i for i in range(8)]
    for copy in loads:
        copy.wait()

    def scatter(j, carry):
        for g0 in range(0, 16, NACC):
            updates = []
            for a in range(NACC):
                sg = g0 + a
                row = table[pl.ds(sg * 128 + j, 1), :]
                for i in range(8):
                    c = cells[j, sg * 8 + i]
                    updates.append((a, i, c, grids[a][pl.ds(c, 1), :] + row))
            for a, i, c, total in updates:
                pltpu.store(grids[a].at[pl.ds(c, 1), :], total, mask=masks[i])
        return carry

    lax.fori_loop(0, 128, scatter, 0)

    lane8 = lax.broadcasted_iota(jnp.int32, (8, 128), 1) // 16
    b0 = (lane8 & 1) == 0
    b1 = (lane8 & 2) == 0
    b2 = (lane8 & 4) == 0
    packed = table

    def swap(keep, a, b, shift):
        return jnp.where(keep, a, b) + pltpu.roll(jnp.where(keep, b, a), shift, 1)

    def first(chunk, to):
        for s in range(CHUNK):
            base = chunk * (8 * CHUNK) + s * 8
            a = []
            for q in range(8):
                off = pl.multiple_of(BITREV[q] * 4096 + base, 8)
                x = grids[0][pl.ds(off, 8), :]
                for grid in grids[1:]:
                    x = x + grid[pl.ds(off, 8), :]
                a.append(x)
            for q in range(4):
                to[s * 4 + q] = swap(b0, a[q], a[q + 4], 16)

    def second(src, to):
        for s in range(CHUNK):
            for q in range(2):
                to[s * 2 + q] = swap(b1, src[s * 4 + q], src[s * 4 + q + 2], 32)

    def third(src, chunk):
        for s in range(CHUNK):
            base = pl.multiple_of(chunk * (8 * CHUNK) + s * 8, 8)
            packed[pl.ds(base, 8), :] = swap(b2, src[s * 2], src[s * 2 + 1], 64)

    def gather(t, carry):
        last = 4096 // (8 * CHUNK) - 1
        for u in range(2):
            chunk = t * 2 + u
            third(half2[u], jnp.maximum(chunk - 2, 0))
            second(half1[1 - u], half2[1 - u])
            first(jnp.minimum(chunk, last), half1[u])
        return carry

    lax.fori_loop(0, 2048 // (8 * CHUNK) + 1, gather, 0)

    def turn(k2, carry):
        for cb in range(4):
            block = packed[pl.ds(pl.multiple_of(k2 * 512 + cb * 128, 128), 128), :].T
            block = block.reshape(8, 2, 8, 128)
            for v in range(2):
                for h in range(2):
                    out[h, v, k2, :, :, pl.ds(cb * 128, 128)] = block[h * 4 : h * 4 + 4, v]
        return carry

    lax.fori_loop(0, 8, turn, 0)
    write = pltpu.make_async_copy(out, out_hbm, sems.at[2])
    write.start()

    quarter = lax.broadcasted_iota(jnp.int32, (32, 128), 1) // 32
    for h in range(2):
        for v in range(2):
            for kk in range(2):
                for side, (col, at) in enumerate(((0, 0), (384, 96))):
                    total = None
                    for kq in range(4):
                        x = out[h, v, kk * 4 + kq, :, :, pl.ds(col, 128)].reshape(32, 128)
                        shift = (kq * 32 - at) % 128
                        x = pltpu.roll(x, shift, 1) if shift else x
                        total = x if total is None else jnp.where(quarter == kq, x, total)
                    edges[side, h, v, pl.ds(kk * 32, 32), :] = total
    write.wait()


def grid_tile(table, cells):
    hbm = pl.BlockSpec(memory_space=pl.ANY)
    return pl.pallas_call(
        grid_kernel,
        out_shape=(
            jax.ShapeDtypeStruct((2, 2, 8, 4, 8, 512), jnp.float32),
            jax.ShapeDtypeStruct((2, 2, 2, 64, 128), jnp.float32),
        ),
        in_specs=[hbm, hbm],
        out_specs=[hbm, pl.BlockSpec(memory_space=pltpu.VMEM)],
        scratch_shapes=[
            pltpu.VMEM((4096, 128), jnp.float32),
            pltpu.SMEM((128, 128), jnp.int32),
            pltpu.VMEM((2, 2, 8, 4, 8, 512), jnp.float32),
            pltpu.SemaphoreType.DMA((3,)),
        ]
        + [pltpu.VMEM((32768, 128), jnp.float32)] * NACC
        + [pltpu.VMEM((4 * CHUNK, 8, 128), jnp.float32)] * 2
        + [pltpu.VMEM((2 * CHUNK, 8, 128), jnp.float32)] * 2,
        compiler_params=pltpu.CompilerParams(vmem_limit_bytes=VMEM),
        cost_estimate=pl.CostEstimate(flops=10**9, bytes_accessed=4 * 2**20, transcendentals=0),
        name="scatter",
    )(table, cells)


def filter_kernel(n_lat, n_lon, x_hbm, e_hbm, t_hbm, w_hbm, a_hbm, out, x, e, y, t, w, a, send, recv, local):
    lat = lax.axis_index("lat")
    lon = lax.axis_index("lon")
    west = lax.rem(lon + n_lon - 1, n_lon)
    east = lax.rem(lon + 1, n_lon)
    north = lat - 1
    south = lat + 1
    has_north = lat > 0
    has_south = lat < n_lat - 1

    own_x = pltpu.make_async_copy(x_hbm, x.at[pl.ds(0, 2)], local.at[0])
    loads = [
        own_x,
        pltpu.make_async_copy(t_hbm, t, local.at[1]),
        pltpu.make_async_copy(w_hbm, w, local.at[2]),
        pltpu.make_async_copy(a_hbm, a, local.at[3]),
    ]
    for copy in loads:
        copy.start()

    barrier = pltpu.get_barrier_semaphore()

    def greet(where):
        pl.semaphore_signal(barrier, inc=1, device_id=where, device_id_type=MESH)

    greet((lat, west))
    greet((lat, east))

    @pl.when(has_north)
    def _():
        for side in (west, lon, east):
            greet((north, side))

    @pl.when(has_south)
    def _():
        for side in (west, lon, east):
            greet((south, side))

    ends = lat * (n_lat - 1 - lat)
    pl.semaphore_wait(barrier, jnp.where(ends == 0, 5, 8))

    def remote(src, dst, slot, where):
        return pltpu.make_async_remote_copy(
            src_ref=src, dst_ref=dst, send_sem=send.at[slot], recv_sem=recv.at[slot],
            device_id=where, device_id_type=MESH,
        )

    sides = [
        remote(e_hbm.at[0], e.at[1, pl.ds(0, 2)], 0, (lat, west)),
        remote(e_hbm.at[1], e.at[0, pl.ds(0, 2)], 1, (lat, east)),
    ]
    up = [
        remote(e_hbm.at[0, 0], e.at[1, 3], 2, (north, west)),
        remote(e_hbm.at[1, 0], e.at[0, 3], 3, (north, east)),
        remote(x_hbm.at[0, 0], x.at[3, 0], 4, (north, lon)),
        remote(x_hbm.at[0, 1], x.at[3, 1], 5, (north, lon)),
    ]
    down = [
        remote(e_hbm.at[0, 1], e.at[1, 2], 6, (south, west)),
        remote(e_hbm.at[1, 1], e.at[0, 2], 7, (south, east)),
        remote(x_hbm.at[1, 0], x.at[2, 0], 8, (south, lon)),
        remote(x_hbm.at[1, 1], x.at[2, 1], 9, (south, lon)),
    ]
    for copy in sides:
        copy.start()

    @pl.when(has_north)
    def _():
        for copy in up:
            copy.start()

    @pl.when(has_south)
    def _():
        for copy in down:
            copy.start()

    @pl.when(jnp.logical_not(has_north))
    def _():
        x[2] = jnp.zeros((2, 256, 512), jnp.float32)
        e[:, 2] = jnp.zeros((2, 2, 64, 128), jnp.float32)

    @pl.when(jnp.logical_not(has_south))
    def _():
        x[3] = jnp.zeros((2, 256, 512), jnp.float32)
        e[:, 3] = jnp.zeros((2, 2, 64, 128), jnp.float32)

    def along_lon(s, v):
        rows = dot3(split(x[s, v]), (t[0, v], t[1, v]))
        for cb in range(4):
            y[s, v, cb] = rows[:, cb * 128 : cb * 128 + 128]
        for side in range(2):
            rim = dot3(split(e[side, s, v]), (w[0, v, side], w[1, v, side]))
            for kk in range(2):
                for kq in range(4):
                    at = pl.ds((kk * 4 + kq) * 32, 32)
                    y[s, v, side * 3, at] += rim[kk * 32 : kk * 32 + 32, kq * 128 : kq * 128 + 128]

    def along_lat(v):
        band = a[0, v], a[1, v]

        def level(l, carry):
            rows = jnp.concatenate(
                [
                    jnp.concatenate([y[s, v, cb, pl.ds(l, 32, stride=8), :] for cb in range(4)], axis=1)
                    for s in range(4)
                ],
                axis=0,
            )
            out[v, l] = dot3(band, split(rows))
            return carry

        lax.fori_loop(0, LEV, level, 0)

    for copy in loads:
        copy.wait()
    for copy in sides:
        copy.wait_recv()

    def own(i, carry):
        along_lon(i // 2, i % 2)
        return carry

    lax.fori_loop(0, 4, own, 0)

    for v in range(2):
        @pl.when(has_north)
        def _():
            if v == 0:
                down[0].wait_recv()
                down[1].wait_recv()
            down[2 + v].wait_recv()

        @pl.when(has_south)
        def _():
            if v == 0:
                up[0].wait_recv()
                up[1].wait_recv()
            up[2 + v].wait_recv()

        lax.fori_loop(2, 4, lambda s, carry: (along_lon(s, v), carry)[1], 0)
        along_lat(v)

    for copy in sides:
        copy.wait_send()

    @pl.when(has_north)
    def _():
        for copy in up:
            copy.wait_send()

    @pl.when(has_south)
    def _():
        for copy in down:
            copy.wait_send()


def filter_tile(n_lat, n_lon, x, e, weights):
    return pl.pallas_call(
        functools.partial(filter_kernel, n_lat, n_lon),
        out_shape=jax.ShapeDtypeStruct((2, 8, 64, 512), jnp.float32),
        in_specs=[pl.BlockSpec(memory_space=pl.ANY)] * 5,
        out_specs=pl.BlockSpec(memory_space=pltpu.VMEM),
        scratch_shapes=[
            pltpu.VMEM((4, 2, 256, 512), jnp.float32),
            pltpu.VMEM((2, 4, 2, 64, 128), jnp.float32),
            pltpu.VMEM((4, 2, 4, 256, 128), jnp.float32),
            pltpu.VMEM((2, 2, 512, 512), jnp.bfloat16),
            pltpu.VMEM((2, 2, 2, 128, 512), jnp.bfloat16),
            pltpu.VMEM((2, 2, 64, 128), jnp.bfloat16),
            pltpu.SemaphoreType.DMA((10,)),
            pltpu.SemaphoreType.DMA((10,)),
            pltpu.SemaphoreType.DMA((4,)),
        ],
        compiler_params=pltpu.CompilerParams(
            vmem_limit_bytes=VMEM, collective_id=0, has_side_effects=True
        ),
        cost_estimate=pl.CostEstimate(flops=6 * 10**9, bytes_accessed=8 * 2**20, transcendentals=0),
        name="filters",
    )(x, e, *weights)


def route_kernel(n_lat, n_lon, obs_hbm, cells_hbm, counts_hbm, lengths_hbm, weights_hbm, mix_hbm,
                 table, cells_out, t_out, w_out, a_out,
                 box, cell_box, vals, cells, counts, lengths, weights, mix, tiles, local, send, recv):
    lat = lax.axis_index("lat")
    lon = lax.axis_index("lon")
    me = lat * n_lon + lon
    count = n_lat * n_lon

    loads = [
        pltpu.make_async_copy(src, dst, local.at[i])
        for i, (src, dst) in enumerate(
            ((obs_hbm, box), (cells_hbm, cell_box), (counts_hbm, counts), (lengths_hbm, lengths),
             (weights_hbm, weights), (mix_hbm, mix))
        )
    ]
    for copy in loads:
        copy.start()

    barrier = pltpu.get_barrier_semaphore()

    def peer(k):
        return lax.rem(lat + k // n_lon, n_lat), lax.rem(lon + lax.rem(k, n_lon), n_lon)

    def greet(k, carry):
        pl.semaphore_signal(barrier, inc=1, device_id=peer(k), device_id_type=MESH)
        return carry

    lax.fori_loop(1, count, greet, 0)
    for copy in loads:
        copy.wait()

    slot = lax.broadcasted_iota(jnp.int32, (16, 128), 1)

    def mask(i, carry):
        for u in range(8):
            d = i * 8 + u
            box[d] = jnp.where(slot < counts[0, d], box[d], 0.0)
        return carry

    lax.fori_loop(0, count // 8, mask, 0)
    pl.semaphore_wait(barrier, count - 1)

    def to(k, carry):
        to_lat, to_lon = peer(k)
        d = to_lat * n_lon + to_lon
        pltpu.make_async_remote_copy(
            src_ref=cell_box.at[d], dst_ref=cells.at[me], send_sem=send.at[0], recv_sem=recv.at[n_lat],
            device_id=(to_lat, to_lon), device_id_type=MESH,
        ).start()
        pltpu.make_async_remote_copy(
            src_ref=box.at[d], dst_ref=vals.at[me], send_sem=send.at[1], recv_sem=recv.at[lat],
            device_id=(to_lat, to_lon), device_id_type=MESH,
        ).start()
        return carry

    lax.fori_loop(1, count, to, 0)
    pltpu.make_async_copy(cell_box.at[me], cells.at[me], recv.at[n_lat]).start()
    pltpu.make_async_copy(box.at[me], vals.at[me], recv.at[lat]).start()

    def iota(shape, dim):
        return lax.broadcasted_iota(jnp.int32, shape, dim)

    def profile(v, offset):
        t = offset.astype(jnp.float32)
        total = 0.0
        for s in range(3):
            scale = t / lengths[v, s]
            total = total + weights[v, s] * jnp.exp(-0.5 * (scale * scale))
        return jnp.where(jnp.abs(offset) <= HALF, total, 0.0)

    flat = (128, 128)
    for v in range(2):
        taps = profile(v, iota((8, 128), 1) - HALF)
        norm = lax.rsqrt(jnp.sum(taps * taps, axis=1, keepdims=True))[0:1, 0:1]
        for i in range(3):
            hi, lo = split(profile(v, iota(flat, 0) - iota(flat, 1) + (i - 1) * 128) * norm)
            tiles[0, i] = hi
            tiles[1, i] = lo
        blank = jnp.zeros(flat, jnp.bfloat16)
        for p in range(2):
            for i in range(4):
                for j in range(4):
                    piece = tiles[p, i - j + 1] if abs(i - j) <= 1 else blank
                    t_out[p, v, pl.ds(i * 128, 128), pl.ds(j * 128, 128)] = piece
            w_out[p, v] = jnp.zeros((2, 128, 512), jnp.bfloat16)
            for kq in range(4):
                at = pl.ds(kq * 32, 32), pl.ds(kq * 128, 128)
                w_out[(p, v, 0) + at] = tiles[p, 0, pl.ds(96, 32)]
                w_out[(p, v, 1) + at] = tiles[p, 2, pl.ds(0, 32)]
        k = iota((64, 128), 1)
        band = k // 32
        base = jnp.where(band == 0, 0, jnp.where(band == 1, 32, jnp.where(band == 2, -32, 64)))
        row = base + lax.rem(k, 4) * 8 + lax.rem(k, 32) // 4
        a_out[0, v], a_out[1, v] = split(profile(v, row - iota((64, 128), 0)) * norm)

    row, col = iota((16, 128), 0), iota((16, 128), 1)
    small = jnp.zeros((16, 128), jnp.float32)
    for v in range(2):
        for l in range(LEV):
            for m in range(LEV):
                here = (row == v * LEV + m) & (lax.rem(col, 16) == v * LEV + l)
                small = jnp.where(here, mix[v, l, m], small)
    mixer = split(jnp.concatenate([jnp.where(col // 16 == i, small, 0.0) for i in range(8)], axis=0))

    def group(i, carry):
        g = lax.rem(lat + n_lat - i, n_lat)
        here = pl.ds(pl.multiple_of(g * 8, 8), 8)
        pltpu.make_async_copy(vals.at[here], vals.at[here], recv.at[g]).wait()
        rows = vals[here].reshape(128, 128).T
        table[pl.ds(pl.multiple_of(g * 128, 128), 128), :] = dot3(split(rows), mixer)
        return carry

    lax.fori_loop(0, n_lat, group, 0)
    pltpu.make_async_copy(cells, cells, recv.at[n_lat]).wait()
    cells_out[...] = cells[:, 0, :].T
    rest = pl.ds(0, count - 1)
    pltpu.make_async_copy(cell_box.at[rest], cells.at[rest], send.at[0]).wait()
    pltpu.make_async_copy(box.at[rest], vals.at[rest], send.at[1]).wait()


def route(n_lat, n_lon, obs, cells, counts, lengths, weights, mix):
    n = n_lat * n_lon
    hbm = pl.BlockSpec(memory_space=pl.ANY)
    bf16 = jnp.bfloat16
    return pl.pallas_call(
        functools.partial(route_kernel, n_lat, n_lon),
        out_shape=(
            jax.ShapeDtypeStruct((n * 16, 128), jnp.float32),
            jax.ShapeDtypeStruct((n, 128), jnp.int32),
            jax.ShapeDtypeStruct((2, 2, 512, 512), bf16),
            jax.ShapeDtypeStruct((2, 2, 2, 128, 512), bf16),
            jax.ShapeDtypeStruct((2, 2, 64, 128), bf16),
        ),
        in_specs=[hbm] * 6,
        out_specs=[pl.BlockSpec(memory_space=pltpu.VMEM)] * 5,
        scratch_shapes=[
            pltpu.VMEM((n, 16, 128), jnp.float32),
            pltpu.VMEM((n, 1, 128), jnp.int32),
            pltpu.VMEM((n, 16, 128), jnp.float32),
            pltpu.VMEM((n, 1, 128), jnp.int32),
            pltpu.SMEM((1, n), jnp.int32),
            pltpu.SMEM((2, 3), jnp.float32),
            pltpu.SMEM((2, 3), jnp.float32),
            pltpu.SMEM((2, LEV, LEV), jnp.float32),
            pltpu.VMEM((2, 3, 128, 128), bf16),
            pltpu.SemaphoreType.DMA((6,)),
            pltpu.SemaphoreType.DMA((2,)),
            pltpu.SemaphoreType.DMA((n_lat + 1,)),
        ],
        compiler_params=pltpu.CompilerParams(vmem_limit_bytes=VMEM, collective_id=1, has_side_effects=True),
        cost_estimate=pl.CostEstimate(flops=10**7, bytes_accessed=4 * 2**20, transcendentals=0),
        name="route",
    )(obs, cells, counts, lengths, weights, mix)


def local(obs_values, obs_cells, obs_counts, filter_lengths, filter_weights, vertical_mix):
    n_lat, n_lon = lax.axis_size("lat"), lax.axis_size("lon")
    n = n_lat * n_lon
    table, cells, *weights = route(
        n_lat, n_lon, obs_values.reshape(n, 16, 128), obs_cells.reshape(n, 1, 128), obs_counts,
        filter_lengths, filter_weights, vertical_mix,
    )
    x, e = grid_tile(table, cells)
    return filter_tile(n_lat, n_lon, x.reshape(2, 2, 256, 512), e, weights)


def solution(mesh):
    in_specs = (
        P(("lat", "lon"), None, None, None, None),
        P(("lat", "lon"), None, None),
        P(("lat", "lon"), None),
        P(),
        P(),
        P(),
    )
    return jax.shard_map(
        local, mesh=mesh, in_specs=in_specs, out_specs=P(None, None, "lat", "lon"), check_vma=False
    )
```

```python
import functools

import jax
import jax.numpy as jnp
from jax import lax
from jax.experimental import pallas as pl
from jax.experimental.pallas import tpu as pltpu
from jax.sharding import PartitionSpec as P

HALF = 31
LEV = 8
NACC = 2
UNROLL = 2
BLOCKS = 4
VMEM = 62 * 2**20
MESH = pl.DeviceIdType.MESH


def split(x):
    hi = x.astype(jnp.bfloat16)
    return hi, (x - hi.astype(jnp.float32)).astype(jnp.bfloat16)


def dot(a, b):
    return jnp.dot(a, b, preferred_element_type=jnp.float32)


def dot3(a, b):
    return dot(a[0], b[0]) + dot(a[1], b[0]) + dot(a[0], b[1])


def grid_kernel(table_hbm, cells_hbm, out_hbm, table, out, picker, sized, sems, ga, gb, *cells):
    grids = (ga, gb)
    load = pltpu.make_async_copy(table_hbm, table, sems.at[0])
    load.start()
    for s in range(128):
        pltpu.make_async_copy(cells_hbm.at[s, 0], cells[s], sems.at[1]).start()

    def clear(i, carry):
        for grid in grids:
            grid[pl.ds(pl.multiple_of(i * 256, 256), 256), :] = jnp.zeros((256, 128), jnp.float32)
        return carry

    lax.fori_loop(0, 32768 // 256, clear, 0)
    lane = lax.broadcasted_iota(jnp.int32, (1, 128), 1) // 16
    masks = [lane == i for i in range(8)]
    load.wait()
    pltpu.make_async_copy(cells_hbm, sized, sems.at[1]).wait()

    def batch(n, j):
        row = table[pl.ds(n * 128 + j, 1), :]
        places = [cells[n * 8 + i][j] for i in range(8)]
        return n % NACC, places, [grids[n % NACC][pl.ds(c, 1), :] + row for c in places]

    def scatter(t, carry):
        order = [(n, t * UNROLL + u) for u in range(UNROLL) for n in range(16)]
        ahead = batch(*order[0])
        for following in order[1:] + [None]:
            a, places, totals = ahead
            if following:
                ahead = batch(*following)
            for c, total, live in zip(places, totals, masks):
                pltpu.store(grids[a].at[pl.ds(c, 1), :], total, mask=live)
        return carry

    lax.fori_loop(0, 128 // UNROLL, scatter, 0)

    r, c = lax.broadcasted_iota(jnp.int32, (128, 128), 0), lax.broadcasted_iota(jnp.int32, (128, 128), 1)
    for rg in range(8):
        hit = (lax.rem(r, 16) == lax.rem(c, 16)) & (r // 16 == rg)
        picker[:, pl.ds(rg * 128, 128)] = jnp.where(hit, 1.0, 0.0).astype(jnp.bfloat16)

    def gather(t, carry):
        k2 = t // (4 // BLOCKS)
        rows = 128 * BLOCKS
        base = t * rows
        parts = []
        for rg in range(8):
            at = pl.ds(pl.multiple_of(rg * 4096 + base, rows), rows)
            parts.append(ga[at, :] + gb[at, :])
        hi, lo = split(jnp.concatenate(parts, axis=1))
        dims = (((1,), (1,)), ((), ()))
        block = lax.dot_general(picker[...], hi, dims, preferred_element_type=jnp.float32)
        block = block + lax.dot_general(picker[...], lo, dims, preferred_element_type=jnp.float32)
        block = block.reshape(8, 2, 8, rows)
        at = pl.ds(pl.multiple_of(lax.rem(t, 4 // BLOCKS) * rows, rows), rows)
        for v in range(2):
            for h in range(2):
                out[h, v, pl.ds(k2 * 4, 4), :, at] = block[h * 4 : h * 4 + 4, v]
        return carry

    lax.fori_loop(0, 32 // BLOCKS, gather, 0)
    body = pl.ds(0, 32)
    write = pltpu.make_async_copy(out.at[:, :, body], out_hbm.at[:, :, body], sems.at[2])
    write.start()

    quarter = lax.broadcasted_iota(jnp.int32, (32, 128), 1) // 32
    for h in range(2):
        for v in range(2):
            for side, (col, at) in enumerate(((0, 0), (384, 96))):
                for kk in range(2):
                    total = None
                    for kq in range(4):
                        x = out[h, v, pl.ds((kk * 4 + kq) * 4, 4), :, pl.ds(col, 128)].reshape(32, 128)
                        shift = (kq * 32 - at) % 128
                        x = pltpu.roll(x, shift, 1) if shift else x
                        total = x if total is None else jnp.where(quarter == kq, x, total)
                    out[h, v, pl.ds(32, 4), :, pl.ds((side * 2 + kk) * 128, 128)] = total.reshape(4, 8, 128)
    edge = pl.ds(32, 4)
    write_edge = pltpu.make_async_copy(out.at[:, :, edge], out_hbm.at[:, :, edge], sems.at[3])
    write_edge.start()
    write.wait()
    write_edge.wait()


def grid_tile(table, cells):
    hbm = pl.BlockSpec(memory_space=pl.ANY)
    return pl.pallas_call(
        grid_kernel,
        out_shape=jax.ShapeDtypeStruct((2, 2, 36, 8, 512), jnp.float32),
        in_specs=[hbm, hbm],
        out_specs=hbm,
        scratch_shapes=[
            pltpu.VMEM((2048, 128), jnp.float32),
            pltpu.VMEM((2, 2, 36, 8, 512), jnp.float32),
            pltpu.VMEM((128, 1024), jnp.bfloat16),
            pltpu.VMEM((128, 1, 128), jnp.int32),
            pltpu.SemaphoreType.DMA((4,)),
        ]
        + [pltpu.VMEM((32768, 128), jnp.float32)] * NACC
        + [pltpu.SMEM((128,), jnp.int32)] * 128,
        compiler_params=pltpu.CompilerParams(vmem_limit_bytes=VMEM),
        cost_estimate=pl.CostEstimate(flops=10**9, bytes_accessed=4 * 2**20, transcendentals=0),
        name="scatter",
    )(table, cells)


def filter_kernel(n_lat, n_lon, x_hbm, t_hbm, w_hbm, a_hbm, out, x, e, y, t, w, a, send, recv, local):
    lat = lax.axis_index("lat")
    lon = lax.axis_index("lon")
    west = lax.rem(lon + n_lon - 1, n_lon)
    east = lax.rem(lon + 1, n_lon)
    north = lat - 1
    south = lat + 1
    has_north = lat > 0
    has_south = lat < n_lat - 1
    rows = pl.ds(0, 256)
    edge = pl.ds(256, 32)
    own = pl.ds(0, 2)
    upper, lower = pl.ds(0, 248), pl.ds(8, 248)

    barrier = pltpu.get_barrier_semaphore()

    def greet(where):
        pl.semaphore_signal(barrier, inc=1, device_id=where, device_id_type=MESH)

    @pl.when(has_north)
    def _():
        greet((north, lon))

    @pl.when(has_south)
    def _():
        greet((south, lon))

    greet((lat, west))
    greet((lat, east))

    loads = [
        pltpu.make_async_copy(x_hbm.at[:, :, rows], x.at[own], local.at[0]),
        pltpu.make_async_copy(t_hbm, t, local.at[1]),
        pltpu.make_async_copy(w_hbm, w, local.at[2]),
        pltpu.make_async_copy(a_hbm, a, local.at[3]),
    ]
    for copy in loads:
        copy.start()
    ends = lat * (n_lat - 1 - lat)
    pl.semaphore_wait(barrier, jnp.where(ends == 0, 3, 4))

    def remote(src, dst, slot, where):
        return pltpu.make_async_remote_copy(
            src_ref=src, dst_ref=dst, send_sem=send.at[slot], recv_sem=recv.at[slot],
            device_id=where, device_id_type=MESH,
        )

    sides = [
        remote(x_hbm.at[:, :, edge, pl.ds(0, 256)], e.at[1, own], 0, (lat, west)),
        remote(x_hbm.at[:, :, edge, pl.ds(256, 256)], e.at[0, own], 1, (lat, east)),
    ]
    up = [
        remote(x_hbm.at[0, 0, upper], x.at[3, 0, upper], 2, (north, lon)),
        remote(x_hbm.at[0, 1, upper], x.at[3, 1, upper], 3, (north, lon)),
        remote(e.at[:, 0], e.at[:, 3], 4, (north, lon)),
    ]
    down = [
        remote(x_hbm.at[1, 0, lower], x.at[2, 0, lower], 5, (south, lon)),
        remote(x_hbm.at[1, 1, lower], x.at[2, 1, lower], 6, (south, lon)),
        remote(e.at[:, 1], e.at[:, 2], 7, (south, lon)),
    ]

    def ends_do(act, which):
        @pl.when(has_north)
        def _():
            for i in which:
                act(up[i])

        @pl.when(has_south)
        def _():
            for i in which:
                act(down[i])

    def arrived(which):
        @pl.when(has_north)
        def _():
            for i in which:
                down[i].wait_recv()

        @pl.when(has_south)
        def _():
            for i in which:
                up[i].wait_recv()

    for copy in sides:
        copy.start()
    ends_do(lambda copy: copy.start(), (0,))

    x[2, :, pl.ds(0, 8)] = jnp.zeros((2, 8, 512), jnp.float32)
    x[3, :, pl.ds(248, 8)] = jnp.zeros((2, 8, 512), jnp.float32)
    for s, there in ((2, has_north), (3, has_south)):
        @pl.when(jnp.logical_not(there))
        def _():
            x[s] = jnp.zeros((2, 256, 512), jnp.float32)
            e[:, s] = jnp.zeros((2, 2, 32, 256), jnp.float32)

    def centre(s, v):
        total = dot3(split(x[pl.ds(s, 2), v].reshape(512, 512)), (t[0, v], t[1, v]))
        for u in range(2):
            for cb in range(4):
                y[s + u, v, cb] = total[u * 256 : u * 256 + 256, cb * 128 : cb * 128 + 128]

    def rims(s, v):
        for side in range(2):
            lines = [e[side, s + u, v, :, pl.ds(kk * 128, 128)] for u in range(2) for kk in range(2)]
            rim = dot3(split(jnp.concatenate(lines, axis=0)), (w[0, v, side], w[1, v, side]))
            for u in range(2):
                for k2 in range(8):
                    line = (u * 2 + k2 // 4) * 32
                    col = (k2 % 4) * 128
                    y[s + u, v, side * 3, pl.ds(k2 * 32, 32)] += rim[line : line + 32, col : col + 128]

    def along_lat(s, v):
        def levels(i, carry):
            for u in range(4):
                l = i * 4 + u
                line = jnp.concatenate(
                    [
                        jnp.concatenate([y[s + k, v, cb, pl.ds(l, 32, stride=8), :] for cb in range(4)], axis=1)
                        for k in range(2)
                    ],
                    axis=0,
                )
                hi, lo = split(line)
                part = dot(a[s // 2, v], jnp.concatenate([hi, hi, lo], axis=0))
                out[v, l] = part if s == 0 else out[v, l] + part
            return carry

        lax.fori_loop(0, LEV // 4, levels, 0)

    for copy in loads:
        copy.wait()
    centre(0, 0)
    for copy in sides:
        copy.wait_recv()
    ends_do(lambda copy: copy.start(), (2, 1))
    centre(0, 1)
    for v in range(2):
        rims(0, v)
        along_lat(0, v)

    for v in range(2):
        arrived((v, 2) if v == 0 else (v,))
        centre(2, v)
        rims(2, v)
        along_lat(2, v)

    for copy in sides:
        copy.wait_send()
    ends_do(lambda copy: copy.wait_send(), (0, 1, 2))


def filter_tile(n_lat, n_lon, x, weights):
    return pl.pallas_call(
        functools.partial(filter_kernel, n_lat, n_lon),
        out_shape=jax.ShapeDtypeStruct((2, 8, 64, 512), jnp.float32),
        in_specs=[pl.BlockSpec(memory_space=pltpu.HBM)] * 4,
        out_specs=pl.BlockSpec(memory_space=pltpu.VMEM),
        scratch_shapes=[
            pltpu.VMEM((4, 2, 256, 512), jnp.float32),
            pltpu.VMEM((2, 4, 2, 32, 256), jnp.float32),
            pltpu.VMEM((4, 2, 4, 256, 128), jnp.float32),
            pltpu.VMEM((2, 2, 512, 512), jnp.bfloat16),
            pltpu.VMEM((2, 2, 2, 128, 512), jnp.bfloat16),
            pltpu.VMEM((2, 2, 64, 192), jnp.bfloat16),
            pltpu.SemaphoreType.DMA((8,)),
            pltpu.SemaphoreType.DMA((8,)),
            pltpu.SemaphoreType.DMA((4,)),
        ],
        compiler_params=pltpu.CompilerParams(
            vmem_limit_bytes=40 * 2**20, collective_id=0, has_side_effects=True
        ),
        cost_estimate=pl.CostEstimate(flops=6 * 10**9, bytes_accessed=8 * 2**20, transcendentals=0),
        name="filters",
    )(x, *weights)


def route_kernel(n_lat, n_lon, obs_hbm, cells_hbm, counts_hbm, lengths_hbm, weights_hbm, mix_hbm,
                 table, cells_out, t_out, w_out, a_out,
                 box, cell_box, vals, cells, counts, lengths, weights, mix, tiles, local, send, recv):
    lat = lax.axis_index("lat")
    lon = lax.axis_index("lon")
    me = lat * n_lon + lon
    count = n_lat * n_lon

    loads = [
        pltpu.make_async_copy(src, dst, local.at[i])
        for i, (src, dst) in enumerate(
            ((obs_hbm, box), (cells_hbm, cell_box), (counts_hbm, counts), (lengths_hbm, lengths),
             (weights_hbm, weights), (mix_hbm, mix))
        )
    ]
    for copy in loads:
        copy.start()

    barrier = pltpu.get_barrier_semaphore()

    def peer(k):
        return lax.rem(lat + k // n_lon, n_lat), lax.rem(lon + lax.rem(k, n_lon), n_lon)

    def greet(k, carry):
        pl.semaphore_signal(barrier, inc=1, device_id=peer(k), device_id_type=MESH)
        return carry

    lax.fori_loop(1, count, greet, 0)
    for copy in loads:
        copy.wait()

    slot = lax.broadcasted_iota(jnp.int32, (16, 128), 1)

    def mask(i, carry):
        for u in range(8):
            d = i * 8 + u
            box[d] = jnp.where(slot < counts[0, d], box[d], 0.0)
        return carry

    lax.fori_loop(0, count // 8, mask, 0)
    pl.semaphore_wait(barrier, count - 1)

    def to(k, carry):
        to_lat, to_lon = peer(k)
        d = to_lat * n_lon + to_lon
        pltpu.make_async_remote_copy(
            src_ref=cell_box.at[d], dst_ref=cells.at[me], send_sem=send.at[0], recv_sem=recv.at[n_lat],
            device_id=(to_lat, to_lon), device_id_type=MESH,
        ).start()
        pltpu.make_async_remote_copy(
            src_ref=box.at[d], dst_ref=vals.at[me], send_sem=send.at[1], recv_sem=recv.at[lat],
            device_id=(to_lat, to_lon), device_id_type=MESH,
        ).start()
        return carry

    lax.fori_loop(1, count, to, 0)
    pltpu.make_async_copy(cell_box.at[me], cells.at[me], recv.at[n_lat]).start()
    pltpu.make_async_copy(box.at[me], vals.at[me], recv.at[lat]).start()

    def iota(shape, dim):
        return lax.broadcasted_iota(jnp.int32, shape, dim)

    def profile(v, offset):
        t = offset.astype(jnp.float32)
        total = 0.0
        for s in range(3):
            scale = t / lengths[v, s]
            total = total + weights[v, s] * jnp.exp(-0.5 * (scale * scale))
        return jnp.where(jnp.abs(offset) <= HALF, total, 0.0)

    flat = (128, 128)
    for v in range(2):
        taps = profile(v, iota((8, 128), 1) - HALF)
        norm = lax.rsqrt(jnp.sum(taps * taps, axis=1, keepdims=True))[0:1, 0:1]
        for i in range(3):
            hi, lo = split(profile(v, iota(flat, 0) - iota(flat, 1) + (i - 1) * 128) * norm)
            tiles[0, i] = hi
            tiles[1, i] = lo
        blank = jnp.zeros(flat, jnp.bfloat16)
        for p in range(2):
            for i in range(4):
                for j in range(4):
                    piece = tiles[p, i - j + 1] if abs(i - j) <= 1 else blank
                    t_out[p, v, pl.ds(i * 128, 128), pl.ds(j * 128, 128)] = piece
            w_out[p, v] = jnp.zeros((2, 128, 512), jnp.bfloat16)
            for kq in range(4):
                at = pl.ds(kq * 32, 32), pl.ds(kq * 128, 128)
                w_out[(p, v, 0) + at] = tiles[p, 0, pl.ds(96, 32)]
                w_out[(p, v, 1) + at] = tiles[p, 2, pl.ds(0, 32)]
        k = iota((64, 192), 1)
        place = lax.rem(k, 32)
        inner = lax.rem(place, 4) * 8 + place // 4
        second = lax.rem(k, 64) // 32
        for part in range(2):
            base = second * 32 if part == 0 else second * 96 - 32
            hi, lo = split(profile(v, base + inner - iota((64, 192), 0)) * norm)
            a_out[part, v] = jnp.where(k // 64 == 1, lo.astype(jnp.float32), hi.astype(jnp.float32)).astype(jnp.bfloat16)

    row, col = iota((16, 128), 0), iota((16, 128), 1)
    small = jnp.zeros((16, 128), jnp.float32)
    for v in range(2):
        for l in range(LEV):
            for m in range(LEV):
                here = (row == v * LEV + m) & (lax.rem(col, 16) == v * LEV + l)
                small = jnp.where(here, mix[v, l, m], small)
    mixer = split(jnp.concatenate([jnp.where(col // 16 == i, small, 0.0) for i in range(8)], axis=0))

    def group(i, carry):
        g = lax.rem(lat + n_lat - i, n_lat)
        here = pl.ds(pl.multiple_of(g * 8, 8), 8)
        pltpu.make_async_copy(vals.at[here], vals.at[here], recv.at[g]).wait()
        rows = vals[here].reshape(128, 128).T
        table[pl.ds(pl.multiple_of(g * 128, 128), 128), :] = dot3(split(rows), mixer)
        return carry

    lax.fori_loop(0, n_lat, group, 0)
    pltpu.make_async_copy(cells, cells, recv.at[n_lat]).wait()
    cells_out[...] = cells[...]
    rest = pl.ds(0, count - 1)
    pltpu.make_async_copy(cell_box.at[rest], cells.at[rest], send.at[0]).wait()
    pltpu.make_async_copy(box.at[rest], vals.at[rest], send.at[1]).wait()


def route(n_lat, n_lon, obs, cells, counts, lengths, weights, mix):
    n = n_lat * n_lon
    hbm = pl.BlockSpec(memory_space=pl.ANY)
    bf16 = jnp.bfloat16
    return pl.pallas_call(
        functools.partial(route_kernel, n_lat, n_lon),
        out_shape=(
            jax.ShapeDtypeStruct((n * 16, 128), jnp.float32),
            jax.ShapeDtypeStruct((n, 1, 128), jnp.int32),
            jax.ShapeDtypeStruct((2, 2, 512, 512), bf16),
            jax.ShapeDtypeStruct((2, 2, 2, 128, 512), bf16),
            jax.ShapeDtypeStruct((2, 2, 64, 192), bf16),
        ),
        in_specs=[hbm] * 6,
        out_specs=[pl.BlockSpec(memory_space=pltpu.VMEM)] * 5,
        scratch_shapes=[
            pltpu.VMEM((n, 16, 128), jnp.float32),
            pltpu.VMEM((n, 1, 128), jnp.int32),
            pltpu.VMEM((n, 16, 128), jnp.float32),
            pltpu.VMEM((n, 1, 128), jnp.int32),
            pltpu.SMEM((1, n), jnp.int32),
            pltpu.SMEM((2, 3), jnp.float32),
            pltpu.SMEM((2, 3), jnp.float32),
            pltpu.SMEM((2, LEV, LEV), jnp.float32),
            pltpu.VMEM((2, 3, 128, 128), bf16),
            pltpu.SemaphoreType.DMA((6,)),
            pltpu.SemaphoreType.DMA((2,)),
            pltpu.SemaphoreType.DMA((n_lat + 1,)),
        ],
        compiler_params=pltpu.CompilerParams(vmem_limit_bytes=VMEM, collective_id=1, has_side_effects=True),
        cost_estimate=pl.CostEstimate(flops=10**7, bytes_accessed=4 * 2**20, transcendentals=0),
        name="route",
    )(obs, cells, counts, lengths, weights, mix)


def local(obs_values, obs_cells, obs_counts, filter_lengths, filter_weights, vertical_mix):
    n_lat, n_lon = lax.axis_size("lat"), lax.axis_size("lon")
    n = n_lat * n_lon
    table, cells, *weights = route(
        n_lat, n_lon, obs_values.reshape(n, 16, 128), obs_cells.reshape(n, 1, 128), obs_counts,
        filter_lengths, filter_weights, vertical_mix,
    )
    x = grid_tile(table, cells)
    return filter_tile(n_lat, n_lon, x.reshape(2, 2, 288, 512), weights)


def solution(mesh):
    in_specs = (
        P(("lat", "lon"), None, None, None, None),
        P(("lat", "lon"), None, None),
        P(("lat", "lon"), None),
        P(),
        P(),
        P(),
    )
    return jax.shard_map(
        local, mesh=mesh, in_specs=in_specs, out_specs=P(None, None, "lat", "lon"), check_vma=False
    )
```

```python
import functools

import jax
import jax.numpy as jnp
from jax import lax
from jax.experimental import pallas as pl
from jax.experimental.pallas import tpu as pltpu
from jax.sharding import PartitionSpec as P

HALF = 31
LEV = 8
NACC = 2
UNROLL = 2
BLOCKS = 4
VMEM = 62 * 2**20
MESH = pl.DeviceIdType.MESH


def split(x):
    hi = x.astype(jnp.bfloat16)
    return hi, (x - hi.astype(jnp.float32)).astype(jnp.bfloat16)


def dot(a, b):
    return jnp.dot(a, b, preferred_element_type=jnp.float32)


def dot3(a, b):
    return dot(a[0], b[0]) + dot(a[1], b[0]) + dot(a[0], b[1])


def grid_kernel(vals_hbm, cells_hbm, mixer_hbm, out_hbm, vals, mixer, table, out, picker, sized, sems, ga, gb, *cells):
    grids = (ga, gb)
    loads = [
        pltpu.make_async_copy(vals_hbm, vals, sems.at[0]),
        pltpu.make_async_copy(mixer_hbm, mixer, sems.at[2]),
    ]
    for copy in loads:
        copy.start()
    for s in range(128):
        pltpu.make_async_copy(cells_hbm.at[s, 0], cells[s], sems.at[1]).start()

    def clear(i, carry):
        gb[pl.ds(pl.multiple_of(i * 512, 512), 512), :] = jnp.zeros((512, 128), jnp.float32)
        return carry

    lax.fori_loop(0, 64, clear, 0)
    for copy in loads:
        copy.wait()
    mix = split(mixer[...])

    def fill(i, carry):
        ga[pl.ds(pl.multiple_of(i * 4096, 4096), 4096), :] = jnp.zeros((4096, 128), jnp.float32)
        for u in range(2):
            g = i * 2 + u
            rows = vals[pl.ds(pl.multiple_of(g * 8, 8), 8)].reshape(128, 128).T
            table[pl.ds(pl.multiple_of(g * 128, 128), 128), :] = dot3(split(rows), mix)
        return carry

    lax.fori_loop(0, 8, fill, 0)
    lane = lax.broadcasted_iota(jnp.int32, (1, 128), 1) // 16
    masks = [lane == i for i in range(8)]
    pltpu.make_async_copy(cells_hbm, sized, sems.at[1]).wait()

    def batch(n, j):
        row = table[pl.ds(n * 128 + j, 1), :]
        places = [cells[n * 8 + i][j] for i in range(8)]
        return n % NACC, places, [grids[n % NACC][pl.ds(c, 1), :] + row for c in places]

    def scatter(t, carry):
        order = [(n, t * UNROLL + u) for u in range(UNROLL) for n in range(16)]
        ahead = batch(*order[0])
        for following in order[1:] + [None]:
            a, places, totals = ahead
            if following:
                ahead = batch(*following)
            for c, total, live in zip(places, totals, masks):
                pltpu.store(grids[a].at[pl.ds(c, 1), :], total, mask=live)
        return carry

    lax.fori_loop(0, 128 // UNROLL, scatter, 0)

    r, c = lax.broadcasted_iota(jnp.int32, (128, 128), 0), lax.broadcasted_iota(jnp.int32, (128, 128), 1)
    for rg in range(8):
        hit = (lax.rem(r, 16) == lax.rem(c, 16)) & (r // 16 == rg)
        picker[:, pl.ds(rg * 128, 128)] = jnp.where(hit, 1.0, 0.0).astype(jnp.bfloat16)

    def gather(t, carry):
        k2 = t // (4 // BLOCKS)
        rows = 128 * BLOCKS
        base = t * rows
        parts = []
        for rg in range(8):
            at = pl.ds(pl.multiple_of(rg * 4096 + base, rows), rows)
            parts.append(ga[at, :] + gb[at, :])
        hi, lo = split(jnp.concatenate(parts, axis=1))
        dims = (((1,), (1,)), ((), ()))
        block = lax.dot_general(picker[...], hi, dims, preferred_element_type=jnp.float32)
        block = block + lax.dot_general(picker[...], lo, dims, preferred_element_type=jnp.float32)
        block = block.reshape(8, 2, 8, rows)
        at = pl.ds(pl.multiple_of(lax.rem(t, 4 // BLOCKS) * rows, rows), rows)
        for v in range(2):
            for h in range(2):
                out[h, v, pl.ds(k2 * 4, 4), :, at] = block[h * 4 : h * 4 + 4, v]
        return carry

    lax.fori_loop(0, 32 // BLOCKS, gather, 0)
    body = pl.ds(0, 32)
    write = pltpu.make_async_copy(out.at[:, :, body], out_hbm.at[:, :, body], sems.at[2])
    write.start()

    quarter = lax.broadcasted_iota(jnp.int32, (32, 128), 1) // 32
    for h in range(2):
        for v in range(2):
            for side, (col, at) in enumerate(((0, 0), (384, 96))):
                for kk in range(2):
                    total = None
                    for kq in range(4):
                        x = out[h, v, pl.ds((kk * 4 + kq) * 4, 4), :, pl.ds(col, 128)].reshape(32, 128)
                        shift = (kq * 32 - at) % 128
                        x = pltpu.roll(x, shift, 1) if shift else x
                        total = x if total is None else jnp.where(quarter == kq, x, total)
                    out[h, v, pl.ds(32, 4), :, pl.ds((side * 2 + kk) * 128, 128)] = total.reshape(4, 8, 128)
    edge = pl.ds(32, 4)
    write_edge = pltpu.make_async_copy(out.at[:, :, edge], out_hbm.at[:, :, edge], sems.at[3])
    write_edge.start()
    write.wait()
    write_edge.wait()


def grid_tile(vals, cells, mixer):
    hbm = pl.BlockSpec(memory_space=pl.ANY)
    return pl.pallas_call(
        grid_kernel,
        out_shape=jax.ShapeDtypeStruct((2, 2, 36, 8, 512), jnp.float32),
        in_specs=[hbm] * 3,
        out_specs=hbm,
        scratch_shapes=[
            pltpu.VMEM((128, 16, 128), jnp.float32),
            pltpu.VMEM((128, 128), jnp.float32),
            pltpu.VMEM((2048, 128), jnp.float32),
            pltpu.VMEM((2, 2, 36, 8, 512), jnp.float32),
            pltpu.VMEM((128, 1024), jnp.bfloat16),
            pltpu.VMEM((128, 1, 128), jnp.int32),
            pltpu.SemaphoreType.DMA((4,)),
        ]
        + [pltpu.VMEM((32768, 128), jnp.float32)] * NACC
        + [pltpu.SMEM((128,), jnp.int32)] * 128,
        compiler_params=pltpu.CompilerParams(vmem_limit_bytes=VMEM),
        cost_estimate=pl.CostEstimate(flops=10**9, bytes_accessed=4 * 2**20, transcendentals=0),
        name="scatter",
    )(vals, cells, mixer)


def filter_kernel(n_lat, n_lon, x_hbm, t_hbm, a_hbm, out, x, e, y, t, a, send, recv, local):
    lat = lax.axis_index("lat")
    lon = lax.axis_index("lon")
    west = lax.rem(lon + n_lon - 1, n_lon)
    east = lax.rem(lon + 1, n_lon)
    north = lat - 1
    south = lat + 1
    has_north = lat > 0
    has_south = lat < n_lat - 1
    rows = pl.ds(0, 256)
    edge = pl.ds(256, 32)
    own = pl.ds(0, 2)
    upper, lower = pl.ds(0, 248), pl.ds(8, 248)

    barrier = pltpu.get_barrier_semaphore()

    def greet(where):
        pl.semaphore_signal(barrier, inc=1, device_id=where, device_id_type=MESH)

    @pl.when(has_north)
    def _():
        greet((north, lon))

    @pl.when(has_south)
    def _():
        greet((south, lon))

    greet((lat, west))
    greet((lat, east))

    loads = [
        pltpu.make_async_copy(x_hbm.at[:, :, rows], x.at[own], local.at[0]),
        pltpu.make_async_copy(t_hbm, t, local.at[1]),
        pltpu.make_async_copy(a_hbm, a, local.at[2]),
    ]
    for copy in loads:
        copy.start()
    ends = lat * (n_lat - 1 - lat)
    pl.semaphore_wait(barrier, jnp.where(ends == 0, 3, 4))

    def remote(src, dst, slot, where):
        return pltpu.make_async_remote_copy(
            src_ref=src, dst_ref=dst, send_sem=send.at[slot], recv_sem=recv.at[slot],
            device_id=where, device_id_type=MESH,
        )

    sides = [
        remote(x_hbm.at[:, :, edge, pl.ds(0, 256)], e.at[1, own], 0, (lat, west)),
        remote(x_hbm.at[:, :, edge, pl.ds(256, 256)], e.at[0, own], 1, (lat, east)),
    ]
    up = [
        remote(x_hbm.at[0, 0, upper], x.at[3, 0, upper], 2, (north, lon)),
        remote(x_hbm.at[0, 1, upper], x.at[3, 1, upper], 3, (north, lon)),
        remote(e.at[:, 0], e.at[:, 3], 4, (north, lon)),
    ]
    down = [
        remote(x_hbm.at[1, 0, lower], x.at[2, 0, lower], 5, (south, lon)),
        remote(x_hbm.at[1, 1, lower], x.at[2, 1, lower], 6, (south, lon)),
        remote(e.at[:, 1], e.at[:, 2], 7, (south, lon)),
    ]

    def ends_do(act, which):
        @pl.when(has_north)
        def _():
            for i in which:
                act(up[i])

        @pl.when(has_south)
        def _():
            for i in which:
                act(down[i])

    def arrived(which):
        @pl.when(has_north)
        def _():
            for i in which:
                down[i].wait_recv()

        @pl.when(has_south)
        def _():
            for i in which:
                up[i].wait_recv()

    for copy in sides:
        copy.start()
    ends_do(lambda copy: copy.start(), (0,))

    x[2, :, pl.ds(0, 8)] = jnp.zeros((2, 8, 512), jnp.float32)
    x[3, :, pl.ds(248, 8)] = jnp.zeros((2, 8, 512), jnp.float32)
    for s, there in ((2, has_north), (3, has_south)):
        @pl.when(jnp.logical_not(there))
        def _():
            x[s] = jnp.zeros((2, 256, 512), jnp.float32)
            e[:, s] = jnp.zeros((2, 2, 32, 256), jnp.float32)

    def centre(s, v):
        total = dot3(split(x[pl.ds(s, 2), v].reshape(512, 512)), (t[0, v, 0:512], t[1, v, 0:512]))
        for u in range(2):
            for cb in range(4):
                y[s + u, v, cb] = total[u * 256 : u * 256 + 256, cb * 128 : cb * 128 + 128]

    def rims(s, v):
        for side in range(2):
            lines = [e[side, s + u, v, :, pl.ds(kk * 128, 128)] for u in range(2) for kk in range(2)]
            rim = dot3(split(jnp.concatenate(lines, axis=0)), (t[0, v, pl.ds(512 + side * 128, 128)], t[1, v, pl.ds(512 + side * 128, 128)]))
            for u in range(2):
                for k2 in range(8):
                    line = (u * 2 + k2 // 4) * 32
                    col = (k2 % 4) * 128
                    y[s + u, v, side * 3, pl.ds(k2 * 32, 32)] += rim[line : line + 32, col : col + 128]

    def along_lat(s, v):
        def levels(i, carry):
            for u in range(4):
                l = i * 4 + u
                line = jnp.concatenate(
                    [
                        jnp.concatenate([y[s + k, v, cb, pl.ds(l, 32, stride=8), :] for cb in range(4)], axis=1)
                        for k in range(2)
                    ],
                    axis=0,
                )
                hi, lo = split(line)
                part = dot(a[s // 2, v], jnp.concatenate([hi, hi, lo], axis=0))
                out[v, l] = part if s == 0 else out[v, l] + part
            return carry

        lax.fori_loop(0, LEV // 4, levels, 0)

    for copy in loads:
        copy.wait()
    centre(0, 0)
    for copy in sides:
        copy.wait_recv()
    ends_do(lambda copy: copy.start(), (2, 1))
    centre(0, 1)
    for v in range(2):
        rims(0, v)
        along_lat(0, v)

    for v in range(2):
        arrived((v, 2) if v == 0 else (v,))
        centre(2, v)
        rims(2, v)
        along_lat(2, v)

    for copy in sides:
        copy.wait_send()
    ends_do(lambda copy: copy.wait_send(), (0, 1, 2))


def filter_tile(n_lat, n_lon, x, weights):
    return pl.pallas_call(
        functools.partial(filter_kernel, n_lat, n_lon),
        out_shape=jax.ShapeDtypeStruct((2, 8, 64, 512), jnp.float32),
        in_specs=[pl.BlockSpec(memory_space=pl.ANY)] * 3,
        out_specs=pl.BlockSpec(memory_space=pltpu.VMEM),
        scratch_shapes=[
            pltpu.VMEM((4, 2, 256, 512), jnp.float32),
            pltpu.VMEM((2, 4, 2, 32, 256), jnp.float32),
            pltpu.VMEM((4, 2, 4, 256, 128), jnp.float32),
            pltpu.VMEM((2, 2, 768, 512), jnp.bfloat16),
            pltpu.VMEM((2, 2, 64, 192), jnp.bfloat16),
            pltpu.SemaphoreType.DMA((8,)),
            pltpu.SemaphoreType.DMA((8,)),
            pltpu.SemaphoreType.DMA((3,)),
        ],
        compiler_params=pltpu.CompilerParams(
            vmem_limit_bytes=101 * 2**19, collective_id=0, has_side_effects=True
        ),
        cost_estimate=pl.CostEstimate(flops=6 * 10**9, bytes_accessed=8 * 2**20, transcendentals=0),
        name="filters",
    )(x, *weights)


def route_kernel(n_lat, n_lon, obs_hbm, cells_hbm, counts_hbm, lengths_hbm, weights_hbm, mix_hbm,
                 vals, cells, mixer, t_out, a_out,
                 box, cell_box, counts, lengths, weights, mix, tiles, local, send, recv):
    lat = lax.axis_index("lat")
    lon = lax.axis_index("lon")
    me = lat * n_lon + lon
    count = n_lat * n_lon

    loads = [
        pltpu.make_async_copy(src, dst, local.at[i])
        for i, (src, dst) in enumerate(
            ((obs_hbm, box), (cells_hbm, cell_box), (counts_hbm, counts), (lengths_hbm, lengths),
             (weights_hbm, weights), (mix_hbm, mix))
        )
    ]
    for copy in loads:
        copy.start()

    barrier = pltpu.get_barrier_semaphore()

    columns = [lon] + [lax.rem(lon + k, n_lon) for k in range(1, n_lon)]

    def each_peer(act):
        for k in range(1, n_lon):
            act(lat, columns[k])

        def line(i, carry):
            for column in columns:
                act(lax.rem(lat + i, n_lat), column)
            return carry

        lax.fori_loop(1, n_lat, line, 0)

    def greet(to_lat, to_lon):
        pl.semaphore_signal(barrier, inc=1, device_id=(to_lat, to_lon), device_id_type=MESH)

    each_peer(greet)
    for copy in loads:
        copy.wait()

    slot = lax.broadcasted_iota(jnp.int32, (16, 128), 1)

    def mask(i, carry):
        for u in range(8):
            d = i * 8 + u
            box[d] = jnp.where(slot < counts[0, d], box[d], 0.0)
        return carry

    lax.fori_loop(0, count // 8, mask, 0)
    pl.semaphore_wait(barrier, count - 1)

    def give(to_lat, to_lon):
        d = to_lat * n_lon + to_lon
        for i, (src, dst) in enumerate(((box, vals), (cell_box, cells))):
            pltpu.make_async_remote_copy(
                src_ref=src.at[d], dst_ref=dst.at[me], send_sem=send.at[i], recv_sem=recv.at[i],
                device_id=(to_lat, to_lon), device_id_type=MESH,
            ).start()

    each_peer(give)
    pltpu.make_async_copy(cell_box.at[me], cells.at[me], recv.at[1]).start()
    pltpu.make_async_copy(box.at[me], vals.at[me], recv.at[0]).start()

    def iota(shape, dim):
        return lax.broadcasted_iota(jnp.int32, shape, dim)

    def profile(v, offset):
        t = offset.astype(jnp.float32)
        total = 0.0
        for s in range(3):
            scale = t / lengths[v, s]
            total = total + weights[v, s] * jnp.exp(-0.5 * (scale * scale))
        return jnp.where(jnp.abs(offset) <= HALF, total, 0.0)

    flat = (128, 128)
    for v in range(2):
        taps = profile(v, iota((8, 128), 1) - HALF)
        norm = lax.rsqrt(jnp.sum(taps * taps, axis=1, keepdims=True))[0:1, 0:1]
        for i in range(3):
            hi, lo = split(profile(v, iota(flat, 0) - iota(flat, 1) + (i - 1) * 128) * norm)
            tiles[0, i] = hi
            tiles[1, i] = lo
        blank = jnp.zeros(flat, jnp.bfloat16)
        for p in range(2):
            for i in range(4):
                for j in range(4):
                    piece = tiles[p, i - j + 1] if abs(i - j) <= 1 else blank
                    t_out[p, v, pl.ds(i * 128, 128), pl.ds(j * 128, 128)] = piece
            t_out[p, v, pl.ds(512, 256)] = jnp.zeros((256, 512), jnp.bfloat16)
            for kq in range(4):
                at = pl.ds(kq * 128, 128)
                t_out[p, v, pl.ds(512 + kq * 32, 32), at] = tiles[p, 0, pl.ds(96, 32)]
                t_out[p, v, pl.ds(640 + kq * 32, 32), at] = tiles[p, 2, pl.ds(0, 32)]
        k = iota((64, 192), 1)
        place = lax.rem(k, 32)
        inner = lax.rem(place, 4) * 8 + place // 4
        second = lax.rem(k, 64) // 32
        for part in range(2):
            base = second * 32 if part == 0 else second * 96 - 32
            hi, lo = split(profile(v, base + inner - iota((64, 192), 0)) * norm)
            a_out[part, v] = jnp.where(k // 64 == 1, lo.astype(jnp.float32), hi.astype(jnp.float32)).astype(jnp.bfloat16)

    row, col = iota((16, 128), 0), iota((16, 128), 1)
    small = jnp.zeros((16, 128), jnp.float32)
    for v in range(2):
        for l in range(LEV):
            for m in range(LEV):
                here = (row == v * LEV + m) & (lax.rem(col, 16) == v * LEV + l)
                small = jnp.where(here, mix[v, l, m], small)
    for i in range(8):
        mixer[pl.ds(i * 16, 16)] = jnp.where(col // 16 == i, small, 0.0)

    rest = pl.ds(0, count - 1)
    for i, (src, dst) in enumerate(((box, vals), (cell_box, cells))):
        pltpu.make_async_copy(dst, dst, recv.at[i]).wait()
        pltpu.make_async_copy(src.at[rest], dst.at[rest], send.at[i]).wait()


def route(n_lat, n_lon, obs, cells, counts, lengths, weights, mix):
    n = n_lat * n_lon
    hbm = pl.BlockSpec(memory_space=pl.ANY)
    bf16 = jnp.bfloat16
    return pl.pallas_call(
        functools.partial(route_kernel, n_lat, n_lon),
        out_shape=(
            jax.ShapeDtypeStruct((n, 16, 128), jnp.float32),
            jax.ShapeDtypeStruct((n, 1, 128), jnp.int32),
            jax.ShapeDtypeStruct((128, 128), jnp.float32),
            jax.ShapeDtypeStruct((2, 2, 768, 512), bf16),
            jax.ShapeDtypeStruct((2, 2, 64, 192), bf16),
        ),
        in_specs=[hbm] * 6,
        out_specs=[hbm] * 2 + [pl.BlockSpec(memory_space=pltpu.VMEM)] * 3,
        scratch_shapes=[
            pltpu.VMEM((n, 16, 128), jnp.float32),
            pltpu.VMEM((n, 1, 128), jnp.int32),
            pltpu.SMEM((1, n), jnp.int32),
            pltpu.SMEM((2, 3), jnp.float32),
            pltpu.SMEM((2, 3), jnp.float32),
            pltpu.SMEM((2, LEV, LEV), jnp.float32),
            pltpu.VMEM((2, 3, 128, 128), bf16),
            pltpu.SemaphoreType.DMA((6,)),
            pltpu.SemaphoreType.DMA((2,)),
            pltpu.SemaphoreType.DMA((2,)),
        ],
        compiler_params=pltpu.CompilerParams(vmem_limit_bytes=VMEM, collective_id=1, has_side_effects=True),
        cost_estimate=pl.CostEstimate(flops=10**7, bytes_accessed=4 * 2**20, transcendentals=0),
        name="route",
    )(obs, cells, counts, lengths, weights, mix)


def local(obs_values, obs_cells, obs_counts, filter_lengths, filter_weights, vertical_mix):
    n_lat, n_lon = lax.axis_size("lat"), lax.axis_size("lon")
    n = n_lat * n_lon
    vals, cells, mixer, *weights = route(
        n_lat, n_lon, obs_values.reshape(n, 16, 128), obs_cells.reshape(n, 1, 128), obs_counts,
        filter_lengths, filter_weights, vertical_mix,
    )
    x = grid_tile(vals, cells, mixer)
    return filter_tile(n_lat, n_lon, x.reshape(2, 2, 288, 512), weights)


def solution(mesh):
    in_specs = (
        P(("lat", "lon"), None, None, None, None),
        P(("lat", "lon"), None, None),
        P(("lat", "lon"), None),
        P(),
        P(),
        P(),
    )
    return jax.shard_map(
        local, mesh=mesh, in_specs=in_specs, out_specs=P(None, None, "lat", "lon"), check_vma=False
    )
```

```python
import functools

import jax
import jax.numpy as jnp
from jax import lax
from jax.experimental import pallas as pl
from jax.experimental.pallas import tpu as pltpu
from jax.sharding import PartitionSpec as P

HALF = 31
LEV = 8
NACC = 3
UNROLL = 4
AHEAD = 1
BLOCKS = 4
VMEM = 62 * 2**20
MESH = pl.DeviceIdType.MESH


def split(x):
    hi = x.astype(jnp.bfloat16)
    return hi, (x - hi.astype(jnp.float32)).astype(jnp.bfloat16)


def dot(a, b):
    return jnp.dot(a, b, preferred_element_type=jnp.float32)


def dot3(a, b):
    return dot(a[0], b[0]) + dot(a[1], b[0]) + dot(a[0], b[1])


def grid_kernel(vals_hbm, cells_hbm, mixer_hbm, out_hbm, vals, mixer, table, out, picker, sized, sems, ga, gb, gc, *cells):
    grids = (ga, gb, gc)
    loads = [
        pltpu.make_async_copy(vals_hbm, vals, sems.at[0]),
        pltpu.make_async_copy(mixer_hbm, mixer, sems.at[2]),
    ]
    for copy in loads:
        copy.start()
    for s in range(128):
        pltpu.make_async_copy(cells_hbm.at[s, 0], cells[s], sems.at[1]).start()

    def clear(i, carry):
        for grid in (gb, gc):
            grid[pl.ds(pl.multiple_of(i * 512, 512), 512), :] = jnp.zeros((512, 128), jnp.float32)
        return carry

    lax.fori_loop(0, 64, clear, 0)
    for copy in loads:
        copy.wait()
    mix = split(mixer[...])

    def fill(i, carry):
        ga[pl.ds(pl.multiple_of(i * 4096, 4096), 4096), :] = jnp.zeros((4096, 128), jnp.float32)
        for u in range(2):
            g = i * 2 + u
            rows = vals[pl.ds(pl.multiple_of(g * 8, 8), 8)].reshape(128, 128).T
            table[pl.ds(pl.multiple_of(g * 128, 128), 128), :] = dot3(split(rows), mix)
        return carry

    lax.fori_loop(0, 8, fill, 0)
    lane = lax.broadcasted_iota(jnp.int32, (1, 128), 1) // 16
    masks = [lane == i for i in range(8)]
    pltpu.make_async_copy(cells_hbm, sized, sems.at[1]).wait()

    def batch(turn, n, j):
        grid = grids[turn % NACC]
        row = table[pl.ds(n * 128 + j, 1), :]
        places = [cells[n * 8 + i][j] for i in range(8)]
        return grid, places, [grid[pl.ds(c, 1), :] + row for c in places]

    def scatter(t, carry):
        order = [(n, t * UNROLL + u) for u in range(UNROLL) for n in range(16)]
        ahead = [batch(i, *order[i]) for i in range(AHEAD)]
        for i in range(len(order)):
            grid, places, totals = ahead.pop(0)
            if i + AHEAD < len(order):
                ahead.append(batch(i + AHEAD, *order[i + AHEAD]))
            for c, total, live in zip(places, totals, masks):
                pltpu.store(grid.at[pl.ds(c, 1), :], total, mask=live)
        return carry

    lax.fori_loop(0, 128 // UNROLL, scatter, 0)

    r, c = lax.broadcasted_iota(jnp.int32, (128, 128), 0), lax.broadcasted_iota(jnp.int32, (128, 128), 1)
    for rg in range(8):
        hit = (lax.rem(r, 16) == lax.rem(c, 16)) & (r // 16 == rg)
        picker[:, pl.ds(rg * 128, 128)] = jnp.where(hit, 1.0, 0.0).astype(jnp.bfloat16)

    def gather(t, carry):
        k2 = t // (4 // BLOCKS)
        rows = 128 * BLOCKS
        base = t * rows
        parts = []
        for rg in range(8):
            at = pl.ds(pl.multiple_of(rg * 4096 + base, rows), rows)
            parts.append(ga[at, :] + gb[at, :] + gc[at, :])
        hi, lo = split(jnp.concatenate(parts, axis=1))
        dims = (((1,), (1,)), ((), ()))
        block = lax.dot_general(picker[...], hi, dims, preferred_element_type=jnp.float32)
        block = block + lax.dot_general(picker[...], lo, dims, preferred_element_type=jnp.float32)
        block = block.reshape(8, 2, 8, rows)
        at = pl.ds(pl.multiple_of(lax.rem(t, 4 // BLOCKS) * rows, rows), rows)
        for v in range(2):
            for h in range(2):
                out[h, v, pl.ds(k2 * 4, 4), :, at] = block[h * 4 : h * 4 + 4, v]
        return carry

    lax.fori_loop(0, 32 // BLOCKS, gather, 0)
    body = pl.ds(0, 32)
    write = pltpu.make_async_copy(out.at[:, :, body], out_hbm.at[:, :, body], sems.at[2])
    write.start()

    quarter = lax.broadcasted_iota(jnp.int32, (32, 128), 1) // 32
    for h in range(2):
        for v in range(2):
            for side, (col, at) in enumerate(((0, 0), (384, 96))):
                for kk in range(2):
                    total = None
                    for kq in range(4):
                        x = out[h, v, pl.ds((kk * 4 + kq) * 4, 4), :, pl.ds(col, 128)].reshape(32, 128)
                        shift = (kq * 32 - at) % 128
                        x = pltpu.roll(x, shift, 1) if shift else x
                        total = x if total is None else jnp.where(quarter == kq, x, total)
                    out[h, v, pl.ds(32, 4), :, pl.ds((side * 2 + kk) * 128, 128)] = total.reshape(4, 8, 128)
    edge = pl.ds(32, 4)
    write_edge = pltpu.make_async_copy(out.at[:, :, edge], out_hbm.at[:, :, edge], sems.at[3])
    write_edge.start()
    write.wait()
    write_edge.wait()


def grid_tile(vals, cells, mixer):
    hbm = pl.BlockSpec(memory_space=pl.ANY)
    return pl.pallas_call(
        grid_kernel,
        out_shape=jax.ShapeDtypeStruct((2, 2, 36, 8, 512), jnp.float32),
        in_specs=[hbm] * 3,
        out_specs=hbm,
        scratch_shapes=[
            pltpu.VMEM((128, 16, 128), jnp.float32),
            pltpu.VMEM((128, 128), jnp.float32),
            pltpu.VMEM((2048, 128), jnp.float32),
            pltpu.VMEM((2, 2, 36, 8, 512), jnp.float32),
            pltpu.VMEM((128, 1024), jnp.bfloat16),
            pltpu.VMEM((128, 1, 128), jnp.int32),
            pltpu.SemaphoreType.DMA((4,)),
        ]
        + [pltpu.VMEM((32768, 128), jnp.float32)] * NACC
        + [pltpu.SMEM((128,), jnp.int32)] * 128,
        compiler_params=pltpu.CompilerParams(vmem_limit_bytes=VMEM),
        cost_estimate=pl.CostEstimate(flops=10**9, bytes_accessed=4 * 2**20, transcendentals=0),
        name="scatter",
    )(vals, cells, mixer)


def filter_kernel(n_lat, n_lon, x_hbm, t_hbm, a_hbm, out, x, e, y, t, a, send, recv, local):
    lat = lax.axis_index("lat")
    lon = lax.axis_index("lon")
    west = lax.rem(lon + n_lon - 1, n_lon)
    east = lax.rem(lon + 1, n_lon)
    north = lat - 1
    south = lat + 1
    has_north = lat > 0
    has_south = lat < n_lat - 1
    rows = pl.ds(0, 256)
    edge = pl.ds(256, 32)
    own = pl.ds(0, 2)
    upper, lower = pl.ds(0, 248), pl.ds(8, 248)

    barrier = pltpu.get_barrier_semaphore()

    def greet(where):
        pl.semaphore_signal(barrier, inc=1, device_id=where, device_id_type=MESH)

    @pl.when(has_north)
    def _():
        greet((north, lon))

    @pl.when(has_south)
    def _():
        greet((south, lon))

    greet((lat, west))
    greet((lat, east))

    loads = [
        pltpu.make_async_copy(x_hbm.at[:, :, rows], x.at[own], local.at[0]),
        pltpu.make_async_copy(t_hbm, t, local.at[1]),
        pltpu.make_async_copy(a_hbm, a, local.at[2]),
    ]
    for copy in loads:
        copy.start()
    ends = lat * (n_lat - 1 - lat)
    pl.semaphore_wait(barrier, jnp.where(ends == 0, 3, 4))

    def remote(src, dst, slot, where):
        return pltpu.make_async_remote_copy(
            src_ref=src, dst_ref=dst, send_sem=send.at[slot], recv_sem=recv.at[slot],
            device_id=where, device_id_type=MESH,
        )

    sides = [
        remote(x_hbm.at[:, :, edge, pl.ds(0, 256)], e.at[1, own], 0, (lat, west)),
        remote(x_hbm.at[:, :, edge, pl.ds(256, 256)], e.at[0, own], 1, (lat, east)),
    ]
    up = [
        remote(x_hbm.at[0, 0, upper], x.at[3, 0, upper], 2, (north, lon)),
        remote(x_hbm.at[0, 1, pl.ds(0, 128)], x.at[3, 1, pl.ds(0, 128)], 3, (north, lon)),
        remote(x_hbm.at[0, 1, pl.ds(128, 120)], x.at[3, 1, pl.ds(128, 120)], 8, (north, lon)),
        remote(e.at[:, 0], e.at[:, 3], 4, (north, lon)),
    ]
    down = [
        remote(x_hbm.at[1, 0, lower], x.at[2, 0, lower], 5, (south, lon)),
        remote(x_hbm.at[1, 1, pl.ds(128, 128)], x.at[2, 1, pl.ds(128, 128)], 6, (south, lon)),
        remote(x_hbm.at[1, 1, pl.ds(8, 120)], x.at[2, 1, pl.ds(8, 120)], 9, (south, lon)),
        remote(e.at[:, 1], e.at[:, 2], 7, (south, lon)),
    ]

    def ends_do(act, which):
        @pl.when(has_north)
        def _():
            for i in which:
                act(up[i])

        @pl.when(has_south)
        def _():
            for i in which:
                act(down[i])

    def arrived(which):
        @pl.when(has_north)
        def _():
            for i in which:
                down[i].wait_recv()

        @pl.when(has_south)
        def _():
            for i in which:
                up[i].wait_recv()

    for copy in sides:
        copy.start()
    ends_do(lambda copy: copy.start(), (0, 1))

    x[2, :, pl.ds(0, 8)] = jnp.zeros((2, 8, 512), jnp.float32)
    x[3, :, pl.ds(248, 8)] = jnp.zeros((2, 8, 512), jnp.float32)
    for s, there in ((2, has_north), (3, has_south)):
        @pl.when(jnp.logical_not(there))
        def _():
            x[s] = jnp.zeros((2, 256, 512), jnp.float32)
            e[:, s] = jnp.zeros((2, 2, 32, 256), jnp.float32)

    def centre(s, v):
        hi, lo = split(x[pl.ds(s, 2), v].reshape(512, 512))
        for n in range(2):
            deep, wide = slice(n * 128, n * 128 + 384), pl.ds(n * 256, 256)
            band = t[0, v, pl.ds(n * 128, 384), wide], t[1, v, pl.ds(n * 128, 384), wide]
            total = dot3((hi[:, deep], lo[:, deep]), band)
            for u in range(2):
                for cb in range(2):
                    y[s + u, v, n * 2 + cb] = total[u * 256 : u * 256 + 256, cb * 128 : cb * 128 + 128]

    def rims(s, v):
        for side in range(2):
            lines = [e[side, s + u, v, :, pl.ds(kk * 128, 128)] for u in range(2) for kk in range(2)]
            rim = dot3(split(jnp.concatenate(lines, axis=0)), (t[0, v, pl.ds(512 + side * 128, 128)], t[1, v, pl.ds(512 + side * 128, 128)]))
            for u in range(2):
                for k2 in range(8):
                    line = (u * 2 + k2 // 4) * 32
                    col = (k2 % 4) * 128
                    y[s + u, v, side * 3, pl.ds(k2 * 32, 32)] += rim[line : line + 32, col : col + 128]

    def along_lat(s, v):
        def levels(i, carry):
            for u in range(4):
                l = i * 4 + u
                line = jnp.concatenate(
                    [
                        jnp.concatenate([y[s + k, v, cb, pl.ds(l, 32, stride=8), :] for cb in range(4)], axis=1)
                        for k in range(2)
                    ],
                    axis=0,
                )
                hi, lo = split(line)
                part = dot(a[s // 2, v], jnp.concatenate([hi, hi, lo], axis=0))
                out[v, l] = part if s == 0 else out[v, l] + part
            return carry

        lax.fori_loop(0, LEV // 4, levels, 0)

    for copy in loads:
        copy.wait()
    centre(0, 0)
    for copy in sides:
        copy.wait_recv()
    ends_do(lambda copy: copy.start(), (3, 2))
    centre(0, 1)
    for v in range(2):
        rims(0, v)
        along_lat(0, v)

    for v in range(2):
        arrived((0, 3) if v == 0 else (1, 2))
        centre(2, v)
        rims(2, v)
        along_lat(2, v)

    for copy in sides:
        copy.wait_send()
    ends_do(lambda copy: copy.wait_send(), (0, 1, 2, 3))


def filter_tile(n_lat, n_lon, x, weights):
    return pl.pallas_call(
        functools.partial(filter_kernel, n_lat, n_lon),
        out_shape=jax.ShapeDtypeStruct((2, 8, 64, 512), jnp.float32),
        in_specs=[pl.BlockSpec(memory_space=pl.ANY)] * 3,
        out_specs=pl.BlockSpec(memory_space=pltpu.VMEM),
        scratch_shapes=[
            pltpu.VMEM((4, 2, 256, 512), jnp.float32),
            pltpu.VMEM((2, 4, 2, 32, 256), jnp.float32),
            pltpu.VMEM((4, 2, 4, 256, 128), jnp.float32),
            pltpu.VMEM((2, 2, 768, 512), jnp.bfloat16),
            pltpu.VMEM((2, 2, 64, 192), jnp.bfloat16),
            pltpu.SemaphoreType.DMA((10,)),
            pltpu.SemaphoreType.DMA((10,)),
            pltpu.SemaphoreType.DMA((3,)),
        ],
        compiler_params=pltpu.CompilerParams(
            vmem_limit_bytes=101 * 2**19, collective_id=0, has_side_effects=True
        ),
        cost_estimate=pl.CostEstimate(flops=6 * 10**9, bytes_accessed=8 * 2**20, transcendentals=0),
        name="filters",
    )(x, *weights)


def route_kernel(n_lat, n_lon, obs_hbm, cells_hbm, counts_hbm, lengths_hbm, weights_hbm, mix_hbm,
                 vals, cells, mixer, t_out, a_out,
                 box, cell_box, counts, lengths, weights, mix, tiles, local, send, recv):
    lat = lax.axis_index("lat")
    lon = lax.axis_index("lon")
    me = lat * n_lon + lon
    count = n_lat * n_lon

    loads = [
        pltpu.make_async_copy(src, dst, local.at[i])
        for i, (src, dst) in enumerate(
            ((obs_hbm, box), (cells_hbm, cell_box), (counts_hbm, counts), (lengths_hbm, lengths),
             (weights_hbm, weights), (mix_hbm, mix))
        )
    ]
    for copy in loads:
        copy.start()

    barrier = pltpu.get_barrier_semaphore()

    columns = [lon] + [lax.rem(lon + k, n_lon) for k in range(1, n_lon)]

    def each_peer(act):
        for k in range(1, n_lon):
            act(lat, columns[k])

        def line(i, carry):
            for column in columns:
                act(lax.rem(lat + i, n_lat), column)
            return carry

        lax.fori_loop(1, n_lat, line, 0)

    def greet(to_lat, to_lon):
        pl.semaphore_signal(barrier, inc=1, device_id=(to_lat, to_lon), device_id_type=MESH)

    each_peer(greet)
    for copy in loads:
        copy.wait()

    slot = lax.broadcasted_iota(jnp.int32, (16, 128), 1)

    def mask(i, carry):
        for u in range(8):
            d = i * 8 + u
            box[d] = jnp.where(slot < counts[0, d], box[d], 0.0)
        return carry

    lax.fori_loop(0, count // 8, mask, 0)
    pl.semaphore_wait(barrier, count - 1)

    def give(to_lat, to_lon):
        d = to_lat * n_lon + to_lon
        for i, (src, dst) in enumerate(((box, vals), (cell_box, cells))):
            pltpu.make_async_remote_copy(
                src_ref=src.at[d], dst_ref=dst.at[me], send_sem=send.at[i], recv_sem=recv.at[i],
                device_id=(to_lat, to_lon), device_id_type=MESH,
            ).start()

    each_peer(give)
    pltpu.make_async_copy(cell_box.at[me], cells.at[me], recv.at[1]).start()
    pltpu.make_async_copy(box.at[me], vals.at[me], recv.at[0]).start()

    def iota(shape, dim):
        return lax.broadcasted_iota(jnp.int32, shape, dim)

    def profile(v, offset):
        t = offset.astype(jnp.float32)
        total = 0.0
        for s in range(3):
            scale = t / lengths[v, s]
            total = total + weights[v, s] * jnp.exp(-0.5 * (scale * scale))
        return jnp.where(jnp.abs(offset) <= HALF, total, 0.0)

    flat = (128, 128)
    for v in range(2):
        taps = profile(v, iota((8, 128), 1) - HALF)
        norm = lax.rsqrt(jnp.sum(taps * taps, axis=1, keepdims=True))[0:1, 0:1]
        for i in range(3):
            hi, lo = split(profile(v, iota(flat, 0) - iota(flat, 1) + (i - 1) * 128) * norm)
            tiles[0, i] = hi
            tiles[1, i] = lo
        blank = jnp.zeros(flat, jnp.bfloat16)
        for p in range(2):
            for i in range(4):
                for j in range(4):
                    piece = tiles[p, i - j + 1] if abs(i - j) <= 1 else blank
                    t_out[p, v, pl.ds(i * 128, 128), pl.ds(j * 128, 128)] = piece
            t_out[p, v, pl.ds(512, 256)] = jnp.zeros((256, 512), jnp.bfloat16)
            for kq in range(4):
                at = pl.ds(kq * 128, 128)
                t_out[p, v, pl.ds(512 + kq * 32, 32), at] = tiles[p, 0, pl.ds(96, 32)]
                t_out[p, v, pl.ds(640 + kq * 32, 32), at] = tiles[p, 2, pl.ds(0, 32)]
        k = iota((64, 192), 1)
        place = lax.rem(k, 32)
        inner = lax.rem(place, 4) * 8 + place // 4
        second = lax.rem(k, 64) // 32
        for part in range(2):
            base = second * 32 if part == 0 else second * 96 - 32
            hi, lo = split(profile(v, base + inner - iota((64, 192), 0)) * norm)
            a_out[part, v] = jnp.where(k // 64 == 1, lo.astype(jnp.float32), hi.astype(jnp.float32)).astype(jnp.bfloat16)

    row, col = iota((16, 128), 0), iota((16, 128), 1)
    small = jnp.zeros((16, 128), jnp.float32)
    for v in range(2):
        for l in range(LEV):
            for m in range(LEV):
                here = (row == v * LEV + m) & (lax.rem(col, 16) == v * LEV + l)
                small = jnp.where(here, mix[v, l, m], small)
    for i in range(8):
        mixer[pl.ds(i * 16, 16)] = jnp.where(col // 16 == i, small, 0.0)

    rest = pl.ds(0, count - 1)
    for i, (src, dst) in enumerate(((box, vals), (cell_box, cells))):
        pltpu.make_async_copy(dst, dst, recv.at[i]).wait()
        pltpu.make_async_copy(src.at[rest], dst.at[rest], send.at[i]).wait()


def route(n_lat, n_lon, obs, cells, counts, lengths, weights, mix):
    n = n_lat * n_lon
    hbm = pl.BlockSpec(memory_space=pl.ANY)
    bf16 = jnp.bfloat16
    return pl.pallas_call(
        functools.partial(route_kernel, n_lat, n_lon),
        out_shape=(
            jax.ShapeDtypeStruct((n, 16, 128), jnp.float32),
            jax.ShapeDtypeStruct((n, 1, 128), jnp.int32),
            jax.ShapeDtypeStruct((128, 128), jnp.float32),
            jax.ShapeDtypeStruct((2, 2, 768, 512), bf16),
            jax.ShapeDtypeStruct((2, 2, 64, 192), bf16),
        ),
        in_specs=[hbm] * 6,
        out_specs=[hbm] * 2 + [pl.BlockSpec(memory_space=pltpu.VMEM)] * 3,
        scratch_shapes=[
            pltpu.VMEM((n, 16, 128), jnp.float32),
            pltpu.VMEM((n, 1, 128), jnp.int32),
            pltpu.SMEM((1, n), jnp.int32),
            pltpu.SMEM((2, 3), jnp.float32),
            pltpu.SMEM((2, 3), jnp.float32),
            pltpu.SMEM((2, LEV, LEV), jnp.float32),
            pltpu.VMEM((2, 3, 128, 128), bf16),
            pltpu.SemaphoreType.DMA((6,)),
            pltpu.SemaphoreType.DMA((2,)),
            pltpu.SemaphoreType.DMA((2,)),
        ],
        compiler_params=pltpu.CompilerParams(vmem_limit_bytes=VMEM, collective_id=1, has_side_effects=True),
        cost_estimate=pl.CostEstimate(flops=10**7, bytes_accessed=4 * 2**20, transcendentals=0),
        name="route",
    )(obs, cells, counts, lengths, weights, mix)


def local(obs_values, obs_cells, obs_counts, filter_lengths, filter_weights, vertical_mix):
    n_lat, n_lon = lax.axis_size("lat"), lax.axis_size("lon")
    n = n_lat * n_lon
    vals, cells, mixer, *weights = route(
        n_lat, n_lon, obs_values.reshape(n, 16, 128), obs_cells.reshape(n, 1, 128), obs_counts,
        filter_lengths, filter_weights, vertical_mix,
    )
    x = grid_tile(vals, cells, mixer)
    return filter_tile(n_lat, n_lon, x.reshape(2, 2, 288, 512), weights)


def solution(mesh):
    in_specs = (
        P(("lat", "lon"), None, None, None, None),
        P(("lat", "lon"), None, None),
        P(("lat", "lon"), None),
        P(),
        P(),
        P(),
    )
    return jax.shard_map(
        local, mesh=mesh, in_specs=in_specs, out_specs=P(None, None, "lat", "lon"), check_vma=False
    )
```

```python
import functools

import jax
import jax.numpy as jnp
from jax import lax
from jax.experimental import pallas as pl
from jax.experimental.pallas import tpu as pltpu
from jax.sharding import PartitionSpec as P

HALF = 31
LEV = 8
NACC = 3
UNROLL = 4
AHEAD = 1
BLOCKS = 4
VMEM = 62 * 2**20
MESH = pl.DeviceIdType.MESH


def split(x):
    hi = x.astype(jnp.bfloat16)
    return hi, (x - hi.astype(jnp.float32)).astype(jnp.bfloat16)


def dot(a, b):
    return jnp.dot(a, b, preferred_element_type=jnp.float32)


def dot3(a, b):
    return dot(a[0], b[0]) + dot(a[1], b[0]) + dot(a[0], b[1])


def grid_kernel(vals_hbm, cells_hbm, mixer_hbm, out_hbm, vals, mixer, table, out, picker, sized, sems, stores, ga, gb, gc, *cells):
    grids = (ga, gb, gc)
    loads = [
        pltpu.make_async_copy(vals_hbm, vals, sems.at[0]),
        pltpu.make_async_copy(mixer_hbm, mixer, sems.at[2]),
    ]
    for copy in loads:
        copy.start()
    for s in range(128):
        pltpu.make_async_copy(cells_hbm.at[s, 0], cells[s], sems.at[1]).start()

    def clear(i, carry):
        for grid in (gb, gc):
            grid[pl.ds(pl.multiple_of(i * 512, 512), 512), :] = jnp.zeros((512, 128), jnp.float32)
        return carry

    lax.fori_loop(0, 64, clear, 0)
    for copy in loads:
        copy.wait()
    mix = split(mixer[...])

    def fill(i, carry):
        ga[pl.ds(pl.multiple_of(i * 4096, 4096), 4096), :] = jnp.zeros((4096, 128), jnp.float32)
        for u in range(2):
            g = i * 2 + u
            rows = vals[pl.ds(pl.multiple_of(g * 8, 8), 8)].reshape(128, 128).T
            table[pl.ds(pl.multiple_of(g * 128, 128), 128), :] = dot3(split(rows), mix)
        return carry

    lax.fori_loop(0, 8, fill, 0)
    lane = lax.broadcasted_iota(jnp.int32, (1, 128), 1) // 16
    masks = [lane == i for i in range(8)]
    pltpu.make_async_copy(cells_hbm, sized, sems.at[1]).wait()

    def batch(turn, n, j):
        grid = grids[turn % NACC]
        row = table[pl.ds(n * 128 + j, 1), :]
        places = [cells[n * 8 + i][j] for i in range(8)]
        return grid, places, [grid[pl.ds(c, 1), :] + row for c in places]

    def scatter(t, carry):
        order = [(n, t * UNROLL + u) for u in range(UNROLL) for n in range(16)]
        ahead = [batch(i, *order[i]) for i in range(AHEAD)]
        for i in range(len(order)):
            grid, places, totals = ahead.pop(0)
            if i + AHEAD < len(order):
                ahead.append(batch(i + AHEAD, *order[i + AHEAD]))
            for c, total, live in zip(places, totals, masks):
                pltpu.store(grid.at[pl.ds(c, 1), :], total, mask=live)
        return carry

    lax.fori_loop(0, 128 // UNROLL, scatter, 0)

    r, c = lax.broadcasted_iota(jnp.int32, (128, 128), 0), lax.broadcasted_iota(jnp.int32, (128, 128), 1)
    for rg in range(8):
        hit = (lax.rem(r, 16) == lax.rem(c, 16)) & (r // 16 == rg)
        picker[:, pl.ds(rg * 128, 128)] = jnp.where(hit, 1.0, 0.0).astype(jnp.bfloat16)

    def write(k2):
        at = pl.ds(k2 * 4, 4)
        return pltpu.make_async_copy(out.at[:, :, at], out_hbm.at[:, :, at], stores.at[k2])

    def gather(k2, carry):
        t = k2
        rows = 128 * BLOCKS
        base = t * rows
        parts = []
        for rg in range(8):
            at = pl.ds(pl.multiple_of(rg * 4096 + base, rows), rows)
            parts.append(ga[at, :] + gb[at, :] + gc[at, :])
        hi, lo = split(jnp.concatenate(parts, axis=1))
        dims = (((1,), (1,)), ((), ()))
        block = lax.dot_general(picker[...], hi, dims, preferred_element_type=jnp.float32)
        block = block + lax.dot_general(picker[...], lo, dims, preferred_element_type=jnp.float32)
        block = block.reshape(8, 2, 8, rows)
        at = pl.ds(pl.multiple_of(lax.rem(t, 4 // BLOCKS) * rows, rows), rows)
        for v in range(2):
            for h in range(2):
                out[h, v, pl.ds(k2 * 4, 4), :, at] = block[h * 4 : h * 4 + 4, v]
        write(k2).start()
        return carry

    lax.fori_loop(0, 8, gather, 0)

    quarter = lax.broadcasted_iota(jnp.int32, (32, 128), 1) // 32
    for h in range(2):
        for v in range(2):
            for side, (col, at) in enumerate(((0, 0), (384, 96))):
                for kk in range(2):
                    total = None
                    for kq in range(4):
                        x = out[h, v, pl.ds((kk * 4 + kq) * 4, 4), :, pl.ds(col, 128)].reshape(32, 128)
                        shift = (kq * 32 - at) % 128
                        x = pltpu.roll(x, shift, 1) if shift else x
                        total = x if total is None else jnp.where(quarter == kq, x, total)
                    out[h, v, pl.ds(32, 4), :, pl.ds((side * 2 + kk) * 128, 128)] = total.reshape(4, 8, 128)
    edge = pl.ds(32, 4)
    write_edge = pltpu.make_async_copy(out.at[:, :, edge], out_hbm.at[:, :, edge], sems.at[3])
    write_edge.start()
    for k2 in range(8):
        write(k2).wait()
    write_edge.wait()


def grid_tile(vals, cells, mixer):
    hbm = pl.BlockSpec(memory_space=pl.ANY)
    return pl.pallas_call(
        grid_kernel,
        out_shape=jax.ShapeDtypeStruct((2, 2, 36, 8, 512), jnp.float32),
        in_specs=[hbm] * 3,
        out_specs=hbm,
        scratch_shapes=[
            pltpu.VMEM((128, 16, 128), jnp.float32),
            pltpu.VMEM((128, 128), jnp.float32),
            pltpu.VMEM((2048, 128), jnp.float32),
            pltpu.VMEM((2, 2, 36, 8, 512), jnp.float32),
            pltpu.VMEM((128, 1024), jnp.bfloat16),
            pltpu.VMEM((128, 1, 128), jnp.int32),
            pltpu.SemaphoreType.DMA((4,)),
            pltpu.SemaphoreType.DMA((8,)),
        ]
        + [pltpu.VMEM((32768, 128), jnp.float32)] * NACC
        + [pltpu.SMEM((128,), jnp.int32)] * 128,
        compiler_params=pltpu.CompilerParams(vmem_limit_bytes=VMEM),
        cost_estimate=pl.CostEstimate(flops=10**9, bytes_accessed=4 * 2**20, transcendentals=0),
        name="scatter",
    )(vals, cells, mixer)


def filter_kernel(n_lat, n_lon, x_hbm, t_hbm, a_hbm, out, x, e, y, t, a, passing, send, recv, local):
    lat = lax.axis_index("lat")
    lon = lax.axis_index("lon")
    west = lax.rem(lon + n_lon - 1, n_lon)
    east = lax.rem(lon + 1, n_lon)
    north = lat - 1
    south = lat + 1
    has_north = lat > 0
    has_south = lat < n_lat - 1
    last, mid = n_lat - 1, n_lat // 2 - 1
    at_end = (lat == 0) | (lat == last)
    at_mid = (lat == mid) | (lat == mid + 1)
    rows = pl.ds(0, 256)
    edge = pl.ds(256, 32)
    own = pl.ds(0, 2)
    upper, lower = pl.ds(0, 248), pl.ds(8, 248)

    barrier = pltpu.get_barrier_semaphore()

    def greet(where):
        pl.semaphore_signal(barrier, inc=1, device_id=where, device_id_type=MESH)

    @pl.when(has_north)
    def _():
        greet((north, lon))

    @pl.when(has_south)
    def _():
        greet((south, lon))

    greet((lat, west))
    greet((lat, east))

    @pl.when(at_end)
    def _():
        greet((mid, lon))
        greet((mid + 1, lon))

    @pl.when(at_mid)
    def _():
        greet((0, lon))
        greet((last, lon))

    loads = [
        pltpu.make_async_copy(x_hbm.at[:, :, rows], x.at[own], local.at[0]),
        pltpu.make_async_copy(t_hbm, t, local.at[1]),
        pltpu.make_async_copy(a_hbm, a, local.at[2]),
    ]
    for copy in loads:
        copy.start()
    pl.semaphore_wait(barrier, jnp.where(at_end, 5, jnp.where(at_mid, 6, 4)))

    def remote(src, dst, slot, where):
        return pltpu.make_async_remote_copy(
            src_ref=src, dst_ref=dst, send_sem=send.at[slot], recv_sem=recv.at[slot],
            device_id=where, device_id_type=MESH,
        )

    sides = [
        remote(x_hbm.at[:, :, edge, pl.ds(0, 256)], e.at[1, own], 0, (lat, west)),
        remote(x_hbm.at[:, :, edge, pl.ds(256, 256)], e.at[0, own], 1, (lat, east)),
    ]
    up = [
        remote(x_hbm.at[0, 0, upper], x.at[3, 0, upper], 2, (north, lon)),
        remote(x_hbm.at[0, 1, pl.ds(0, 128)], x.at[3, 1, pl.ds(0, 128)], 3, (north, lon)),
        remote(x_hbm.at[0, 1, pl.ds(128, 120)], x.at[3, 1, pl.ds(128, 120)], 8, (north, lon)),
        remote(e.at[:, 0], e.at[:, 3], 4, (north, lon)),
    ]
    down = [
        remote(x_hbm.at[1, 0, lower], x.at[2, 0, lower], 5, (south, lon)),
        remote(x_hbm.at[1, 1, pl.ds(128, 128)], x.at[2, 1, pl.ds(128, 128)], 6, (south, lon)),
        remote(x_hbm.at[1, 1, pl.ds(8, 120)], x.at[2, 1, pl.ds(8, 120)], 9, (south, lon)),
        remote(e.at[:, 1], e.at[:, 2], 7, (south, lon)),
    ]

    first, second = passing.at[0], passing.at[1, pl.ds(0, 120)]
    hop_up = [
        remote(x_hbm.at[0, 1, pl.ds(0, 128)], first, 10, (0, lon)),
        remote(x_hbm.at[0, 1, pl.ds(128, 120)], second, 11, (0, lon)),
    ]
    hop_down = [
        remote(x_hbm.at[1, 1, pl.ds(128, 128)], first, 10, (last, lon)),
        remote(x_hbm.at[1, 1, pl.ds(8, 120)], second, 11, (last, lon)),
    ]
    pass_up = [
        remote(first, x.at[3, 1, pl.ds(0, 128)], 3, (mid, lon)),
        remote(second, x.at[3, 1, pl.ds(128, 120)], 8, (mid, lon)),
    ]
    pass_down = [
        remote(first, x.at[2, 1, pl.ds(128, 128)], 6, (mid + 1, lon)),
        remote(second, x.at[2, 1, pl.ds(8, 120)], 9, (mid + 1, lon)),
    ]

    def ends_do(act, which):
        for cond, copies, hops, turn in ((has_north, up, hop_up, mid + 1), (has_south, down, hop_down, mid)):
            for i in which:
                if i in (1, 2):
                    @pl.when(cond & (lat != turn))
                    def _():
                        act(copies[i])

                    @pl.when(lat == turn)
                    def _():
                        act(hops[i - 1])
                else:
                    @pl.when(cond)
                    def _():
                        act(copies[i])

    def relay(i):
        @pl.when(lat == 0)
        def _():
            hop_up[i].wait_recv()
            pass_up[i].start()

        @pl.when(lat == last)
        def _():
            hop_down[i].wait_recv()
            pass_down[i].start()

    def arrived(which):
        @pl.when(has_north)
        def _():
            for i in which:
                down[i].wait_recv()

        @pl.when(has_south)
        def _():
            for i in which:
                up[i].wait_recv()

    for copy in sides:
        copy.start()
    ends_do(lambda copy: copy.start(), (0, 1))

    x[2, :, pl.ds(0, 8)] = jnp.zeros((2, 8, 512), jnp.float32)
    x[3, :, pl.ds(248, 8)] = jnp.zeros((2, 8, 512), jnp.float32)
    for s, there in ((2, has_north), (3, has_south)):
        @pl.when(jnp.logical_not(there))
        def _():
            x[s] = jnp.zeros((2, 256, 512), jnp.float32)
            e[:, s] = jnp.zeros((2, 2, 32, 256), jnp.float32)

    def centre(s, v):
        hi, lo = split(x[pl.ds(s, 2), v].reshape(512, 512))
        for n in range(2):
            deep, wide = slice(n * 128, n * 128 + 384), pl.ds(n * 256, 256)
            band = t[0, v, pl.ds(n * 128, 384), wide], t[1, v, pl.ds(n * 128, 384), wide]
            total = dot3((hi[:, deep], lo[:, deep]), band)
            for u in range(2):
                for cb in range(2):
                    y[s + u, v, n * 2 + cb] = total[u * 256 : u * 256 + 256, cb * 128 : cb * 128 + 128]

    def rims(s, v):
        for side in range(2):
            lines = [e[side, s + u, v, :, pl.ds(kk * 128, 128)] for u in range(2) for kk in range(2)]
            rim = dot3(split(jnp.concatenate(lines, axis=0)), (t[0, v, pl.ds(512 + side * 128, 128)], t[1, v, pl.ds(512 + side * 128, 128)]))
            for u in range(2):
                for k2 in range(8):
                    line = (u * 2 + k2 // 4) * 32
                    col = (k2 % 4) * 128
                    y[s + u, v, side * 3, pl.ds(k2 * 32, 32)] += rim[line : line + 32, col : col + 128]

    def along_lat(s, v):
        def levels(i, carry):
            for u in range(4):
                l = i * 4 + u
                line = jnp.concatenate(
                    [
                        jnp.concatenate([y[s + k, v, cb, pl.ds(l, 32, stride=8), :] for cb in range(4)], axis=1)
                        for k in range(2)
                    ],
                    axis=0,
                )
                hi, lo = split(line)
                part = dot(a[s // 2, v], jnp.concatenate([hi, hi, lo], axis=0))
                out[v, l] = part if s == 0 else out[v, l] + part
            return carry

        lax.fori_loop(0, LEV // 4, levels, 0)

    for copy in loads:
        copy.wait()
    centre(0, 0)
    for copy in sides:
        copy.wait_recv()
    ends_do(lambda copy: copy.start(), (3, 2))
    relay(0)
    centre(0, 1)
    relay(1)
    for v in range(2):
        rims(0, v)
        along_lat(0, v)

    for v in range(2):
        arrived((0, 3) if v == 0 else (1, 2))
        centre(2, v)
        rims(2, v)
        along_lat(2, v)

    for copy in sides:
        copy.wait_send()
    ends_do(lambda copy: copy.wait_send(), (0, 1, 2, 3))

    @pl.when(lat == 0)
    def _():
        for copy in pass_up:
            copy.wait_send()

    @pl.when(lat == last)
    def _():
        for copy in pass_down:
            copy.wait_send()


def filter_tile(n_lat, n_lon, x, weights):
    return pl.pallas_call(
        functools.partial(filter_kernel, n_lat, n_lon),
        out_shape=jax.ShapeDtypeStruct((2, 8, 64, 512), jnp.float32),
        in_specs=[pl.BlockSpec(memory_space=pl.ANY)] * 3,
        out_specs=pl.BlockSpec(memory_space=pltpu.VMEM),
        scratch_shapes=[
            pltpu.VMEM((4, 2, 256, 512), jnp.float32),
            pltpu.VMEM((2, 4, 2, 32, 256), jnp.float32),
            pltpu.VMEM((4, 2, 4, 256, 128), jnp.float32),
            pltpu.VMEM((2, 2, 768, 512), jnp.bfloat16),
            pltpu.VMEM((2, 2, 64, 192), jnp.bfloat16),
            pltpu.VMEM((2, 128, 512), jnp.float32),
            pltpu.SemaphoreType.DMA((12,)),
            pltpu.SemaphoreType.DMA((12,)),
            pltpu.SemaphoreType.DMA((3,)),
        ],
        compiler_params=pltpu.CompilerParams(
            vmem_limit_bytes=101 * 2**19, collective_id=0, has_side_effects=True
        ),
        cost_estimate=pl.CostEstimate(flops=6 * 10**9, bytes_accessed=8 * 2**20, transcendentals=0),
        name="filters",
    )(x, *weights)


def route_kernel(n_lat, n_lon, obs_hbm, cells_hbm, counts_hbm, lengths_hbm, weights_hbm, mix_hbm,
                 vals, cells, mixer_hbm, t_hbm, a_hbm,
                 box, cell_box, counts, lengths, weights, mix, tiles, mixer, t_out, a_out, local, send, recv):
    lat = lax.axis_index("lat")
    lon = lax.axis_index("lon")
    me = lat * n_lon + lon
    count = n_lat * n_lon

    loads = [
        pltpu.make_async_copy(src, dst, local.at[i])
        for i, (src, dst) in enumerate(
            ((obs_hbm, box), (cells_hbm, cell_box), (counts_hbm, counts), (lengths_hbm, lengths),
             (weights_hbm, weights), (mix_hbm, mix))
        )
    ]
    for copy in loads:
        copy.start()

    barrier = pltpu.get_barrier_semaphore()

    columns = [lon] + [lax.rem(lon + k, n_lon) for k in range(1, n_lon)]

    def each_peer(act):
        for k in range(1, n_lon):
            act(lat, columns[k])

        def line(i, carry):
            for column in columns:
                act(lax.rem(lat + i, n_lat), column)
            return carry

        lax.fori_loop(1, n_lat, line, 0)

    def greet(to_lat, to_lon):
        pl.semaphore_signal(barrier, inc=1, device_id=(to_lat, to_lon), device_id_type=MESH)

    each_peer(greet)
    for copy in loads:
        copy.wait()

    slot = lax.broadcasted_iota(jnp.int32, (16, 128), 1)

    def mask(i, carry):
        for u in range(8):
            d = i * 8 + u
            box[d] = jnp.where(slot < counts[0, d], box[d], 0.0)
        return carry

    lax.fori_loop(0, count // 8, mask, 0)
    pl.semaphore_wait(barrier, count - 1)

    def give(to_lat, to_lon):
        d = to_lat * n_lon + to_lon
        for i, (src, dst) in enumerate(((box, vals), (cell_box, cells))):
            pltpu.make_async_remote_copy(
                src_ref=src.at[d], dst_ref=dst.at[me], send_sem=send.at[i], recv_sem=recv.at[i],
                device_id=(to_lat, to_lon), device_id_type=MESH,
            ).start()

    each_peer(give)
    pltpu.make_async_copy(cell_box.at[me], cells.at[me], recv.at[1]).start()
    pltpu.make_async_copy(box.at[me], vals.at[me], recv.at[0]).start()

    def iota(shape, dim):
        return lax.broadcasted_iota(jnp.int32, shape, dim)

    def profile(v, offset):
        t = offset.astype(jnp.float32)
        total = 0.0
        for s in range(3):
            scale = t / lengths[v, s]
            total = total + weights[v, s] * jnp.exp(-0.5 * (scale * scale))
        return jnp.where(jnp.abs(offset) <= HALF, total, 0.0)

    flat = (128, 128)
    for v in range(2):
        taps = profile(v, iota((8, 128), 1) - HALF)
        norm = lax.rsqrt(jnp.sum(taps * taps, axis=1, keepdims=True))[0:1, 0:1]
        for i in range(3):
            hi, lo = split(profile(v, iota(flat, 0) - iota(flat, 1) + (i - 1) * 128) * norm)
            tiles[0, i] = hi
            tiles[1, i] = lo
        blank = jnp.zeros(flat, jnp.bfloat16)
        for p in range(2):
            for i in range(4):
                for j in range(4):
                    piece = tiles[p, i - j + 1] if abs(i - j) <= 1 else blank
                    t_out[p, v, pl.ds(i * 128, 128), pl.ds(j * 128, 128)] = piece
            t_out[p, v, pl.ds(512, 256)] = jnp.zeros((256, 512), jnp.bfloat16)
            for kq in range(4):
                at = pl.ds(kq * 128, 128)
                t_out[p, v, pl.ds(512 + kq * 32, 32), at] = tiles[p, 0, pl.ds(96, 32)]
                t_out[p, v, pl.ds(640 + kq * 32, 32), at] = tiles[p, 2, pl.ds(0, 32)]
        k = iota((64, 192), 1)
        place = lax.rem(k, 32)
        inner = lax.rem(place, 4) * 8 + place // 4
        second = lax.rem(k, 64) // 32
        for part in range(2):
            base = second * 32 if part == 0 else second * 96 - 32
            hi, lo = split(profile(v, base + inner - iota((64, 192), 0)) * norm)
            a_out[part, v] = jnp.where(k // 64 == 1, lo.astype(jnp.float32), hi.astype(jnp.float32)).astype(jnp.bfloat16)

    row, col = iota((16, 128), 0), iota((16, 128), 1)
    small = jnp.zeros((16, 128), jnp.float32)
    for v in range(2):
        for l in range(LEV):
            for m in range(LEV):
                here = (row == v * LEV + m) & (lax.rem(col, 16) == v * LEV + l)
                small = jnp.where(here, mix[v, l, m], small)
    for i in range(8):
        mixer[pl.ds(i * 16, 16)] = jnp.where(col // 16 == i, small, 0.0)

    writes = [
        pltpu.make_async_copy(src, dst, local.at[i])
        for i, (src, dst) in enumerate(((mixer, mixer_hbm), (t_out, t_hbm), (a_out, a_hbm)))
    ]
    for copy in writes:
        copy.start()
    for copy in writes:
        copy.wait()

    rest = pl.ds(0, count - 1)
    for i, (src, dst) in enumerate(((box, vals), (cell_box, cells))):
        pltpu.make_async_copy(dst, dst, recv.at[i]).wait()
        pltpu.make_async_copy(src.at[rest], dst.at[rest], send.at[i]).wait()


def route(n_lat, n_lon, obs, cells, counts, lengths, weights, mix):
    n = n_lat * n_lon
    hbm = pl.BlockSpec(memory_space=pl.ANY)
    bf16 = jnp.bfloat16
    return pl.pallas_call(
        functools.partial(route_kernel, n_lat, n_lon),
        out_shape=(
            jax.ShapeDtypeStruct((n, 16, 128), jnp.float32),
            jax.ShapeDtypeStruct((n, 1, 128), jnp.int32),
            jax.ShapeDtypeStruct((128, 128), jnp.float32),
            jax.ShapeDtypeStruct((2, 2, 768, 512), bf16),
            jax.ShapeDtypeStruct((2, 2, 64, 192), bf16),
        ),
        in_specs=[hbm] * 6,
        out_specs=[hbm] * 5,
        scratch_shapes=[
            pltpu.VMEM((n, 16, 128), jnp.float32),
            pltpu.VMEM((n, 1, 128), jnp.int32),
            pltpu.SMEM((1, n), jnp.int32),
            pltpu.SMEM((2, 3), jnp.float32),
            pltpu.SMEM((2, 3), jnp.float32),
            pltpu.SMEM((2, LEV, LEV), jnp.float32),
            pltpu.VMEM((2, 3, 128, 128), bf16),
            pltpu.VMEM((128, 128), jnp.float32),
            pltpu.VMEM((2, 2, 768, 512), bf16),
            pltpu.VMEM((2, 2, 64, 192), bf16),
            pltpu.SemaphoreType.DMA((6,)),
            pltpu.SemaphoreType.DMA((2,)),
            pltpu.SemaphoreType.DMA((2,)),
        ],
        compiler_params=pltpu.CompilerParams(vmem_limit_bytes=VMEM, collective_id=1, has_side_effects=True),
        cost_estimate=pl.CostEstimate(flops=10**7, bytes_accessed=4 * 2**20, transcendentals=0),
        name="route",
    )(obs, cells, counts, lengths, weights, mix)


def local(obs_values, obs_cells, obs_counts, filter_lengths, filter_weights, vertical_mix):
    n_lat, n_lon = lax.axis_size("lat"), lax.axis_size("lon")
    n = n_lat * n_lon
    vals, cells, mixer, *weights = route(
        n_lat, n_lon, obs_values.reshape(n, 16, 128), obs_cells.reshape(n, 1, 128), obs_counts,
        filter_lengths, filter_weights, vertical_mix,
    )
    x = grid_tile(vals, cells, mixer)
    return filter_tile(n_lat, n_lon, x.reshape(2, 2, 288, 512), weights)


def solution(mesh):
    in_specs = (
        P(("lat", "lon"), None, None, None, None),
        P(("lat", "lon"), None, None),
        P(("lat", "lon"), None),
        P(),
        P(),
        P(),
    )
    return jax.shard_map(
        local, mesh=mesh, in_specs=in_specs, out_specs=P(None, None, "lat", "lon"), check_vma=False
    )
```

```python
import functools

import jax
import jax.numpy as jnp
from jax import lax
from jax.experimental import pallas as pl
from jax.experimental.pallas import tpu as pltpu
from jax.sharding import PartitionSpec as P

HALF = 31
LEV = 8
NACC = 3
UNROLL = 4
AHEAD = 1
BLOCKS = 4
VMEM = 62 * 2**20
MESH = pl.DeviceIdType.MESH


def split(x):
    hi = x.astype(jnp.bfloat16)
    return hi, (x - hi.astype(jnp.float32)).astype(jnp.bfloat16)


def dot(a, b):
    return jnp.dot(a, b, preferred_element_type=jnp.float32)


def dot3(a, b):
    return dot(a[0], b[0]) + dot(a[1], b[0]) + dot(a[0], b[1])


def grid_kernel(vals_hbm, cells_hbm, mixer_hbm, out_hbm, vals, mixer, table, out, picker, sized, sems, stores, ga, gb, gc, *cells):
    grids = (ga, gb, gc)
    loads = [
        pltpu.make_async_copy(vals_hbm, vals, sems.at[0]),
        pltpu.make_async_copy(mixer_hbm, mixer, sems.at[2]),
    ]
    for copy in loads:
        copy.start()
    for s in range(128):
        pltpu.make_async_copy(cells_hbm.at[s, 0], cells[s], sems.at[1]).start()

    def clear(i, carry):
        for grid in (gb, gc):
            grid[pl.ds(pl.multiple_of(i * 512, 512), 512), :] = jnp.zeros((512, 128), jnp.float32)
        return carry

    lax.fori_loop(0, 64, clear, 0)
    for copy in loads:
        copy.wait()
    mix = split(mixer[...])

    def fill(i, carry):
        ga[pl.ds(pl.multiple_of(i * 4096, 4096), 4096), :] = jnp.zeros((4096, 128), jnp.float32)
        for u in range(2):
            g = i * 2 + u
            rows = vals[pl.ds(pl.multiple_of(g * 8, 8), 8)].reshape(128, 128).T
            table[pl.ds(pl.multiple_of(g * 128, 128), 128), :] = dot3(split(rows), mix)
        return carry

    lax.fori_loop(0, 8, fill, 0)
    lane = lax.broadcasted_iota(jnp.int32, (1, 128), 1) // 16
    masks = [lane == i for i in range(8)]
    pltpu.make_async_copy(cells_hbm, sized, sems.at[1]).wait()

    def batch(turn, n, j):
        grid = grids[turn % NACC]
        row = table[pl.ds(n * 128 + j, 1), :]
        places = [cells[n * 8 + i][j] for i in range(8)]
        return grid, places, [grid[pl.ds(c, 1), :] + row for c in places]

    def scatter(t, carry):
        order = [(n, t * UNROLL + u) for u in range(UNROLL) for n in range(16)]
        ahead = [batch(i, *order[i]) for i in range(AHEAD)]
        for i in range(len(order)):
            grid, places, totals = ahead.pop(0)
            if i + AHEAD < len(order):
                ahead.append(batch(i + AHEAD, *order[i + AHEAD]))
            for c, total, live in zip(places, totals, masks):
                pltpu.store(grid.at[pl.ds(c, 1), :], total, mask=live)
        return carry

    lax.fori_loop(0, 128 // UNROLL, scatter, 0)

    r, c = lax.broadcasted_iota(jnp.int32, (128, 128), 0), lax.broadcasted_iota(jnp.int32, (128, 128), 1)
    for q in range(4):
        hit = (lax.rem(r, 16) == lax.rem(c, 16)) & (r // 16 == q + 4 * (c // 64))
        picker[:, pl.ds(q * 128, 128)] = jnp.where(hit, 1.0, 0.0).astype(jnp.bfloat16)
    low = lax.broadcasted_iota(jnp.int32, (512, 128), 1) < 64

    def write(k2):
        at = pl.ds(k2 * 4, 4)
        return pltpu.make_async_copy(out.at[:, :, at], out_hbm.at[:, :, at], stores.at[k2])

    def gather(k2, carry):
        t = k2
        rows = 128 * BLOCKS
        base = t * rows
        def total(rg):
            at = pl.ds(pl.multiple_of(rg * 4096 + base, rows), rows)
            return ga[at, :] + gb[at, :] + gc[at, :]

        parts = []
        for q in range(4):
            one, other = total(q), total(q + 4)
            parts.append(jnp.where(low, one, other) + pltpu.roll(jnp.where(low, other, one), 64, 1))
        hi, lo = split(jnp.concatenate(parts, axis=1))
        dims = (((1,), (1,)), ((), ()))
        block = lax.dot_general(picker[...], hi, dims, preferred_element_type=jnp.float32)
        block = block + lax.dot_general(picker[...], lo, dims, preferred_element_type=jnp.float32)
        block = block.reshape(8, 2, 8, rows)
        at = pl.ds(pl.multiple_of(lax.rem(t, 4 // BLOCKS) * rows, rows), rows)
        for v in range(2):
            for h in range(2):
                out[h, v, pl.ds(k2 * 4, 4), :, at] = block[h * 4 : h * 4 + 4, v]
        write(k2).start()
        return carry

    lax.fori_loop(0, 8, gather, 0)

    quarter = lax.broadcasted_iota(jnp.int32, (32, 128), 1) // 32
    for h in range(2):
        for v in range(2):
            for side, (col, at) in enumerate(((0, 0), (384, 96))):
                for kk in range(2):
                    total = None
                    for kq in range(4):
                        x = out[h, v, pl.ds((kk * 4 + kq) * 4, 4), :, pl.ds(col, 128)].reshape(32, 128)
                        shift = (kq * 32 - at) % 128
                        x = pltpu.roll(x, shift, 1) if shift else x
                        total = x if total is None else jnp.where(quarter == kq, x, total)
                    out[h, v, pl.ds(32, 4), :, pl.ds((side * 2 + kk) * 128, 128)] = total.reshape(4, 8, 128)
    edge = pl.ds(32, 4)
    write_edge = pltpu.make_async_copy(out.at[:, :, edge], out_hbm.at[:, :, edge], sems.at[3])
    write_edge.start()
    for k2 in range(8):
        write(k2).wait()
    write_edge.wait()


def grid_tile(vals, cells, mixer):
    hbm = pl.BlockSpec(memory_space=pl.ANY)
    return pl.pallas_call(
        grid_kernel,
        out_shape=jax.ShapeDtypeStruct((2, 2, 36, 8, 512), jnp.float32),
        in_specs=[hbm] * 3,
        out_specs=hbm,
        scratch_shapes=[
            pltpu.VMEM((128, 16, 128), jnp.float32),
            pltpu.VMEM((128, 128), jnp.float32),
            pltpu.VMEM((2048, 128), jnp.float32),
            pltpu.VMEM((2, 2, 36, 8, 512), jnp.float32),
            pltpu.VMEM((128, 512), jnp.bfloat16),
            pltpu.VMEM((128, 1, 128), jnp.int32),
            pltpu.SemaphoreType.DMA((4,)),
            pltpu.SemaphoreType.DMA((8,)),
        ]
        + [pltpu.VMEM((32768, 128), jnp.float32)] * NACC
        + [pltpu.SMEM((128,), jnp.int32)] * 128,
        compiler_params=pltpu.CompilerParams(vmem_limit_bytes=VMEM),
        cost_estimate=pl.CostEstimate(flops=10**9, bytes_accessed=4 * 2**20, transcendentals=0),
        name="scatter",
    )(vals, cells, mixer)


def filter_kernel(n_lat, n_lon, x_hbm, t_hbm, a_hbm, out, x, e, y, t, a, passing, send, recv, local):
    lat = lax.axis_index("lat")
    lon = lax.axis_index("lon")
    west = lax.rem(lon + n_lon - 1, n_lon)
    east = lax.rem(lon + 1, n_lon)
    north = lat - 1
    south = lat + 1
    has_north = lat > 0
    has_south = lat < n_lat - 1
    last, mid = n_lat - 1, n_lat // 2 - 1
    at_end = (lat == 0) | (lat == last)
    at_mid = (lat == mid) | (lat == mid + 1)
    rows = pl.ds(0, 256)
    edge = pl.ds(256, 32)
    own = pl.ds(0, 2)
    upper, lower = pl.ds(0, 248), pl.ds(8, 248)

    barrier = pltpu.get_barrier_semaphore()

    def greet(where):
        pl.semaphore_signal(barrier, inc=1, device_id=where, device_id_type=MESH)

    @pl.when(has_north)
    def _():
        greet((north, lon))

    @pl.when(has_south)
    def _():
        greet((south, lon))

    greet((lat, west))
    greet((lat, east))

    @pl.when(at_end)
    def _():
        greet((mid, lon))
        greet((mid + 1, lon))

    @pl.when(at_mid)
    def _():
        greet((0, lon))
        greet((last, lon))

    loads = [
        pltpu.make_async_copy(x_hbm.at[:, :, rows], x.at[own], local.at[0]),
        pltpu.make_async_copy(t_hbm, t, local.at[1]),
        pltpu.make_async_copy(a_hbm, a, local.at[2]),
    ]
    for copy in loads:
        copy.start()
    pl.semaphore_wait(barrier, jnp.where(at_end, 5, jnp.where(at_mid, 6, 4)))

    def remote(src, dst, slot, where):
        return pltpu.make_async_remote_copy(
            src_ref=src, dst_ref=dst, send_sem=send.at[slot], recv_sem=recv.at[slot],
            device_id=where, device_id_type=MESH,
        )

    sides = [
        remote(x_hbm.at[:, :, edge, pl.ds(0, 256)], e.at[1, own], 0, (lat, west)),
        remote(x_hbm.at[:, :, edge, pl.ds(256, 256)], e.at[0, own], 1, (lat, east)),
    ]
    up = [
        remote(x_hbm.at[0, 0, upper], x.at[3, 0, upper], 2, (north, lon)),
        remote(x_hbm.at[0, 1, pl.ds(0, 128)], x.at[3, 1, pl.ds(0, 128)], 3, (north, lon)),
        remote(x_hbm.at[0, 1, pl.ds(128, 120)], x.at[3, 1, pl.ds(128, 120)], 8, (north, lon)),
        remote(e.at[:, 0], e.at[:, 3], 4, (north, lon)),
    ]
    down = [
        remote(x_hbm.at[1, 0, lower], x.at[2, 0, lower], 5, (south, lon)),
        remote(x_hbm.at[1, 1, pl.ds(128, 128)], x.at[2, 1, pl.ds(128, 128)], 6, (south, lon)),
        remote(x_hbm.at[1, 1, pl.ds(8, 120)], x.at[2, 1, pl.ds(8, 120)], 9, (south, lon)),
        remote(e.at[:, 1], e.at[:, 2], 7, (south, lon)),
    ]

    first, second = passing.at[0], passing.at[1, pl.ds(0, 120)]
    hop_up = [
        remote(x_hbm.at[0, 1, pl.ds(0, 128)], first, 10, (0, lon)),
        remote(x_hbm.at[0, 1, pl.ds(128, 120)], second, 11, (0, lon)),
    ]
    hop_down = [
        remote(x_hbm.at[1, 1, pl.ds(128, 128)], first, 10, (last, lon)),
        remote(x_hbm.at[1, 1, pl.ds(8, 120)], second, 11, (last, lon)),
    ]
    pass_up = [
        remote(first, x.at[3, 1, pl.ds(0, 128)], 3, (mid, lon)),
        remote(second, x.at[3, 1, pl.ds(128, 120)], 8, (mid, lon)),
    ]
    pass_down = [
        remote(first, x.at[2, 1, pl.ds(128, 128)], 6, (mid + 1, lon)),
        remote(second, x.at[2, 1, pl.ds(8, 120)], 9, (mid + 1, lon)),
    ]

    def ends_do(act, which):
        for cond, copies, hops, turn in ((has_north, up, hop_up, mid + 1), (has_south, down, hop_down, mid)):
            for i in which:
                if i in (1, 2):
                    @pl.when(cond & (lat != turn))
                    def _():
                        act(copies[i])

                    @pl.when(lat == turn)
                    def _():
                        act(hops[i - 1])
                else:
                    @pl.when(cond)
                    def _():
                        act(copies[i])

    def relay(i):
        @pl.when(lat == 0)
        def _():
            hop_up[i].wait_recv()
            pass_up[i].start()

        @pl.when(lat == last)
        def _():
            hop_down[i].wait_recv()
            pass_down[i].start()

    def arrived(which):
        @pl.when(has_north)
        def _():
            for i in which:
                down[i].wait_recv()

        @pl.when(has_south)
        def _():
            for i in which:
                up[i].wait_recv()

    for copy in sides:
        copy.start()
    ends_do(lambda copy: copy.start(), (0, 1))

    x[2, :, pl.ds(0, 8)] = jnp.zeros((2, 8, 512), jnp.float32)
    x[3, :, pl.ds(248, 8)] = jnp.zeros((2, 8, 512), jnp.float32)
    for s, there in ((2, has_north), (3, has_south)):
        @pl.when(jnp.logical_not(there))
        def _():
            x[s] = jnp.zeros((2, 256, 512), jnp.float32)
            e[:, s] = jnp.zeros((2, 2, 32, 256), jnp.float32)

    def centre(s, v):
        hi, lo = split(x[pl.ds(s, 2), v].reshape(512, 512))
        for n in range(2):
            deep, wide = slice(n * 128, n * 128 + 384), pl.ds(n * 256, 256)
            band = t[0, v, pl.ds(n * 128, 384), wide], t[1, v, pl.ds(n * 128, 384), wide]
            total = dot3((hi[:, deep], lo[:, deep]), band)
            for u in range(2):
                for cb in range(2):
                    y[s + u, v, n * 2 + cb] = total[u * 256 : u * 256 + 256, cb * 128 : cb * 128 + 128]

    def rims(s, v):
        for side in range(2):
            lines = [e[side, s + u, v, :, pl.ds(kk * 128, 128)] for u in range(2) for kk in range(2)]
            rim = dot3(split(jnp.concatenate(lines, axis=0)), (t[0, v, pl.ds(512 + side * 128, 128)], t[1, v, pl.ds(512 + side * 128, 128)]))
            for u in range(2):
                for k2 in range(8):
                    line = (u * 2 + k2 // 4) * 32
                    col = (k2 % 4) * 128
                    y[s + u, v, side * 3, pl.ds(k2 * 32, 32)] += rim[line : line + 32, col : col + 128]

    def along_lat(s, v):
        def levels(i, carry):
            for u in range(4):
                l = i * 4 + u
                line = jnp.concatenate(
                    [
                        jnp.concatenate([y[s + k, v, cb, pl.ds(l, 32, stride=8), :] for cb in range(4)], axis=1)
                        for k in range(2)
                    ],
                    axis=0,
                )
                hi, lo = split(line)
                part = dot(a[s // 2, v], jnp.concatenate([hi, hi, lo], axis=0))
                out[v, l] = part if s == 0 else out[v, l] + part
            return carry

        lax.fori_loop(0, LEV // 4, levels, 0)

    for copy in loads:
        copy.wait()
    centre(0, 0)
    for copy in sides:
        copy.wait_recv()
    ends_do(lambda copy: copy.start(), (3, 2))
    relay(0)
    centre(0, 1)
    relay(1)
    for v in range(2):
        rims(0, v)
        along_lat(0, v)

    for v in range(2):
        arrived((0, 3) if v == 0 else (1, 2))
        centre(2, v)
        rims(2, v)
        along_lat(2, v)

    for copy in sides:
        copy.wait_send()
    ends_do(lambda copy: copy.wait_send(), (0, 1, 2, 3))

    @pl.when(lat == 0)
    def _():
        for copy in pass_up:
            copy.wait_send()

    @pl.when(lat == last)
    def _():
        for copy in pass_down:
            copy.wait_send()


def filter_tile(n_lat, n_lon, x, weights):
    return pl.pallas_call(
        functools.partial(filter_kernel, n_lat, n_lon),
        out_shape=jax.ShapeDtypeStruct((2, 8, 64, 512), jnp.float32),
        in_specs=[pl.BlockSpec(memory_space=pl.ANY)] * 3,
        out_specs=pl.BlockSpec(memory_space=pltpu.VMEM),
        scratch_shapes=[
            pltpu.VMEM((4, 2, 256, 512), jnp.float32),
            pltpu.VMEM((2, 4, 2, 32, 256), jnp.float32),
            pltpu.VMEM((4, 2, 4, 256, 128), jnp.float32),
            pltpu.VMEM((2, 2, 768, 512), jnp.bfloat16),
            pltpu.VMEM((2, 2, 64, 192), jnp.bfloat16),
            pltpu.VMEM((2, 128, 512), jnp.float32),
            pltpu.SemaphoreType.DMA((12,)),
            pltpu.SemaphoreType.DMA((12,)),
            pltpu.SemaphoreType.DMA((3,)),
        ],
        compiler_params=pltpu.CompilerParams(
            vmem_limit_bytes=101 * 2**19, collective_id=0, has_side_effects=True
        ),
        cost_estimate=pl.CostEstimate(flops=6 * 10**9, bytes_accessed=8 * 2**20, transcendentals=0),
        name="filters",
    )(x, *weights)


def route_kernel(n_lat, n_lon, obs_hbm, cells_hbm, counts_hbm, lengths_hbm, weights_hbm, mix_hbm,
                 vals, cells, mixer_hbm, t_hbm, a_hbm,
                 box, cell_box, counts, lengths, weights, mix, tiles, mixer, t_out, a_out, local, send, recv):
    lat = lax.axis_index("lat")
    lon = lax.axis_index("lon")
    me = lat * n_lon + lon
    count = n_lat * n_lon

    loads = [
        pltpu.make_async_copy(src, dst, local.at[i])
        for i, (src, dst) in enumerate(
            ((obs_hbm, box), (cells_hbm, cell_box), (counts_hbm, counts), (lengths_hbm, lengths),
             (weights_hbm, weights), (mix_hbm, mix))
        )
    ]
    for copy in loads:
        copy.start()

    barrier = pltpu.get_barrier_semaphore()

    columns = [lon] + [lax.rem(lon + k, n_lon) for k in range(1, n_lon)]

    def each_peer(act):
        for k in range(1, n_lon):
            act(lat, columns[k])

        def line(i, carry):
            away = jnp.where(i % 2 == 1, (i + 1) // 2, n_lat - i // 2)
            for column in columns:
                act(lax.rem(lat + away, n_lat), column)
            return carry

        lax.fori_loop(1, n_lat, line, 0)

    def greet(to_lat, to_lon):
        pl.semaphore_signal(barrier, inc=1, device_id=(to_lat, to_lon), device_id_type=MESH)

    each_peer(greet)
    for copy in loads:
        copy.wait()

    slot = lax.broadcasted_iota(jnp.int32, (16, 128), 1)

    def mask(i, carry):
        for u in range(8):
            d = i * 8 + u
            box[d] = jnp.where(slot < counts[0, d], box[d], 0.0)
        return carry

    lax.fori_loop(0, count // 8, mask, 0)
    pl.semaphore_wait(barrier, count - 1)

    def give(to_lat, to_lon):
        d = to_lat * n_lon + to_lon
        for i, (src, dst) in enumerate(((box, vals), (cell_box, cells))):
            pltpu.make_async_remote_copy(
                src_ref=src.at[d], dst_ref=dst.at[me], send_sem=send.at[i], recv_sem=recv.at[i],
                device_id=(to_lat, to_lon), device_id_type=MESH,
            ).start()

    each_peer(give)
    pltpu.make_async_copy(cell_box.at[me], cells.at[me], recv.at[1]).start()
    pltpu.make_async_copy(box.at[me], vals.at[me], recv.at[0]).start()

    def iota(shape, dim):
        return lax.broadcasted_iota(jnp.int32, shape, dim)

    def profile(v, offset):
        t = offset.astype(jnp.float32)
        total = 0.0
        for s in range(3):
            scale = t / lengths[v, s]
            total = total + weights[v, s] * jnp.exp(-0.5 * (scale * scale))
        return jnp.where(jnp.abs(offset) <= HALF, total, 0.0)

    flat = (128, 128)
    for v in range(2):
        taps = profile(v, iota((8, 128), 1) - HALF)
        norm = lax.rsqrt(jnp.sum(taps * taps, axis=1, keepdims=True))[0:1, 0:1]
        for i in range(3):
            hi, lo = split(profile(v, iota(flat, 0) - iota(flat, 1) + (i - 1) * 128) * norm)
            tiles[0, i] = hi
            tiles[1, i] = lo
        blank = jnp.zeros(flat, jnp.bfloat16)
        for p in range(2):
            for i in range(4):
                for j in range(4):
                    piece = tiles[p, i - j + 1] if abs(i - j) <= 1 else blank
                    t_out[p, v, pl.ds(i * 128, 128), pl.ds(j * 128, 128)] = piece
            t_out[p, v, pl.ds(512, 256)] = jnp.zeros((256, 512), jnp.bfloat16)
            for kq in range(4):
                at = pl.ds(kq * 128, 128)
                t_out[p, v, pl.ds(512 + kq * 32, 32), at] = tiles[p, 0, pl.ds(96, 32)]
                t_out[p, v, pl.ds(640 + kq * 32, 32), at] = tiles[p, 2, pl.ds(0, 32)]
        k = iota((64, 192), 1)
        place = lax.rem(k, 32)
        inner = lax.rem(place, 4) * 8 + place // 4
        second = lax.rem(k, 64) // 32
        for part in range(2):
            base = second * 32 if part == 0 else second * 96 - 32
            hi, lo = split(profile(v, base + inner - iota((64, 192), 0)) * norm)
            a_out[part, v] = jnp.where(k // 64 == 1, lo.astype(jnp.float32), hi.astype(jnp.float32)).astype(jnp.bfloat16)

    row, col = iota((16, 128), 0), iota((16, 128), 1)
    small = jnp.zeros((16, 128), jnp.float32)
    for v in range(2):
        for l in range(LEV):
            for m in range(LEV):
                here = (row == v * LEV + m) & (lax.rem(col, 16) == v * LEV + l)
                small = jnp.where(here, mix[v, l, m], small)
    for i in range(8):
        mixer[pl.ds(i * 16, 16)] = jnp.where(col // 16 == i, small, 0.0)

    writes = [
        pltpu.make_async_copy(src, dst, local.at[i])
        for i, (src, dst) in enumerate(((mixer, mixer_hbm), (t_out, t_hbm), (a_out, a_hbm)))
    ]
    for copy in writes:
        copy.start()
    for copy in writes:
        copy.wait()

    rest = pl.ds(0, count - 1)
    for i, (src, dst) in enumerate(((box, vals), (cell_box, cells))):
        pltpu.make_async_copy(dst, dst, recv.at[i]).wait()
        pltpu.make_async_copy(src.at[rest], dst.at[rest], send.at[i]).wait()


def route(n_lat, n_lon, obs, cells, counts, lengths, weights, mix):
    n = n_lat * n_lon
    hbm = pl.BlockSpec(memory_space=pl.ANY)
    bf16 = jnp.bfloat16
    return pl.pallas_call(
        functools.partial(route_kernel, n_lat, n_lon),
        out_shape=(
            jax.ShapeDtypeStruct((n, 16, 128), jnp.float32),
            jax.ShapeDtypeStruct((n, 1, 128), jnp.int32),
            jax.ShapeDtypeStruct((128, 128), jnp.float32),
            jax.ShapeDtypeStruct((2, 2, 768, 512), bf16),
            jax.ShapeDtypeStruct((2, 2, 64, 192), bf16),
        ),
        in_specs=[hbm] * 6,
        out_specs=[hbm] * 5,
        scratch_shapes=[
            pltpu.VMEM((n, 16, 128), jnp.float32),
            pltpu.VMEM((n, 1, 128), jnp.int32),
            pltpu.SMEM((1, n), jnp.int32),
            pltpu.SMEM((2, 3), jnp.float32),
            pltpu.SMEM((2, 3), jnp.float32),
            pltpu.SMEM((2, LEV, LEV), jnp.float32),
            pltpu.VMEM((2, 3, 128, 128), bf16),
            pltpu.VMEM((128, 128), jnp.float32),
            pltpu.VMEM((2, 2, 768, 512), bf16),
            pltpu.VMEM((2, 2, 64, 192), bf16),
            pltpu.SemaphoreType.DMA((6,)),
            pltpu.SemaphoreType.DMA((2,)),
            pltpu.SemaphoreType.DMA((2,)),
        ],
        compiler_params=pltpu.CompilerParams(vmem_limit_bytes=VMEM, collective_id=1, has_side_effects=True),
        cost_estimate=pl.CostEstimate(flops=10**7, bytes_accessed=4 * 2**20, transcendentals=0),
        name="route",
    )(obs, cells, counts, lengths, weights, mix)


def local(obs_values, obs_cells, obs_counts, filter_lengths, filter_weights, vertical_mix):
    n_lat, n_lon = lax.axis_size("lat"), lax.axis_size("lon")
    n = n_lat * n_lon
    vals, cells, mixer, *weights = route(
        n_lat, n_lon, obs_values.reshape(n, 16, 128), obs_cells.reshape(n, 1, 128), obs_counts,
        filter_lengths, filter_weights, vertical_mix,
    )
    x = grid_tile(vals, cells, mixer)
    return filter_tile(n_lat, n_lon, x.reshape(2, 2, 288, 512), weights)


def solution(mesh):
    in_specs = (
        P(("lat", "lon"), None, None, None, None),
        P(("lat", "lon"), None, None),
        P(("lat", "lon"), None),
        P(),
        P(),
        P(),
    )
    return jax.shard_map(
        local, mesh=mesh, in_specs=in_specs, out_specs=P(None, None, "lat", "lon"), check_vma=False
    )
```

```python
import functools

import jax
import jax.numpy as jnp
from jax import lax
from jax.experimental import pallas as pl
from jax.experimental.pallas import tpu as pltpu
from jax.sharding import PartitionSpec as P

HALF = 31
LEV = 8
NACC = 3
UNROLL = 4
AHEAD = 1
VMEM = 62 * 2**20
MESH = pl.DeviceIdType.MESH


def split(x):
    hi = x.astype(jnp.bfloat16)
    return hi, (x - hi.astype(jnp.float32)).astype(jnp.bfloat16)


def dot(a, b):
    return jnp.dot(a, b, preferred_element_type=jnp.float32)


def dot3(a, b):
    return dot(a[0], b[0]) + dot(a[1], b[0]) + dot(a[0], b[1])


def grid_kernel(vals_hbm, cells_hbm, mixer_hbm, out_hbm, vals, mixer, table, out, picker, sized, sems, stores, ga, gb, gc, *cells):
    grids = (ga, gb, gc)
    loads = [
        pltpu.make_async_copy(vals_hbm, vals, sems.at[0]),
        pltpu.make_async_copy(mixer_hbm, mixer, sems.at[2]),
    ]
    for copy in loads:
        copy.start()
    for s in range(128):
        pltpu.make_async_copy(cells_hbm.at[s, 0], cells[s], sems.at[1]).start()

    def clear(i, carry):
        for grid in (gb, gc):
            grid[pl.ds(pl.multiple_of(i * 512, 512), 512), :] = jnp.zeros((512, 128), jnp.float32)
        return carry

    lax.fori_loop(0, 64, clear, 0)
    for copy in loads:
        copy.wait()
    mix = split(mixer[...])

    def fill(i, carry):
        ga[pl.ds(pl.multiple_of(i * 4096, 4096), 4096), :] = jnp.zeros((4096, 128), jnp.float32)
        for u in range(2):
            g = i * 2 + u
            rows = vals[pl.ds(pl.multiple_of(g * 8, 8), 8)].reshape(128, 128).T
            table[pl.ds(pl.multiple_of(g * 128, 128), 128), :] = dot3(split(rows), mix)
        return carry

    lax.fori_loop(0, 8, fill, 0)
    lane = lax.broadcasted_iota(jnp.int32, (1, 128), 1) // 16
    masks = [lane == i for i in range(8)]
    pltpu.make_async_copy(cells_hbm, sized, sems.at[1]).wait()

    def batch(turn, n, j):
        grid = grids[turn % NACC]
        row = table[pl.ds(n * 128 + j, 1), :]
        places = [cells[n * 8 + i][j] for i in range(8)]
        return grid, places, [grid[pl.ds(c, 1), :] + row for c in places]

    def scatter(t, carry):
        order = [(n, t * UNROLL + u) for u in range(UNROLL) for n in range(16)]
        ahead = [batch(i, *order[i]) for i in range(AHEAD)]
        for i in range(len(order)):
            grid, places, totals = ahead.pop(0)
            if i + AHEAD < len(order):
                ahead.append(batch(i + AHEAD, *order[i + AHEAD]))
            for c, total, live in zip(places, totals, masks):
                pltpu.store(grid.at[pl.ds(c, 1), :], total, mask=live)
        return carry

    lax.fori_loop(0, 128 // UNROLL, scatter, 0)

    r, c = lax.broadcasted_iota(jnp.int32, (128, 128), 0), lax.broadcasted_iota(jnp.int32, (128, 128), 1)
    for q in range(4):
        hit = (lax.rem(r, 16) == lax.rem(c, 16)) & (r // 16 == q + 4 * (c // 64))
        picker[:, pl.ds(q * 128, 128)] = jnp.where(hit, 1.0, 0.0).astype(jnp.bfloat16)
    low = lax.broadcasted_iota(jnp.int32, (128, 128), 1) < 64

    def write(k2):
        at = pl.ds(k2 * 4, 4)
        return pltpu.make_async_copy(out.at[:, :, at], out_hbm.at[:, :, at], stores.at[k2])

    def gather(k2, carry):
        for piece in range(4):
            base = k2 * 512 + piece * 128

            def total(rg):
                at = pl.ds(pl.multiple_of(rg * 4096 + base, 128), 128)
                return ga[at, :] + gb[at, :] + gc[at, :]

            parts = []
            for q in range(4):
                one, other = total(q), total(q + 4)
                parts.append(jnp.where(low, one, other) + pltpu.roll(jnp.where(low, other, one), 64, 1))
            hi, lo = split(jnp.concatenate(parts, axis=1))
            dims = (((1,), (1,)), ((), ()))
            block = lax.dot_general(picker[...], hi, dims, preferred_element_type=jnp.float32)
            block = block + lax.dot_general(picker[...], lo, dims, preferred_element_type=jnp.float32)
            block = block.reshape(8, 2, 8, 128)
            for v in range(2):
                for h in range(2):
                    out[h, v, pl.ds(k2 * 4, 4), :, pl.ds(piece * 128, 128)] = block[h * 4 : h * 4 + 4, v]
        write(k2).start()
        return carry

    lax.fori_loop(0, 8, gather, 0)

    quarter = lax.broadcasted_iota(jnp.int32, (32, 128), 1) // 32
    for h in range(2):
        for v in range(2):
            for side, (col, at) in enumerate(((0, 0), (384, 96))):
                for kk in range(2):
                    total = None
                    for kq in range(4):
                        x = out[h, v, pl.ds((kk * 4 + kq) * 4, 4), :, pl.ds(col, 128)].reshape(32, 128)
                        shift = (kq * 32 - at) % 128
                        x = pltpu.roll(x, shift, 1) if shift else x
                        total = x if total is None else jnp.where(quarter == kq, x, total)
                    out[h, v, pl.ds(32, 4), :, pl.ds((side * 2 + kk) * 128, 128)] = total.reshape(4, 8, 128)
    edge = pl.ds(32, 4)
    write_edge = pltpu.make_async_copy(out.at[:, :, edge], out_hbm.at[:, :, edge], sems.at[3])
    write_edge.start()
    for k2 in range(8):
        write(k2).wait()
    write_edge.wait()


def grid_tile(vals, cells, mixer):
    hbm = pl.BlockSpec(memory_space=pl.ANY)
    return pl.pallas_call(
        grid_kernel,
        out_shape=jax.ShapeDtypeStruct((2, 2, 36, 8, 512), jnp.float32),
        in_specs=[hbm] * 3,
        out_specs=hbm,
        scratch_shapes=[
            pltpu.VMEM((128, 16, 128), jnp.float32),
            pltpu.VMEM((128, 128), jnp.float32),
            pltpu.VMEM((2048, 128), jnp.float32),
            pltpu.VMEM((2, 2, 36, 8, 512), jnp.float32),
            pltpu.VMEM((128, 512), jnp.bfloat16),
            pltpu.VMEM((128, 1, 128), jnp.int32),
            pltpu.SemaphoreType.DMA((4,)),
            pltpu.SemaphoreType.DMA((8,)),
        ]
        + [pltpu.VMEM((32768, 128), jnp.float32)] * NACC
        + [pltpu.SMEM((128,), jnp.int32)] * 128,
        compiler_params=pltpu.CompilerParams(vmem_limit_bytes=VMEM),
        cost_estimate=pl.CostEstimate(flops=10**9, bytes_accessed=4 * 2**20, transcendentals=0),
        name="scatter",
    )(vals, cells, mixer)


def filter_kernel(n_lat, n_lon, x_hbm, t_hbm, a_hbm, out, x, e, y, t, a, passing, send, recv, local):
    lat = lax.axis_index("lat")
    lon = lax.axis_index("lon")
    west = lax.rem(lon + n_lon - 1, n_lon)
    east = lax.rem(lon + 1, n_lon)
    north = lat - 1
    south = lat + 1
    has_north = lat > 0
    has_south = lat < n_lat - 1
    last, mid = n_lat - 1, n_lat // 2 - 1
    at_end = (lat == 0) | (lat == last)
    at_mid = (lat == mid) | (lat == mid + 1)
    rows = pl.ds(0, 256)
    edge = pl.ds(256, 32)
    own = pl.ds(0, 2)
    upper, lower = pl.ds(0, 248), pl.ds(8, 248)

    barrier = pltpu.get_barrier_semaphore()

    def greet(where):
        pl.semaphore_signal(barrier, inc=1, device_id=where, device_id_type=MESH)

    @pl.when(has_north)
    def _():
        greet((north, lon))

    @pl.when(has_south)
    def _():
        greet((south, lon))

    greet((lat, west))
    greet((lat, east))

    @pl.when(at_end)
    def _():
        greet((mid, lon))
        greet((mid + 1, lon))

    @pl.when(at_mid)
    def _():
        greet((0, lon))
        greet((last, lon))

    loads = [
        pltpu.make_async_copy(x_hbm.at[:, :, rows], x.at[own], local.at[0]),
        pltpu.make_async_copy(t_hbm, t, local.at[1]),
        pltpu.make_async_copy(a_hbm, a, local.at[2]),
    ]
    for copy in loads:
        copy.start()
    pl.semaphore_wait(barrier, jnp.where(at_end, 5, jnp.where(at_mid, 6, 4)))

    def remote(src, dst, slot, where):
        return pltpu.make_async_remote_copy(
            src_ref=src, dst_ref=dst, send_sem=send.at[slot], recv_sem=recv.at[slot],
            device_id=where, device_id_type=MESH,
        )

    sides = [
        remote(x_hbm.at[:, :, edge, pl.ds(0, 256)], e.at[1, own], 0, (lat, west)),
        remote(x_hbm.at[:, :, edge, pl.ds(256, 256)], e.at[0, own], 1, (lat, east)),
    ]
    up = [
        remote(x_hbm.at[0, 0, upper], x.at[3, 0, upper], 2, (north, lon)),
        remote(x_hbm.at[0, 1, pl.ds(0, 128)], x.at[3, 1, pl.ds(0, 128)], 3, (north, lon)),
        remote(x_hbm.at[0, 1, pl.ds(128, 120)], x.at[3, 1, pl.ds(128, 120)], 8, (north, lon)),
        remote(e.at[:, 0], e.at[:, 3], 4, (north, lon)),
    ]
    down = [
        remote(x_hbm.at[1, 0, lower], x.at[2, 0, lower], 5, (south, lon)),
        remote(x_hbm.at[1, 1, pl.ds(128, 128)], x.at[2, 1, pl.ds(128, 128)], 6, (south, lon)),
        remote(x_hbm.at[1, 1, pl.ds(8, 120)], x.at[2, 1, pl.ds(8, 120)], 9, (south, lon)),
        remote(e.at[:, 1], e.at[:, 2], 7, (south, lon)),
    ]

    first, second = passing.at[0], passing.at[1, pl.ds(0, 120)]
    hop_up = [
        remote(x_hbm.at[0, 1, pl.ds(0, 128)], first, 10, (0, lon)),
        remote(x_hbm.at[0, 1, pl.ds(128, 120)], second, 11, (0, lon)),
    ]
    hop_down = [
        remote(x_hbm.at[1, 1, pl.ds(128, 128)], first, 10, (last, lon)),
        remote(x_hbm.at[1, 1, pl.ds(8, 120)], second, 11, (last, lon)),
    ]
    pass_up = [
        remote(first, x.at[3, 1, pl.ds(0, 128)], 3, (mid, lon)),
        remote(second, x.at[3, 1, pl.ds(128, 120)], 8, (mid, lon)),
    ]
    pass_down = [
        remote(first, x.at[2, 1, pl.ds(128, 128)], 6, (mid + 1, lon)),
        remote(second, x.at[2, 1, pl.ds(8, 120)], 9, (mid + 1, lon)),
    ]

    def ends_do(act, which):
        for cond, copies, hops, turn in ((has_north, up, hop_up, mid + 1), (has_south, down, hop_down, mid)):
            for i in which:
                if i in (1, 2):
                    @pl.when(cond & (lat != turn))
                    def _():
                        act(copies[i])

                    @pl.when(lat == turn)
                    def _():
                        act(hops[i - 1])
                else:
                    @pl.when(cond)
                    def _():
                        act(copies[i])

    def relay(i):
        @pl.when(lat == 0)
        def _():
            hop_up[i].wait_recv()
            pass_up[i].start()

        @pl.when(lat == last)
        def _():
            hop_down[i].wait_recv()
            pass_down[i].start()

    def arrived(which):
        @pl.when(has_north)
        def _():
            for i in which:
                down[i].wait_recv()

        @pl.when(has_south)
        def _():
            for i in which:
                up[i].wait_recv()

    for copy in sides:
        copy.start()
    ends_do(lambda copy: copy.start(), (0, 1))

    x[2, :, pl.ds(0, 8)] = jnp.zeros((2, 8, 512), jnp.float32)
    x[3, :, pl.ds(248, 8)] = jnp.zeros((2, 8, 512), jnp.float32)
    for s, there in ((2, has_north), (3, has_south)):
        @pl.when(jnp.logical_not(there))
        def _():
            x[s] = jnp.zeros((2, 256, 512), jnp.float32)
            e[:, s] = jnp.zeros((2, 2, 32, 256), jnp.float32)

    def centre(s, v):
        hi, lo = split(x[pl.ds(s, 2), v].reshape(512, 512))
        for n in range(2):
            deep, wide = slice(n * 128, n * 128 + 384), pl.ds(n * 256, 256)
            band = t[0, v, pl.ds(n * 128, 384), wide], t[1, v, pl.ds(n * 128, 384), wide]
            total = dot3((hi[:, deep], lo[:, deep]), band)
            for u in range(2):
                for cb in range(2):
                    y[s + u, v, n * 2 + cb] = total[u * 256 : u * 256 + 256, cb * 128 : cb * 128 + 128]

    def rims(s, v):
        for side in range(2):
            lines = [e[side, s + u, v, :, pl.ds(kk * 128, 128)] for u in range(2) for kk in range(2)]
            rim = dot3(split(jnp.concatenate(lines, axis=0)), (t[0, v, pl.ds(512 + side * 128, 128)], t[1, v, pl.ds(512 + side * 128, 128)]))
            for u in range(2):
                for k2 in range(8):
                    line = (u * 2 + k2 // 4) * 32
                    col = (k2 % 4) * 128
                    y[s + u, v, side * 3, pl.ds(k2 * 32, 32)] += rim[line : line + 32, col : col + 128]

    def along_lat(s, v):
        def levels(i, carry):
            for u in range(4):
                l = i * 4 + u
                line = jnp.concatenate(
                    [
                        jnp.concatenate([y[s + k, v, cb, pl.ds(l, 32, stride=8), :] for cb in range(4)], axis=1)
                        for k in range(2)
                    ],
                    axis=0,
                )
                hi, lo = split(line)
                part = dot(a[s // 2, v], jnp.concatenate([hi, hi, lo], axis=0))
                out[v, l] = part if s == 0 else out[v, l] + part
            return carry

        lax.fori_loop(0, LEV // 4, levels, 0)

    for copy in loads:
        copy.wait()
    centre(0, 0)
    for copy in sides:
        copy.wait_recv()
    ends_do(lambda copy: copy.start(), (3, 2))
    relay(0)
    centre(0, 1)
    relay(1)
    for v in range(2):
        rims(0, v)
        along_lat(0, v)

    for v in range(2):
        arrived((0, 3) if v == 0 else (1, 2))
        centre(2, v)
        rims(2, v)
        along_lat(2, v)

    for copy in sides:
        copy.wait_send()
    ends_do(lambda copy: copy.wait_send(), (0, 1, 2, 3))

    @pl.when(lat == 0)
    def _():
        for copy in pass_up:
            copy.wait_send()

    @pl.when(lat == last)
    def _():
        for copy in pass_down:
            copy.wait_send()


def filter_tile(n_lat, n_lon, x, weights):
    return pl.pallas_call(
        functools.partial(filter_kernel, n_lat, n_lon),
        out_shape=jax.ShapeDtypeStruct((2, 8, 64, 512), jnp.float32),
        in_specs=[pl.BlockSpec(memory_space=pl.ANY)] * 3,
        out_specs=pl.BlockSpec(memory_space=pltpu.VMEM),
        scratch_shapes=[
            pltpu.VMEM((4, 2, 256, 512), jnp.float32),
            pltpu.VMEM((2, 4, 2, 32, 256), jnp.float32),
            pltpu.VMEM((4, 2, 4, 256, 128), jnp.float32),
            pltpu.VMEM((2, 2, 768, 512), jnp.bfloat16),
            pltpu.VMEM((2, 2, 64, 192), jnp.bfloat16),
            pltpu.VMEM((2, 128, 512), jnp.float32),
            pltpu.SemaphoreType.DMA((12,)),
            pltpu.SemaphoreType.DMA((12,)),
            pltpu.SemaphoreType.DMA((3,)),
        ],
        compiler_params=pltpu.CompilerParams(
            vmem_limit_bytes=101 * 2**19, collective_id=0, has_side_effects=True
        ),
        cost_estimate=pl.CostEstimate(flops=6 * 10**9, bytes_accessed=8 * 2**20, transcendentals=0),
        name="filters",
    )(x, *weights)


def route_kernel(n_lat, n_lon, obs_hbm, cells_hbm, counts_hbm, lengths_hbm, weights_hbm, mix_hbm,
                 vals, cells, mixer_hbm, t_hbm, a_hbm,
                 box, cell_box, counts, lengths, weights, mix, tiles, mixer, t_out, a_out, local, send, recv):
    lat = lax.axis_index("lat")
    lon = lax.axis_index("lon")
    me = lat * n_lon + lon
    count = n_lat * n_lon

    loads = [
        pltpu.make_async_copy(src, dst, local.at[i])
        for i, (src, dst) in enumerate(
            ((obs_hbm, box), (cells_hbm, cell_box), (counts_hbm, counts), (lengths_hbm, lengths),
             (weights_hbm, weights), (mix_hbm, mix))
        )
    ]
    for copy in loads:
        copy.start()

    barrier = pltpu.get_barrier_semaphore()

    columns = [lon] + [lax.rem(lon + k, n_lon) for k in range(1, n_lon)]

    def each_peer(act):
        for k in range(1, n_lon):
            act(lat, columns[k])

        def line(i, carry):
            away = jnp.where(i % 2 == 1, (i + 1) // 2, n_lat - i // 2)
            for column in columns:
                act(lax.rem(lat + away, n_lat), column)
            return carry

        lax.fori_loop(1, n_lat, line, 0)

    def greet(to_lat, to_lon):
        pl.semaphore_signal(barrier, inc=1, device_id=(to_lat, to_lon), device_id_type=MESH)

    each_peer(greet)
    for copy in loads:
        copy.wait()

    slot = lax.broadcasted_iota(jnp.int32, (16, 128), 1)

    def mask(i, carry):
        for u in range(8):
            d = i * 8 + u
            box[d] = jnp.where(slot < counts[0, d], box[d], 0.0)
        return carry

    lax.fori_loop(0, count // 8, mask, 0)
    pl.semaphore_wait(barrier, count - 1)

    def give(to_lat, to_lon):
        d = to_lat * n_lon + to_lon
        for i, (src, dst) in enumerate(((box, vals), (cell_box, cells))):
            pltpu.make_async_remote_copy(
                src_ref=src.at[d], dst_ref=dst.at[me], send_sem=send.at[i], recv_sem=recv.at[i],
                device_id=(to_lat, to_lon), device_id_type=MESH,
            ).start()

    each_peer(give)
    pltpu.make_async_copy(cell_box.at[me], cells.at[me], recv.at[1]).start()
    pltpu.make_async_copy(box.at[me], vals.at[me], recv.at[0]).start()

    def iota(shape, dim):
        return lax.broadcasted_iota(jnp.int32, shape, dim)

    def profile(v, offset):
        t = offset.astype(jnp.float32)
        total = 0.0
        for s in range(3):
            scale = t / lengths[v, s]
            total = total + weights[v, s] * jnp.exp(-0.5 * (scale * scale))
        return jnp.where(jnp.abs(offset) <= HALF, total, 0.0)

    flat = (128, 128)
    for v in range(2):
        taps = profile(v, iota((8, 128), 1) - HALF)
        norm = lax.rsqrt(jnp.sum(taps * taps, axis=1, keepdims=True))[0:1, 0:1]
        for i in range(3):
            hi, lo = split(profile(v, iota(flat, 0) - iota(flat, 1) + (i - 1) * 128) * norm)
            tiles[0, i] = hi
            tiles[1, i] = lo
        blank = jnp.zeros(flat, jnp.bfloat16)
        for p in range(2):
            for i in range(4):
                for j in range(4):
                    piece = tiles[p, i - j + 1] if abs(i - j) <= 1 else blank
                    t_out[p, v, pl.ds(i * 128, 128), pl.ds(j * 128, 128)] = piece
            t_out[p, v, pl.ds(512, 256)] = jnp.zeros((256, 512), jnp.bfloat16)
            for kq in range(4):
                at = pl.ds(kq * 128, 128)
                t_out[p, v, pl.ds(512 + kq * 32, 32), at] = tiles[p, 0, pl.ds(96, 32)]
                t_out[p, v, pl.ds(640 + kq * 32, 32), at] = tiles[p, 2, pl.ds(0, 32)]
        k = iota((64, 192), 1)
        place = lax.rem(k, 32)
        inner = lax.rem(place, 4) * 8 + place // 4
        second = lax.rem(k, 64) // 32
        for part in range(2):
            base = second * 32 if part == 0 else second * 96 - 32
            hi, lo = split(profile(v, base + inner - iota((64, 192), 0)) * norm)
            a_out[part, v] = jnp.where(k // 64 == 1, lo.astype(jnp.float32), hi.astype(jnp.float32)).astype(jnp.bfloat16)

    row, col = iota((16, 128), 0), iota((16, 128), 1)
    small = jnp.zeros((16, 128), jnp.float32)
    for v in range(2):
        for l in range(LEV):
            for m in range(LEV):
                here = (row == v * LEV + m) & (lax.rem(col, 16) == v * LEV + l)
                small = jnp.where(here, mix[v, l, m], small)
    for i in range(8):
        mixer[pl.ds(i * 16, 16)] = jnp.where(col // 16 == i, small, 0.0)

    writes = [
        pltpu.make_async_copy(src, dst, local.at[i])
        for i, (src, dst) in enumerate(((mixer, mixer_hbm), (t_out, t_hbm), (a_out, a_hbm)))
    ]
    for copy in writes:
        copy.start()
    for copy in writes:
        copy.wait()

    rest = pl.ds(0, count - 1)
    for i, (src, dst) in enumerate(((box, vals), (cell_box, cells))):
        pltpu.make_async_copy(dst, dst, recv.at[i]).wait()
        pltpu.make_async_copy(src.at[rest], dst.at[rest], send.at[i]).wait()


def route(n_lat, n_lon, obs, cells, counts, lengths, weights, mix):
    n = n_lat * n_lon
    hbm = pl.BlockSpec(memory_space=pl.ANY)
    bf16 = jnp.bfloat16
    return pl.pallas_call(
        functools.partial(route_kernel, n_lat, n_lon),
        out_shape=(
            jax.ShapeDtypeStruct((n, 16, 128), jnp.float32),
            jax.ShapeDtypeStruct((n, 1, 128), jnp.int32),
            jax.ShapeDtypeStruct((128, 128), jnp.float32),
            jax.ShapeDtypeStruct((2, 2, 768, 512), bf16),
            jax.ShapeDtypeStruct((2, 2, 64, 192), bf16),
        ),
        in_specs=[hbm] * 6,
        out_specs=[hbm] * 5,
        scratch_shapes=[
            pltpu.VMEM((n, 16, 128), jnp.float32),
            pltpu.VMEM((n, 1, 128), jnp.int32),
            pltpu.SMEM((1, n), jnp.int32),
            pltpu.SMEM((2, 3), jnp.float32),
            pltpu.SMEM((2, 3), jnp.float32),
            pltpu.SMEM((2, LEV, LEV), jnp.float32),
            pltpu.VMEM((2, 3, 128, 128), bf16),
            pltpu.VMEM((128, 128), jnp.float32),
            pltpu.VMEM((2, 2, 768, 512), bf16),
            pltpu.VMEM((2, 2, 64, 192), bf16),
            pltpu.SemaphoreType.DMA((6,)),
            pltpu.SemaphoreType.DMA((2,)),
            pltpu.SemaphoreType.DMA((2,)),
        ],
        compiler_params=pltpu.CompilerParams(vmem_limit_bytes=VMEM, collective_id=1, has_side_effects=True),
        cost_estimate=pl.CostEstimate(flops=10**7, bytes_accessed=4 * 2**20, transcendentals=0),
        name="route",
    )(obs, cells, counts, lengths, weights, mix)


def local(obs_values, obs_cells, obs_counts, filter_lengths, filter_weights, vertical_mix):
    n_lat, n_lon = lax.axis_size("lat"), lax.axis_size("lon")
    n = n_lat * n_lon
    vals, cells, mixer, *weights = route(
        n_lat, n_lon, obs_values.reshape(n, 16, 128), obs_cells.reshape(n, 1, 128), obs_counts,
        filter_lengths, filter_weights, vertical_mix,
    )
    x = grid_tile(vals, cells, mixer)
    return filter_tile(n_lat, n_lon, x.reshape(2, 2, 288, 512), weights)


def solution(mesh):
    in_specs = (
        P(("lat", "lon"), None, None, None, None),
        P(("lat", "lon"), None, None),
        P(("lat", "lon"), None),
        P(),
        P(),
        P(),
    )
    return jax.shard_map(
        local, mesh=mesh, in_specs=in_specs, out_specs=P(None, None, "lat", "lon"), check_vma=False
    )
```
